32 devices in a mesh: rep: 4 (over z), seq: 2 (over x), tp: 4 (over y, core).
Axes of the slice: x: 2, y: 2, z: 4, core: 2. Of those that a mesh axis runs over, the one named last changes fastest.
Arguments:
- hidden_in: float32 [8, 1024, 2048], P('rep', 'seq'), may hold values from -6 to 6
- cotangent: float32 [8, 1024, 2048], P('rep', 'seq'), may hold values from -6 to 6
- w_qkv: bfloat16 [1, 2048, 4, 640], P(None, 'seq', 'tp'), may hold values from -0.125 to 0.125
- w_out: bfloat16 [1, 2048, 2048], P(None, 'tp', 'seq'), may hold values from -0.5 to 0.5
- w_gate_up: bfloat16 [1, 2048, 2, 5632], P(None, 'seq', None, 'tp'), may hold values from -0.125 to 0.125
- w_down: bfloat16 [1, 5632, 2048], P(None, 'tp', 'seq'), may hold values from -0.078125 to 0.078125
- norm_gains: bfloat16 [1, 2, 2048], P(None, None, 'seq'), may hold values from 0.099609375 to 1.8984375
- segments: int32 [8, 1024], P('rep'), may hold values from 0 to 3, never falling along the last dimension, each value on 1 to 512 neighbouring positions
Outputs:
- hidden_out: float32 [8, 1024, 2048], P('rep', 'seq')
- grad_in: float32 [8, 1024, 2048], P('rep', 'seq')
- grad_qkv: float32 [1, 2048, 4, 640], P(None, 'seq', 'tp')
- grad_out: float32 [1, 2048, 2048], P(None, 'tp', 'seq')
- grad_gate_up: float32 [1, 2048, 2, 5632], P(None, 'seq', None, 'tp')
- grad_down: float32 [1, 5632, 2048], P(None, 'tp', 'seq')
- grad_gains: float32 [1, 2, 2048], P(None, None, 'seq')
The draws below stay inside these ranges and needn't reach their ends.
Inputs may be any that keep to these rules, and one draw needn't show every extreme that they name: `segments`: in each sequence the document number never falls, each of 0 to 3 occurs, a document has 1 to 512 tokens and one has exactly 512.
All inputs are finite; a program needn't handle non-finite values.
Results may differ from the reference program's by a relative error of at most 0.013.
Values may be sent and summed in bfloat16 or wider, within the bound.
No kernel may reach another device: no remote copies, remote signals or barrier semaphores. Data moves between devices by JAX's collectives and lax.ppermute only.
A program may use at most 320 MiB of HBM per device.

```python
import math
import jax
import jax.numpy as jnp
import numpy as np
from jax import lax

D = 2048
HEADS = 32
KV_HEADS = 4
HEAD_DIM = 64
FF = 5632
LAYERS = 1
SEQ_LEN = 1024
DOCS = 4
QKV_WIDTH = 640
BATCH = 8


def steps_of(stream_key, shape, shards, low, top_value):
    def one(position, shards_of):
        draws = jax.random.uniform(jax.random.fold_in(jax.random.fold_in(stream_key, 6), position), (shards_of,), jnp.float32, low / len(shards), top_value / len(shards))
        return jnp.repeat(jnp.exp(draws), shape[position] // shards_of).reshape((-1,) + (1,) * (len(shape) - position - 1))

    level = one(*shards[0])
    for cut in shards[1:]:
        level = level * one(*cut)
    return level


def profile(count, total, most, skew):
    weights = [(1 << 20) // math.isqrt(standing ** skew) + 1 for standing in range(2, count + 1)]
    surplus, holding = total - most - (count - 1), [1] * (count - 1)
    while surplus > 0:
        free = [i for i in range(count - 1) if holding[i] < most]
        whole, left = sum([weights[i] for i in free]), surplus
        for i in free:
            addition = min(most - holding[i], max(1, left * weights[i] // whole), surplus)
            holding[i] = holding[i] + addition
            surplus = surplus - addition
    return np.array([most] + holding)


def ragged_sizes(key, number_of, total, bound, lean):
    if number_of == 2:
        one = jax.random.randint(key, (), max(1, total - bound), min(bound, total - 1) + 1)
        return jnp.stack([one, total - one])
    sizes = jnp.asarray(profile(number_of, total, bound, lean), jnp.int32)
    pairs = (number_of - 1) // 2
    donor, sink = sizes[1:1 + 2 * pairs:2], sizes[2:2 + 2 * pairs:2]
    room = jnp.minimum(donor - 1, bound - sink)
    shifted = jax.random.randint(jax.random.fold_in(key, 1), (pairs,), 0, 1 << 20) % (room + 1)
    sizes = sizes.at[1:1 + 2 * pairs:2].set(donor - shifted).at[2:2 + 2 * pairs:2].set(sink + shifted)
    return sizes[jax.random.permutation(jax.random.fold_in(key, 2), number_of)]


def normal_values(key, dims, spread, limit, shards=(), kind=jnp.bfloat16):
    level = steps_of(key, dims, shards, -0.22, 0.18) if shards else 1.0
    values = jax.random.normal(key, dims, jnp.float32) * spread * level
    return jnp.minimum(jnp.maximum(values, -limit), limit).astype(kind)


def setup_inputs(seed: int = 0) -> dict:
    streams_of = jax.random.split(jax.random.key(seed), 9)
    return {
        "hidden_in": normal_values(streams_of[0], (BATCH, SEQ_LEN, D), 1.0, 6.0, ((0, 4), (1, 2)), jnp.float32),
        "cotangent": normal_values(streams_of[1], (BATCH, SEQ_LEN, D), 1.0, 6.0, ((0, 4), (1, 2)), jnp.float32),
        "w_qkv": normal_values(streams_of[2], (LAYERS, D, KV_HEADS, QKV_WIDTH), D ** -0.5, 0.125, ((1, 2), (2, 4))),
        "w_out": normal_values(streams_of[3], (LAYERS, HEADS * HEAD_DIM, D), (HEADS * HEAD_DIM // 16) ** -0.5, 0.5, ((1, 4), (2, 2))),
        "w_gate_up": normal_values(streams_of[4], (LAYERS, D, 2, FF), D ** -0.5, 0.125, ((1, 2), (3, 4))),
        "w_down": normal_values(streams_of[5], (LAYERS, FF, D), FF ** -0.5, 0.078125, ((1, 4), (2, 2))),
        "norm_gains": jnp.clip(1.0 + 0.18 * jax.random.normal(streams_of[6], (LAYERS, 2, D), jnp.float32), 0.099609375, 1.8984375).astype(jnp.bfloat16),
        "segments": jax.vmap(lambda own: jnp.searchsorted(jnp.cumsum(ragged_sizes(own, DOCS, SEQ_LEN, SEQ_LEN // 2, 2)), jnp.arange(SEQ_LEN), side="right"))(jax.random.split(streams_of[7], BATCH)).reshape((BATCH, SEQ_LEN)).astype(jnp.int32),
    }


NORM_EPS = 1e-05
ROPE_THETA = 10000.0

def doc_positions(seg_ids):
    column_ids = jnp.arange(seg_ids.shape[1], dtype=jnp.int32)
    change = jnp.concatenate([jnp.ones(seg_ids[:, :1].shape, dtype=bool), seg_ids[:, 1:] != seg_ids[:, :-1]], axis=1)
    doc_start = lax.cummax(jnp.where(change, column_ids[None, :], 0).astype(jnp.int32), axis=1)
    return column_ids[None, :] - doc_start

def rope_tables(positions, half_dim):
    inverse_freq = ROPE_THETA ** (-(jnp.arange(half_dim, dtype=jnp.float32) / half_dim))
    angles = positions.astype(jnp.float32)[..., None] * inverse_freq
    return (jnp.cos(angles), jnp.sin(angles))

def rotate(values, cos_tab, sin_tab):
    half_dim = values.shape[-1] // 2
    first_half = values[..., :half_dim]
    second_half = values[..., half_dim:]
    return jnp.concatenate([first_half * cos_tab - second_half * sin_tab, second_half * cos_tab + first_half * sin_tab], axis=-1)

def unrotate(upstream, cos_tab, sin_tab):
    half_dim = upstream.shape[-1] // 2
    first_half = upstream[..., :half_dim]
    second_half = upstream[..., half_dim:]
    return jnp.concatenate([first_half * cos_tab + second_half * sin_tab, second_half * cos_tab - first_half * sin_tab], axis=-1)

def rms_norm(hidden, gain_row):
    inv_rms = lax.rsqrt(lax.optimization_barrier(jnp.mean(hidden * hidden, axis=-1, keepdims=True)) + NORM_EPS)
    return (hidden * inv_rms * gain_row, inv_rms)

def rms_back(hidden, inv_rms, gain_row, upstream):
    weighted = gain_row * upstream
    grad_hidden = inv_rms * weighted - hidden * inv_rms * inv_rms * inv_rms * lax.optimization_barrier(jnp.mean(weighted * hidden, axis=-1, keepdims=True))
    grad_gain = lax.optimization_barrier(jnp.sum(upstream * hidden * inv_rms, axis=0))
    return (grad_hidden, grad_gain)

def as_bf16_f32(values):
    return lax.optimization_barrier(values.astype(jnp.bfloat16)).astype(jnp.float32)

def reference(hidden_in, cotangent, w_qkv, w_out, w_gate_up, w_down, norm_gains, segments):
    batch_n, seq_n, model_width = hidden_in.shape
    kv_heads = w_qkv.shape[2]
    qkv_width = w_qkv.shape[3]
    kv_group = qkv_width // HEAD_DIM - 2
    ff_width = w_down.shape[1]
    row_count = batch_n * seq_n
    att_scale = float(HEAD_DIM) ** (-0.5)
    gains32 = norm_gains.astype(jnp.float32)
    positions = doc_positions(segments)
    cos_tab, sin_tab = rope_tables(positions, HEAD_DIM // 2)
    q_cos = cos_tab[:, :, None, None, :]
    q_sin = sin_tab[:, :, None, None, :]
    k_cos = cos_tab[:, :, None, :]
    k_sin = sin_tab[:, :, None, :]
    seq_ids = jnp.arange(seq_n, dtype=jnp.int32)
    causal = seq_ids[None, :] <= seq_ids[:, None]

    def attend(items):
        queries, keys, values, seg_row = items
        allowed = (causal & (seg_row[None, :] == seg_row[:, None]))[None, None]
        scores = jnp.einsum('qkgd,nkd->kgqn', queries.astype(jnp.float32), keys.astype(jnp.float32)) * att_scale
        top_score = lax.optimization_barrier(jnp.max(jnp.where(allowed, scores, -jnp.inf), axis=-1, keepdims=True))
        expo = jnp.where(allowed, jnp.exp(scores - top_score), 0.0)
        totals = lax.optimization_barrier(jnp.sum(expo, axis=-1, keepdims=True))
        mixed = jnp.einsum('kgqn,nkd->qkgd', as_bf16_f32(expo), values.astype(jnp.float32))
        mixed = mixed / jnp.transpose(totals, (2, 0, 1, 3))
        return (mixed.astype(jnp.bfloat16), (top_score + jnp.log(totals))[..., 0])

    def attend_back(items):
        queries, keys, values, seg_row, mixed, d_mixed, log_total = items
        allowed = (causal & (seg_row[None, :] == seg_row[:, None]))[None, None]
        scores = jnp.einsum('qkgd,nkd->kgqn', queries.astype(jnp.float32), keys.astype(jnp.float32)) * att_scale
        probs = jnp.where(allowed, jnp.exp(scores - log_total[..., None]), 0.0)
        d_mixed32 = d_mixed.astype(jnp.float32)
        delta = jnp.transpose(lax.optimization_barrier(jnp.sum(d_mixed32 * mixed.astype(jnp.float32), axis=-1)), (1, 2, 0))
        d_values = jnp.einsum('kgqn,qkgd->nkd', as_bf16_f32(probs), d_mixed32)
        d_probs = jnp.einsum('qkgd,nkd->kgqn', d_mixed32, values.astype(jnp.float32))
        d_scores = as_bf16_f32(probs * (d_probs - delta[..., None]) * att_scale)
        d_queries = jnp.einsum('kgqn,nkd->qkgd', d_scores, keys.astype(jnp.float32))
        d_keys = jnp.einsum('kgqn,qkgd->nkd', d_scores, queries.astype(jnp.float32))
        return (d_queries, d_keys, d_values)
    hidden = hidden_in.reshape(row_count, model_width)
    caches = []
    for layer_no in range(LAYERS):
        qkv_matrix = w_qkv[layer_no].reshape(model_width, kv_heads * qkv_width)
        normed1, inv_rms1 = rms_norm(hidden, gains32[layer_no, 0])
        normed1 = normed1.astype(jnp.bfloat16)
        projected = jnp.dot(normed1, qkv_matrix, preferred_element_type=jnp.float32).reshape(batch_n, seq_n, kv_heads, qkv_width)
        queries = projected[..., :kv_group * HEAD_DIM].reshape(batch_n, seq_n, kv_heads, kv_group, HEAD_DIM)
        keys = projected[..., kv_group * HEAD_DIM:(kv_group + 1) * HEAD_DIM]
        values = projected[..., (kv_group + 1) * HEAD_DIM:]
        q_rot = rotate(queries, q_cos, q_sin).astype(jnp.bfloat16)
        k_rot = rotate(keys, k_cos, k_sin).astype(jnp.bfloat16)
        v_rot = values.astype(jnp.bfloat16)
        mixed, log_total = lax.map(attend, (q_rot, k_rot, v_rot, segments))
        mixed_rows = mixed.reshape(row_count, kv_heads * kv_group * HEAD_DIM)
        hidden2 = hidden + jnp.dot(mixed_rows, w_out[layer_no], preferred_element_type=jnp.float32)
        normed2, inv_rms2 = rms_norm(hidden2, gains32[layer_no, 1])
        normed2 = normed2.astype(jnp.bfloat16)
        gate_up = jnp.dot(normed2, w_gate_up[layer_no].reshape(model_width, 2 * ff_width), preferred_element_type=jnp.float32)
        gate_up = gate_up.reshape(row_count, 2, ff_width)
        gate_val = gate_up[:, 0]
        up_val = gate_up[:, 1]
        act_val = (jax.nn.silu(gate_val) * up_val).astype(jnp.bfloat16)
        hidden3 = hidden2 + jnp.dot(act_val, w_down[layer_no], preferred_element_type=jnp.float32)
        caches.append((hidden, inv_rms1, normed1, q_rot, k_rot, v_rot, mixed, mixed_rows, log_total, hidden2, inv_rms2, normed2, gate_val, up_val, act_val))
        hidden = hidden3
    hidden_out = hidden.reshape(batch_n, seq_n, model_width)
    d_hidden = cotangent.reshape(row_count, model_width)
    grads = [None] * LAYERS
    for layer_no in reversed(range(LAYERS)):
        hidden, inv_rms1, normed1, q_rot, k_rot, v_rot, mixed, mixed_rows, log_total, hidden2, inv_rms2, normed2, gate_val, up_val, act_val = caches[layer_no]
        qkv_matrix = w_qkv[layer_no].reshape(model_width, kv_heads * qkv_width)
        gu_matrix = w_gate_up[layer_no].reshape(model_width, 2 * ff_width)
        d_hid_b = d_hidden.astype(jnp.bfloat16)
        g_down = jnp.dot(act_val.T, d_hid_b, preferred_element_type=jnp.float32)
        d_act = jnp.dot(d_hid_b, w_down[layer_no].T, preferred_element_type=jnp.float32)
        sigm = jax.nn.sigmoid(gate_val)
        d_gate = d_act * up_val * sigm * (1.0 + gate_val * (1.0 - sigm))
        d_up = d_act * gate_val * sigm
        d_gu = jnp.stack([d_gate, d_up], axis=1).astype(jnp.bfloat16).reshape(row_count, 2 * ff_width)
        g_gate_up = jnp.dot(normed2.T, d_gu, preferred_element_type=jnp.float32).reshape(model_width, 2, ff_width)
        d_normed2 = jnp.dot(d_gu, gu_matrix.T, preferred_element_type=jnp.float32)
        d_hidden2, g_gain2 = rms_back(hidden2, inv_rms2, gains32[layer_no, 1], d_normed2)
        d_hidden2 = d_hidden2 + d_hidden
        d_hid2_b = d_hidden2.astype(jnp.bfloat16)
        g_out = jnp.dot(mixed_rows.T, d_hid2_b, preferred_element_type=jnp.float32)
        d_mixed = jnp.dot(d_hid2_b, w_out[layer_no].T, preferred_element_type=jnp.float32).astype(jnp.bfloat16)
        d_mixed = d_mixed.reshape(batch_n, seq_n, kv_heads, kv_group, HEAD_DIM)
        d_queries, d_keys, d_values = lax.map(attend_back, (q_rot, k_rot, v_rot, segments, mixed, d_mixed, log_total))
        d_queries = unrotate(d_queries, q_cos, q_sin)
        d_keys = unrotate(d_keys, k_cos, k_sin)
        d_qkv = jnp.concatenate([d_queries.reshape(batch_n, seq_n, kv_heads, kv_group * HEAD_DIM), d_keys, d_values], axis=-1)
        d_qkv = d_qkv.astype(jnp.bfloat16).reshape(row_count, kv_heads * qkv_width)
        g_qkv = jnp.dot(normed1.T, d_qkv, preferred_element_type=jnp.float32).reshape(model_width, kv_heads, qkv_width)
        d_normed1 = jnp.dot(d_qkv, qkv_matrix.T, preferred_element_type=jnp.float32)
        d_prev, g_gain1 = rms_back(hidden, inv_rms1, gains32[layer_no, 0], d_normed1)
        d_hidden = d_prev + d_hidden2
        grads[layer_no] = (g_qkv, g_out, g_gate_up, g_down, jnp.stack([g_gain1, g_gain2]))
    grad_in = d_hidden.reshape(batch_n, seq_n, model_width)
    grad_qkv = jnp.stack([item[0] for item in grads])
    grad_out = jnp.stack([item[1] for item in grads])
    grad_gate_up = jnp.stack([item[2] for item in grads])
    grad_down = jnp.stack([item[3] for item in grads])
    grad_gains = jnp.stack([item[4] for item in grads])
    return (hidden_out, grad_in, grad_qkv, grad_out, grad_gate_up, grad_down, grad_gains)
```

```python
import functools

import jax
import jax.numpy as jnp
from jax import lax
from jax.experimental import pallas as pl
from jax.experimental.pallas import tpu as pltpu
from jax.sharding import PartitionSpec as P

HEAD_DIM = 64
NORM_EPS = 1e-05
ROPE_THETA = 10000.0
LOG2E = 1.4426950408889634
MASKED = -1e30
F32 = jnp.float32
BF16 = jnp.bfloat16
VMEM_BYTES = 48 * 1024 * 1024


def dot(a, b, ca=1, cb=0):
    return lax.dot_general(a, b, (((ca,), (cb,)), ((), ())), preferred_element_type=F32)


def call(body, grid, ins, outs, shapes, scratch=(), scalars=0, alias=None):
    return pl.pallas_call(
        body,
        out_shape=shapes,
        grid_spec=pltpu.PrefetchScalarGridSpec(
            num_scalar_prefetch=scalars,
            grid=grid,
            in_specs=ins,
            out_specs=outs,
            scratch_shapes=list(scratch),
        ),
        input_output_aliases=alias or {},
        compiler_params=pltpu.CompilerParams(vmem_limit_bytes=VMEM_BYTES),
        cost_estimate=pl.CostEstimate(flops=1, bytes_accessed=1, transcendentals=0),
    )


class Order:
    def __init__(self):
        self.last = ()

    def __call__(self, step, *xs):
        flat, tree = jax.tree.flatten(xs)
        if self.last:
            flat = lax.optimization_barrier((tuple(flat), self.last))[0]
        out = step(*jax.tree.unflatten(tree, flat))
        self.last = tuple(jax.tree.leaves(out))
        return out


def first_norm(hidden, gain, place, block):
    rows, width = hidden.shape
    half = width // 2

    def body(p, a_ref, b_ref, g_ref, n_ref):
        a, b = a_ref[...], b_ref[...]
        total = jnp.sum(a * a, -1, keepdims=True) + jnp.sum(b * b, -1, keepdims=True)
        inv = lax.rsqrt(total * (1.0 / width) + NORM_EPS)
        n_ref[:, :half] = (a * inv * g_ref[:, :half]).astype(BF16)
        n_ref[:, half:] = (b * inv * g_ref[:, half:]).astype(BF16)

    return call(
        body,
        (rows // block,),
        [
            pl.BlockSpec((block, half), lambda i, p: (i, p[1])),
            pl.BlockSpec((block, half), lambda i, p: (i, 1 - p[1])),
            pl.BlockSpec((1, width), lambda i, p: (0, 0)),
        ],
        pl.BlockSpec((block, width), lambda i, p: (i, 0)),
        jax.ShapeDtypeStruct((rows, width), BF16),
        scalars=1,
    )(place, hidden, hidden, gain)


def local_cast(x, place, block):
    rows, width = x.shape
    half = width // 2

    def body(p, a_ref, b_ref, o_ref):
        o_ref[:, :half] = a_ref[...].astype(BF16)
        o_ref[:, half:] = b_ref[...].astype(BF16)

    def row(i, p):
        return (i // 4) * 4 + ((i % 4) ^ p[0])

    return call(
        body,
        (rows // block,),
        [
            pl.BlockSpec((block, half), lambda i, p: (row(i, p), p[1])),
            pl.BlockSpec((block, half), lambda i, p: (row(i, p), 1 - p[1])),
        ],
        pl.BlockSpec((block, width), lambda i, p: (i, 0)),
        jax.ShapeDtypeStruct((rows, width), BF16),
        scalars=1,
    )(place, x, x)


def add_local(x, deltas, place, block):
    rows, width = x.shape
    half = width // 2
    count = len(deltas)

    def body(p, x_ref, *refs):
        o_ref = refs[-1]
        i = pl.program_id(0)
        for k in range(count):

            @pl.when((i // 4) * 4 + ((i % 4) ^ p[0]) == k)
            def _():
                @pl.when(p[1] == 0)
                def _():
                    o_ref[...] = x_ref[...] + refs[k][...].astype(F32)

                @pl.when(p[1] == 1)
                def _():
                    o_ref[:, :half] = x_ref[:, :half] + refs[k][:, half:].astype(F32)
                    o_ref[:, half:] = x_ref[:, half:] + refs[k][:, :half].astype(F32)

    return call(
        body,
        (rows // block,),
        [pl.BlockSpec((block, width), lambda i, p: (i, 0))]
        + [pl.BlockSpec((block, width), lambda i, p: (0, 0))] * count,
        pl.BlockSpec((block, width), lambda i, p: (i, 0)),
        jax.ShapeDtypeStruct((rows, width), F32),
        scalars=1,
    )(place, x, *deltas)


def spread_gate_up(w, place, width, side, pieces, before):
    rows, _, ff = w.shape
    block = min(128, rows)
    steps = rows // block if side is None else rows // block // 2

    def body(p, w_ref, *refs):
        outs = refs[len(before) :]
        for j in range(ff // 128):
            for g in range(2):
                outs[0][:, 256 * j + 128 * g : 256 * j + 128 * (g + 1)] = w_ref[
                    :, g, 128 * j : 128 * (j + 1)
                ]
        for k in range(len(outs) - 1):

            @pl.when(pl.program_id(0) == k)
            def _():
                outs[k + 1][...] = outs[0][...]

    def row(i, p):
        if side is None:
            return i
        return i + steps * (p[2] if side == 0 else 1 - p[2])

    return call(
        body,
        (steps,),
        [pl.BlockSpec((block, 2, ff), lambda i, p: (row(i, p), 0, 0))]
        + [pl.BlockSpec(memory_space=pl.ANY)] * len(before),
        [pl.BlockSpec((block, 2 * ff), lambda i, p: (row(i, p), 0))]
        + [pl.BlockSpec((block, 2 * ff), lambda i, p: (0, 0))] * pieces,
        [jax.ShapeDtypeStruct((width, 2 * ff), BF16)]
        + [jax.ShapeDtypeStruct((block, 2 * ff), BF16)] * pieces,
        scalars=1,
        alias={2 + k: k for k in range(len(before))},
    )(place, w, *before)


def join_gate_up(a, b, middle, at, rows, before):
    count, cols = a.shape
    ff = cols // 2
    block = min(128, count)

    def body(p, a_ref, b_ref, *refs):
        o_ref = refs[-1]

        def put(src):
            for j in range(ff // 128):
                for g in range(2):
                    o_ref[0, :, g, 128 * j : 128 * (j + 1)] = src[
                        :, 256 * j + 128 * g : 256 * j + 128 * (g + 1)
                    ].astype(F32)

        @pl.when(p[0] == 1)
        def _():
            put(a_ref)

        @pl.when(p[0] == 0)
        def _():
            put(b_ref)

    return call(
        body,
        (count // block,),
        [pl.BlockSpec((block, cols), lambda i, p: (i, 0))] * 2
        + [pl.BlockSpec(memory_space=pl.ANY)] * len(before),
        pl.BlockSpec((1, block, 2, ff), lambda i, p: (0, at // block + i, 0, 0)),
        jax.ShapeDtypeStruct((1, rows, 2, ff), F32),
        scalars=1,
        alias={3 + k: k for k in range(len(before))},
    )(middle, a, b, *before)


def project_qkv(normed, weights, cos_t, sin_t, group):
    rows, width = normed.shape
    seqs, half, length = cos_t.shape
    cols = weights[0].shape[1]
    tile = min(256, length)
    per = length // tile
    depth = width // len(weights)
    parts = len(weights)

    def body(n_ref, cos_ref, sin_ref, *refs):
        q_ref, kv_ref = refs[parts:]
        acc = dot(n_ref[:, :depth], refs[0][...])
        for k in range(1, parts):
            acc = acc + dot(n_ref[:, k * depth : (k + 1) * depth], refs[k][...])
        t = acc.T
        cos, sin = cos_ref[0], sin_ref[0]
        for h in range(group + 1):
            a, b = t[2 * half * h : 2 * half * h + half], t[2 * half * h + half : 2 * half * (h + 1)]
            r = jnp.concatenate([a * cos - b * sin, b * cos + a * sin], 0).astype(BF16)
            if h < group:
                q_ref[0, 2 * half * h : 2 * half * (h + 1)] = r
            else:
                kv_ref[0, : 2 * half] = r
        kv_ref[0, 2 * half :] = t[2 * half * (group + 1) :].astype(BF16)

    return call(
        body,
        (seqs, per),
        [
            pl.BlockSpec((tile, width), lambda s, i: (s * per + i, 0)),
            pl.BlockSpec((1, half, tile), lambda s, i: (s, 0, i)),
            pl.BlockSpec((1, half, tile), lambda s, i: (s, 0, i)),
        ]
        + [pl.BlockSpec((depth, cols), lambda s, i: (0, 0))] * parts,
        [
            pl.BlockSpec((1, group * HEAD_DIM, tile), lambda s, i: (s, 0, i)),
            pl.BlockSpec((1, 2 * HEAD_DIM, tile), lambda s, i: (s, 0, i)),
        ],
        [
            jax.ShapeDtypeStruct((seqs, group * HEAD_DIM, length), BF16),
            jax.ShapeDtypeStruct((seqs, 2 * HEAD_DIM, length), BF16),
        ],
    )(normed, cos_t, sin_t, *weights)


def attend(s, q_t, kv_t, starts, bounds, scale, quarter):
    seqs, cols, length = q_t.shape
    total = kv_t.shape[2]
    heads = cols // HEAD_DIM
    tq, tk = min(256, length), min(256, total)

    def body(b_ref, q_ref, kv_ref, st_ref, att_ref, att_t_ref, lse_ref, kn, m, l, acc):
        i = pl.program_id(0)

        @pl.when(i == 0)
        def _():
            kn[...] = kv_ref[0, :HEAD_DIM].astype(F32).T.astype(BF16)

        qid = b_ref[0] + i * tq + lax.broadcasted_iota(jnp.int32, (1, tq), 1)
        start = st_ref[0]
        m[...] = jnp.full_like(m, MASKED)
        l[...] = jnp.zeros_like(l)
        acc[...] = jnp.zeros_like(acc)

        def step(t, _):
            k0 = pl.multiple_of(t * tk, tk)
            kid = k0 + lax.broadcasted_iota(jnp.int32, (tk, 1), 0)
            ok = (kid <= qid) & (kid >= start)
            keys = kn[pl.ds(k0, tk), :]
            vals = kv_ref[0, HEAD_DIM:, pl.ds(k0, tk)]
            for h in range(heads):
                lo = h * HEAD_DIM
                sc = dot(keys, q_ref[0, lo : lo + HEAD_DIM]) * (scale * LOG2E)
                sc = jnp.where(ok, sc, MASKED)
                old = m[h : h + 1]
                new = jnp.maximum(old, jnp.max(sc, 0, keepdims=True))
                e = jnp.exp2(sc - new)
                fade = jnp.exp2(old - new)
                m[h : h + 1] = new
                l[h : h + 1] = l[h : h + 1] * fade + jnp.sum(e, 0, keepdims=True)
                acc[lo : lo + HEAD_DIM] = acc[lo : lo + HEAD_DIM] * fade + dot(vals, e.astype(BF16))
            return 0

        lax.fori_loop(b_ref[2 + 2 * i], b_ref[3 + 2 * i], step, 0)
        for h in range(heads):
            lo = h * HEAD_DIM
            acc[lo : lo + HEAD_DIM] = acc[lo : lo + HEAD_DIM] / l[h : h + 1]
        att_t_ref[...] = acc[...].astype(BF16)
        out = acc[...].T.astype(BF16)
        for q in range(tq // quarter):
            at = ((i * (tq // quarter) + q) ^ b_ref[1]) * quarter
            att_ref[pl.ds(pl.multiple_of(at, quarter), quarter), :] = out[
                q * quarter : (q + 1) * quarter
            ]
        lse_ref[...] = m[...] + jnp.log2(l[...])

    return call(
        body,
        (length // tq,),
        [
            pl.BlockSpec((1, cols, tq), lambda i, b: (s, 0, i)),
            pl.BlockSpec((1, 2 * HEAD_DIM, total), lambda i, b: (s, 0, 0)),
            pl.BlockSpec((1, 1, tq), lambda i, b: (s, 0, i)),
        ],
        [
            pl.BlockSpec((length, cols), lambda i, b: (0, 0)),
            pl.BlockSpec((cols, tq), lambda i, b: (0, i)),
            pl.BlockSpec((heads, tq), lambda i, b: (0, i)),
        ],
        [
            jax.ShapeDtypeStruct((length, cols), BF16),
            jax.ShapeDtypeStruct((cols, length), BF16),
            jax.ShapeDtypeStruct((heads, length), F32),
        ],
        scratch=[
            pltpu.VMEM((total, HEAD_DIM), BF16),
            pltpu.VMEM((heads, tq), F32),
            pltpu.VMEM((heads, tq), F32),
            pltpu.VMEM((cols, tq), F32),
        ],
        scalars=1,
    )(bounds, q_t, kv_t, starts)


def attend_back(s, q_t, kv_t, starts, bounds, att_t, d_att_t, lse, cos_t, sin_t, scale):
    seqs, cols, length = q_t.shape
    total = kv_t.shape[2]
    heads = cols // HEAD_DIM
    half = HEAD_DIM // 2
    tq, tk = min(256, length), min(256, total)

    def body(
        b_ref, q_ref, kv_ref, st_ref, a_ref, d_ref, lse_ref, cos_ref, sin_ref,
        dq_ref, dkv_ref, kn, vn, delta, acc,
    ):
        i = pl.program_id(0)

        @pl.when(i == 0)
        def _():
            kn[...] = kv_ref[0, :HEAD_DIM].astype(F32).T.astype(BF16)
            vn[...] = kv_ref[0, HEAD_DIM:].astype(F32).T.astype(BF16)
            dkv_ref[...] = jnp.zeros_like(dkv_ref)

        qid = b_ref[0] + i * tq + lax.broadcasted_iota(jnp.int32, (1, tq), 1)
        start = st_ref[0]
        for h in range(heads):
            lo = h * HEAD_DIM
            prod = d_ref[lo : lo + HEAD_DIM].astype(F32) * a_ref[lo : lo + HEAD_DIM].astype(F32)
            delta[h : h + 1] = jnp.sum(prod, 0, keepdims=True)
        acc[...] = jnp.zeros_like(acc)

        def step(t, _):
            k0 = pl.multiple_of(t * tk, tk)
            kid = k0 + lax.broadcasted_iota(jnp.int32, (tk, 1), 0)
            ok = (kid <= qid) & (kid >= start)
            keys, vals = kn[pl.ds(k0, tk), :], vn[pl.ds(k0, tk), :]
            keys_t = kv_ref[0, :HEAD_DIM, pl.ds(k0, tk)]
            dk = jnp.zeros((HEAD_DIM, tk), F32)
            dv = jnp.zeros((HEAD_DIM, tk), F32)
            for h in range(heads):
                lo = h * HEAD_DIM
                q, d = q_ref[0, lo : lo + HEAD_DIM], d_ref[lo : lo + HEAD_DIM]
                sc = dot(keys, q) * (scale * LOG2E) - lse_ref[h : h + 1]
                p = jnp.exp2(jnp.where(ok, sc, MASKED))
                dp = dot(vals, d)
                ds = (p * (dp - delta[h : h + 1]) * scale).astype(BF16)
                dv = dv + dot(d, p.astype(BF16), 1, 1)
                dk = dk + dot(q, ds, 1, 1)
                acc[lo : lo + HEAD_DIM] += dot(keys_t, ds)
            dkv_ref[:HEAD_DIM, pl.ds(k0, tk)] += dk
            dkv_ref[HEAD_DIM:, pl.ds(k0, tk)] += dv
            return 0

        lax.fori_loop(b_ref[2 + 2 * i], b_ref[3 + 2 * i], step, 0)
        cos, sin = cos_ref[0], sin_ref[0]
        for h in range(heads):
            lo = h * HEAD_DIM
            c, e = acc[lo : lo + half], acc[lo + half : lo + HEAD_DIM]
            acc[lo : lo + HEAD_DIM] = jnp.concatenate([c * cos + e * sin, e * cos - c * sin], 0)
        dq_ref[...] = acc[...].T.astype(BF16)

    return call(
        body,
        (length // tq,),
        [
            pl.BlockSpec((1, cols, tq), lambda i, b: (s, 0, i)),
            pl.BlockSpec((1, 2 * HEAD_DIM, total), lambda i, b: (s, 0, 0)),
            pl.BlockSpec((1, 1, tq), lambda i, b: (s, 0, i)),
            pl.BlockSpec((cols, tq), lambda i, b: (0, i)),
            pl.BlockSpec((cols, tq), lambda i, b: (0, i)),
            pl.BlockSpec((heads, tq), lambda i, b: (0, i)),
            pl.BlockSpec((1, half, tq), lambda i, b: (s, 0, i)),
            pl.BlockSpec((1, half, tq), lambda i, b: (s, 0, i)),
        ],
        [
            pl.BlockSpec((tq, cols), lambda i, b: (i, 0)),
            pl.BlockSpec((2 * HEAD_DIM, total), lambda i, b: (0, 0)),
        ],
        [
            jax.ShapeDtypeStruct((length, cols), BF16),
            jax.ShapeDtypeStruct((2 * HEAD_DIM, total), F32),
        ],
        scratch=[
            pltpu.VMEM((total, HEAD_DIM), BF16),
            pltpu.VMEM((total, HEAD_DIM), BF16),
            pltpu.VMEM((heads, tq), F32),
            pltpu.VMEM((cols, tq), F32),
        ],
        scalars=1,
    )(bounds, q_t, kv_t, starts, att_t, d_att_t, lse, cos_t, sin_t)


def gate_up(normed, weight):
    rows, width = normed.shape
    ff = weight.shape[1] // 2
    tile = 128

    def body(n_ref, w_ref, act_ref, gu_ref):
        gu = dot(n_ref[...], w_ref[...])
        gate, up = gu[:, :tile], gu[:, tile:]
        sig = 1.0 / (1.0 + jnp.exp2(gate * (-LOG2E)))
        act_ref[...] = (gate * sig * up).astype(BF16)
        gu_ref[...] = gu.astype(BF16)

    return call(
        body,
        (ff // tile,),
        [
            pl.BlockSpec((rows, width), lambda j: (0, 0)),
            pl.BlockSpec((width, 2 * tile), lambda j: (0, j)),
        ],
        [
            pl.BlockSpec((rows, tile), lambda j: (0, j)),
            pl.BlockSpec((rows, 2 * tile), lambda j: (0, j)),
        ],
        [
            jax.ShapeDtypeStruct((rows, ff), BF16),
            jax.ShapeDtypeStruct((rows, 2 * ff), BF16),
        ],
    )(normed, weight)


def gate_back(dhb, w_down, gu):
    rows, width = dhb.shape
    ff = w_down.shape[0]
    tile = 256

    def body(d_ref, w_ref, gu_ref, o_ref):
        d_act = dot(d_ref[...], w_ref[...], 1, 1)
        for k in range(tile // 128):
            d = d_act[:, 128 * k : 128 * (k + 1)]
            gate = gu_ref[:, 256 * k : 256 * k + 128].astype(F32)
            up = gu_ref[:, 256 * k + 128 : 256 * (k + 1)].astype(F32)
            sig = 1.0 / (1.0 + jnp.exp2(gate * (-LOG2E)))
            o_ref[:, 256 * k : 256 * k + 128] = (
                d * up * sig * (1.0 + gate * (1.0 - sig))
            ).astype(BF16)
            o_ref[:, 256 * k + 128 : 256 * (k + 1)] = (d * gate * sig).astype(BF16)

    return call(
        body,
        (pl.cdiv(ff, tile),),
        [
            pl.BlockSpec((rows, width), lambda j: (0, 0)),
            pl.BlockSpec((tile, width), lambda j: (j, 0)),
            pl.BlockSpec((rows, 2 * tile), lambda j: (0, j)),
        ],
        pl.BlockSpec((rows, 2 * tile), lambda j: (0, j)),
        jax.ShapeDtypeStruct((rows, 2 * ff), BF16),
    )(dhb, w_down, gu)


def split_matmul(a, w, transposed, natural, place, seqs):
    rows, depth = a.shape
    cols = w.shape[0] if transposed else w.shape[1]
    tile = min(256, cols)
    length = rows // seqs
    quarter = length // 4

    def body(p, a_ref, w_ref, *refs):
        acc = refs[-1]
        acc[...] = dot(a_ref[...], w_ref[...], 1, 1 if transposed else 0)
        for s in range(seqs):
            send, keep = refs[2 * s], refs[2 * s + 1]
            for j in range(4):
                at = s * length + (j ^ p[0] if natural else j) * quarter
                part = acc[pl.ds(at, quarter), :]
                if j < 2:
                    keep[j * quarter : (j + 1) * quarter] = part
                else:
                    send[(j - 2) * quarter : (j - 1) * quarter] = part.astype(BF16)

    w_spec = (
        pl.BlockSpec((tile, depth), lambda j, p: (j, 0))
        if transposed
        else pl.BlockSpec((depth, tile), lambda j, p: (0, j))
    )
    return call(
        body,
        (cols // tile,),
        [pl.BlockSpec((rows, depth), lambda j, p: (0, 0)), w_spec],
        [pl.BlockSpec((length // 2, tile), lambda j, p: (0, j))] * (2 * seqs),
        [
            jax.ShapeDtypeStruct((length // 2, cols), BF16),
            jax.ShapeDtypeStruct((length // 2, cols), F32),
        ]
        * seqs,
        scratch=[pltpu.VMEM((rows, tile), F32)],
        scalars=1,
    )(place, a, w)


def per_device(
    sizes, hidden_in, cotangent, w_qkv, w_out, w_gate_up, w_down, norm_gains, segments
):
    n_seq, n_tp, n_rep = sizes
    seqs, length, width = hidden_in.shape
    total = segments.shape[1]
    qkv_width = w_qkv.shape[3]
    group = qkv_width // HEAD_DIM - 2
    ff = w_down.shape[1]
    rows = seqs * length
    scale = float(HEAD_DIM) ** (-0.5)
    two = n_seq == 2
    si = lax.axis_index("seq")
    ti = lax.axis_index("tp")
    zi = lax.axis_index("rep")
    core, yi = ti % 2, ti // 2
    half = width // 2
    fourth = width // 4
    quarter = length // 4
    own = core * 2 + yi
    col_swap = si if two else jnp.int32(0) * si
    pz = zi % 2
    place = jnp.stack([own, col_swap, pz]).astype(jnp.int32)
    middle = (zi == 1) | (zi == 2)
    mid_flag = jnp.reshape(middle, (1,)).astype(jnp.int32)
    order = Order()

    def swap_seq(x):
        return lax.ppermute(x, "seq", [(0, 1), (1, 0)])

    def swap_core(x):
        return lax.ppermute(x, "tp", [(0, 1), (1, 0), (2, 3), (3, 2)])

    def swap_y(x):
        return lax.ppermute(x, "tp", [(0, 2), (2, 0), (1, 3), (3, 1)])

    def swap_z(x):
        return lax.ppermute(x, "rep", [(0, 1), (1, 0), (2, 3), (3, 2)])

    def hop_in(x):
        return lax.ppermute(x, "rep", [(0, 1), (3, 2)])

    def hop_mid(x):
        return lax.ppermute(x, "rep", [(1, 2), (2, 1)])

    def hop_out(x):
        return lax.ppermute(x, "rep", [(1, 0), (2, 3)])

    def whole(shard, axis):
        return lax.all_gather(shard, "seq", axis=axis, tiled=True)

    def local_cols(x):
        if not two:
            return x
        return jnp.where(si == 0, x, jnp.concatenate([x[..., half:], x[..., :half]], -1))

    def own_rows(x, s):
        x = lax.dynamic_slice_in_dim(x, s * length + own * quarter, quarter, 0)
        return local_cols(x)

    def join(own_part, x, z, axis):
        first, second = jnp.where(pz == 0, x, z), jnp.where(pz == 0, z, x)
        return jnp.concatenate([own_part, first, second], axis)

    wq, wo, wd, wg = w_qkv[0, :, 0, :], w_out[0], w_down[0], w_gate_up[0]
    if two:
        gains = jnp.concatenate([norm_gains[0], swap_seq(norm_gains[0])], 1).astype(F32)
        qkv_x = swap_seq(lax.dynamic_slice_in_dim(wq, pz * fourth, fourth, 0))
        out_x = swap_seq(lax.dynamic_slice_in_dim(wo, pz * fourth, fourth, 1))
        n_piece = 4
        got = order(lambda w, p: spread_gate_up(w, p, width, 0, n_piece, []), wg, place)
        gu_w, gu_send = got[0], got[1:]
        gu_x = [swap_seq(gu_send[0])]
    else:
        gains = whole(norm_gains[0], 1).astype(F32)
        qkv_w, out_w, down_w = whole(wq, 0), whole(wo, 1), whole(wd, 1)
        gu_w = spread_gate_up(whole(wg, 0), place, width, None, 0, [])[0]

    first_row = si * length
    ids = jnp.arange(total, dtype=jnp.int32)
    change = jnp.concatenate(
        [jnp.ones((seqs, 1), bool), segments[:, 1:] != segments[:, :-1]], axis=1
    )
    doc_start = lax.cummax(jnp.where(change, ids[None, :], 0), axis=1)
    starts = lax.dynamic_slice_in_dim(doc_start, first_row, length, 1)
    pos = first_row + jnp.arange(length, dtype=jnp.int32)[None, :] - starts
    inverse_freq = ROPE_THETA ** (-(jnp.arange(HEAD_DIM // 2, dtype=F32) / (HEAD_DIM // 2)))
    angles = inverse_freq[None, :, None] * pos.astype(F32)[:, None, :]
    cos_t, sin_t = jnp.cos(angles), jnp.sin(angles)
    starts3 = starts[:, None, :]
    tq, tk = min(256, length), min(256, total)
    tiles = jnp.arange(length // tq, dtype=jnp.int32)
    ends = (first_row + (tiles + 1) * tq + tk - 1) // tk
    bounds = [
        jnp.concatenate(
            [
                jnp.stack([first_row, own]),
                jnp.stack([starts[s, ::tq] // tk, ends], axis=1).reshape(-1),
            ]
        ).astype(jnp.int32)
        for s in range(seqs)
    ]

    hidden = hidden_in.reshape(rows, width)
    d_hidden = cotangent.reshape(rows, width)
    normed1 = order(lambda h, g, p: first_norm(h, g, p, 2 * quarter), hidden, gains[:1], place)
    if two:
        qkv_z, out_z = swap_z(qkv_x), swap_z(out_x)
        gu_w = order(lambda w, p, b: spread_gate_up(w, p, width, 1, 0, [b]), wg, place, gu_w)[0]
        qkv_w = order(lambda a, x, z: join(a, x, z, 0), wq, qkv_x, qkv_z)
    q_t, kv_t = order(
        lambda n, w, c, s: project_qkv(n, w, c, s, group), normed1, [qkv_w], cos_t, sin_t
    )
    if two:
        got = lax.ppermute(kv_t, "seq", [(0, 1)])
        *gu_send, wd_late, kv_t = lax.optimization_barrier((*gu_send, wd, kv_t))
        gu_x += [swap_seq(x) for x in gu_send[1:]]
        ff_half = ff // 2
        down_send = lax.dynamic_slice_in_dim(wd_late, pz * fourth, fourth, 1)
        down_x = [swap_seq(down_send[k * ff_half : (k + 1) * ff_half]) for k in range(2)]
        dhb = order(lambda d, p: local_cast(d, p, quarter), d_hidden, place)
        all_kv = order(
            lambda a, g: jnp.concatenate(
                [jnp.where(si == 0, a, g), jnp.where(si == 0, g, a)], axis=2
            ),
            kv_t,
            got,
        )
        gu_z = [swap_z(x) for x in gu_x]
        down_z = [swap_z(x) for x in down_x]
    else:
        dhb = local_cast(d_hidden, place, quarter)
        all_kv = whole(kv_t, 2)

    piece = 128

    def put_gu(w, x, k, parity):
        return lax.dynamic_update_slice(w, x, (half + parity * fourth + k * piece, 0))

    def put_down(w, x, k, parity):
        return lax.dynamic_update_slice(w, x, (k * (ff // 2), half + parity * fourth))

    att, att_t, lse = [None] * seqs, [None] * seqs, [None] * seqs
    hold, keep = [None] * seqs, [None] * seqs

    def first_sum(k, g):
        x = k + g.astype(F32)
        return x[quarter:].astype(BF16), x[:quarter]

    def attention(s):
        att[s], att_t[s], lse[s] = order(
            lambda q, kv, st, b, s=s: attend(s, q, kv, st, b, scale, quarter),
            q_t, all_kv, starts3, bounds[s],
        )

    def out_product(s):
        send, keep[s] = order(
            lambda a, w, p: split_matmul(a, w, False, False, p, 1), att[s], out_w, place
        )
        hold[s] = swap_core(send)

    def summed(s):
        send, keep[s] = order(first_sum, keep[s], hold[s])
        hold[s] = swap_y(send)

    attention(0)
    if two:
        out_w = order(lambda a, x, z: join(a, x, z, 1), wo, out_x, out_z)
    out_product(0)
    for s in range(1, seqs):
        attention(s)
        summed(s - 1)
        out_product(s)
    if two:
        gu_w = order(lambda w, x: put_gu(w, x, 0, pz), gu_w, gu_x[0])
        gu_w = order(lambda w, x: put_gu(w, x, 1, pz), gu_w, gu_x[1])
    summed(seqs - 1)
    if two:
        gu_w = order(lambda w, x: put_gu(w, x, 0, 1 - pz), gu_w, gu_z[0])
    h2, i2, n2 = [None] * seqs, [None] * seqs, [None] * seqs

    def second_norm(h, k, g, gain):
        x = h + k + g.astype(F32)
        inv = lax.rsqrt(jnp.mean(x * x, axis=-1, keepdims=True) + NORM_EPS)
        return x, inv, (x * inv * gain).astype(BF16)

    def share(x):
        far = swap_y(x)
        return [x, far, swap_core(x), swap_core(far)]

    for s in range(seqs):
        h2[s], i2[s], mine = order(
            lambda h, k, g, gain, s=s: second_norm(own_rows(h, s), k, g, gain),
            hidden, keep[s], hold[s], gains[1],
        )
        n2[s] = share(mine)
    if two:
        down_w = order(lambda w: jnp.concatenate([w, w], 1), wd)
        gu_w = order(lambda w, x: put_gu(w, x, 2, pz), gu_w, gu_x[2])
        gu_w = order(lambda w, x: put_gu(w, x, 1, 1 - pz), gu_w, gu_z[1])
    n2_all = order(lambda a: jnp.concatenate([x for b in a for x in b]), n2)
    if two:
        gu_w = order(lambda w, x: put_gu(w, x, 3, pz), gu_w, gu_x[3])
        gu_w = order(lambda w, x: put_gu(w, x, 2, 1 - pz), gu_w, gu_z[2])
        gu_w = order(lambda w, x: put_gu(w, x, 3, 1 - pz), gu_w, gu_z[3])
    act, gu = order(gate_up, n2_all, gu_w)

    def piece_of(x, k, at, size):
        return x[:, k * half + at : k * half + at + size]

    class Chunk:
        def __init__(self, make, finish=None, dtype=BF16):
            self.make, self.finish, self.dtype, self.stage = make, finish, dtype, 0

        def begin(self, *xs):
            self.xs = xs
            self.got = swap_seq(order(lambda *x: self.make(1, *x).astype(self.dtype), *xs))

        def next(self):
            k = self.stage
            self.stage += 1
            if k == 0:
                self.sum = order(
                    lambda g, *x: (self.make(0, *x) + g.astype(F32)).astype(self.dtype),
                    self.got, *self.xs,
                )
                self.got = hop_in(self.sum)
            elif k < 3:
                self.sum = order(
                    lambda a, b: (a.astype(F32) + b.astype(F32)).astype(self.dtype),
                    self.sum, self.got,
                )
                self.got = hop_mid(self.sum) if k == 1 else hop_out(self.sum)
            elif self.finish is not None:
                self.finish(self.sum, self.got)
            else:
                self.out = order(
                    lambda a, b: jnp.where(middle, a, b).astype(F32), self.sum, self.got
                )

    chunks = {}

    def begin(name, make, *xs, finish=None, dtype=BF16):
        if two:
            chunks[name] = Chunk(make, finish, dtype)
            chunks[name].begin(*xs)

    def go(*names):
        for name in names:
            if two:
                chunks[name].next()

    fr = ff // 2
    gu_rows = [256, 256, 256, 128, 128]
    gu_grad = []

    def begin_down(j):
        begin(
            f"d{j}",
            lambda k, a, d: dot(a[:, j * fr : (j + 1) * fr], piece_of(d, k, 0, half), 0, 0),
            act, dhb,
        )

    def begin_gu(j):
        at = sum(gu_rows[:j])

        def finish(a, b):
            gu_grad[:] = [
                order(
                    lambda a, b, m, g: join_gate_up(a, b, m, at, half, g), a, b, mid_flag, gu_grad
                )
            ]

        begin(
            f"g{j}",
            lambda k, n, d: dot(piece_of(n, k, at, gu_rows[j]), d, 0, 0),
            n2_all, dgu, finish=finish,
        )

    begin_down(0)
    begin_down(1)
    if two:
        down_w = order(lambda w, x: put_down(w, x, 0, pz), down_w, down_x[0])
        down_w = order(lambda w, x: put_down(w, x, 1, pz), down_w, down_x[1])
        down_w = order(lambda w, x: put_down(w, x, 0, 1 - pz), down_w, down_z[0])
        down_w = order(lambda w, x: put_down(w, x, 1, 1 - pz), down_w, down_z[1])
    dgu = order(gate_back, dhb, down_w, gu)

    def product(a, w, transposed, natural):
        got = order(lambda a, w, p: split_matmul(a, w, transposed, natural, p, seqs), a, w, place)
        return list(got[1::2]), [swap_core(x) for x in got[::2]]

    keep, hold = product(dgu, gu_w, True, False)
    go("d0")
    for s in range(seqs):
        summed(s)
    begin_gu(0)
    begin_gu(1)
    gain2 = []
    d_h2, d2 = [None] * seqs, [None] * seqs

    def second_back(k, g, x, inv, d, gain):
        mine = k + g.astype(F32)
        w = gain * mine
        back = inv * w - x * (inv * inv * inv) * jnp.mean(w * x, axis=-1, keepdims=True)
        back = back + d
        return back, back.astype(BF16), jnp.sum(mine * x * inv, axis=0)

    for s in range(seqs):
        d_h2[s], mine, g2 = order(
            lambda k, g, x, inv, d, gain, s=s: second_back(k, g, x, inv, own_rows(d, s), gain),
            keep[s], hold[s], h2[s], i2[s], d_hidden, gains[1],
        )
        gain2.append(g2)
        d2[s] = share(mine)
    go("d1", "d0")
    dq, dkv = [None] * seqs, [None] * seqs

    def out_back(w, d):
        x = dot(w, d, 1, 1).astype(BF16).reshape(-1, 2, 2, quarter)
        x = jnp.where(core == 0, x, x[:, ::-1])
        x = jnp.where(yi == 0, x, x[:, :, ::-1])
        return x.reshape(-1, length)

    for s in range(seqs):
        d2[s] = order(lambda a: jnp.concatenate(a), d2[s])
        d_att_t = order(out_back, out_w, d2[s])
        dq[s], dkv[s] = order(
            lambda *x, s=s: attend_back(s, *x, scale),
            q_t, all_kv, starts3, bounds[s], att_t[s], d_att_t, lse[s], cos_t, sin_t,
        )
    dkv_all = order(lambda a: jnp.stack(a), dkv)
    if two:
        dkv_got = lax.ppermute(dkv_all[:, :, :length].astype(BF16), "seq", [(1, 0)])
    begin(
        "out",
        lambda k, a, d: sum(dot(x, piece_of(y, k, 0, half), 0, 0) for x, y in zip(a, d)),
        att, d2,
    )
    go("g0", "d1", "d0")
    keep, hold = product(act, down_w, False, False)
    if two:
        dkv_mine = lax.dynamic_slice_in_dim(dkv_all, first_row, length, 2) + dkv_got.astype(F32)
    else:
        dkv_mine = lax.psum_scatter(dkv_all, "seq", scatter_dimension=2, tiled=True)

    def make_dqkv(q, kv, c, si_):
        lo, hi = kv[:, : HEAD_DIM // 2], kv[:, HEAD_DIM // 2 : HEAD_DIM]
        k = jnp.concatenate([lo * c + hi * si_, hi * c - lo * si_, kv[:, HEAD_DIM:]], 1)
        k = jnp.swapaxes(k.astype(BF16), 1, 2)
        return jnp.concatenate([jnp.stack(q), k], -1).reshape(rows, qkv_width)

    d_qkv = order(make_dqkv, dq, dkv_mine, cos_t, sin_t)
    keep1, hold1 = product(d_qkv, qkv_w, True, True)
    begin("qkv", lambda k, n, d: dot(piece_of(n, k, 0, half), d, 0, 0), normed1, d_qkv)
    begin_gu(2)
    begin_gu(3)
    begin_gu(4)

    def summed_list(keep, hold):
        for s in range(seqs):
            send, keep[s] = order(first_sum, keep[s], hold[s])
            hold[s] = swap_y(send)

    summed_list(keep1, hold1)
    go("g1", "g0", "d1", "d0")
    gain1 = []
    d1 = [None] * seqs

    def first_back(k, g, x, gain, d2, d):
        mine = k + g.astype(F32)
        inv = lax.rsqrt(jnp.mean(x * x, axis=-1, keepdims=True) + NORM_EPS)
        w = gain * mine
        back = inv * w - x * (inv * inv * inv) * jnp.mean(w * x, axis=-1, keepdims=True)
        return (back + (d2 - d)).astype(BF16), jnp.sum(mine * x * inv, axis=0)

    for s in range(seqs):
        mine, g1 = order(
            lambda k, g, h, gain, d2, d, s=s: first_back(
                k, g, own_rows(h, s), gain, d2, own_rows(d, s)
            ),
            keep1[s], hold1[s], hidden, gains[0], d_h2[s], d_hidden,
        )
        gain1.append(g1)
        d1[s] = share(mine)
    gain_sum = order(lambda a, b: jnp.stack([sum(a), sum(b)]), gain1, gain2)
    add = lambda a, b: a + b
    gain_sum = order(add, gain_sum, swap_core(gain_sum))
    gain_sum = order(add, gain_sum, swap_y(gain_sum))
    begin("gain", lambda k, g: piece_of(g, k, 0, half), gain_sum, dtype=F32)
    summed_list(keep, hold)
    go("out", "g1", "g0", "d1")
    grad_in = order(
        lambda d, x, p: add_local(d, x, p, quarter), d_hidden, [x for b in d1 for x in b], place
    )
    hb = [None] * seqs
    for s in range(seqs):
        mine = order(
            lambda k, g, x, h, s=s: (x + k + g.astype(F32) - own_rows(h, s)).astype(BF16),
            keep[s], hold[s], h2[s], hidden,
        )
        hb[s] = share(mine)
    go("qkv", "out", "g1", "g0")
    go("g2", "qkv", "out", "g1")
    hidden_out = order(
        lambda d, x, p: add_local(d, x, p, quarter), hidden, [x for b in hb for x in b], place
    )
    go("g3", "gain", "g2", "qkv", "out")
    go("g4", "g3", "gain", "g2", "qkv")
    go("g4", "g3", "gain", "g2")
    go("g4", "g3", "gain")
    go("g4")
    if two:
        g_qkv, g_out = chunks["qkv"].out, chunks["out"].out
        g_down = jnp.concatenate([chunks["d0"].out, chunks["d1"].out])
        g_gu, gain_own = gu_grad[0], chunks["gain"].out
    else:

        def reduce_rep(x):
            if n_rep != 4:
                return lax.psum(x.astype(F32), "rep").astype(BF16)
            x = x.astype(BF16)
            x = (x.astype(F32) + hop_in(x).astype(F32)).astype(BF16)
            x = (x.astype(F32) + hop_mid(x).astype(F32)).astype(BF16)
            return jnp.where(middle, x, hop_out(x))

        def reduce(x, axis):
            return reduce_rep(lax.psum_scatter(x, "seq", scatter_dimension=axis, tiled=True))

        g_down = reduce(dot(act, dhb, 0, 0), 1).astype(F32)
        g_out = reduce(sum(dot(x, y, 0, 0) for x, y in zip(att, d2)), 1).astype(F32)
        g_qkv = reduce(dot(normed1, d_qkv, 0, 0), 0).astype(F32)
        g_gu = reduce(dot(n2_all, dgu, 0, 0), 0)
        g_gu = join_gate_up(g_gu, g_gu, mid_flag, 0, g_gu.shape[0], [])
        gain_own = lax.psum_scatter(gain_sum, "seq", scatter_dimension=1, tiled=True)
        gain_own = lax.psum(gain_own, "rep")
    return (
        hidden_out.reshape(seqs, length, width),
        grad_in.reshape(seqs, length, width),
        g_qkv[None, :, None, :],
        g_out[None],
        g_gu,
        g_down[None],
        gain_own[None],
    )


def solution(mesh):
    in_specs = (
        P("rep", "seq", None),
        P("rep", "seq", None),
        P(None, "seq", "tp", None),
        P(None, "tp", "seq"),
        P(None, "seq", None, "tp"),
        P(None, "tp", "seq"),
        P(None, None, "seq"),
        P("rep", None),
    )
    out_specs = (
        P("rep", "seq", None),
        P("rep", "seq", None),
        P(None, "seq", "tp", None),
        P(None, "tp", "seq"),
        P(None, "seq", None, "tp"),
        P(None, "tp", "seq"),
        P(None, None, "seq"),
    )
    sizes = (mesh.shape["seq"], mesh.shape["tp"], mesh.shape["rep"])
    return jax.shard_map(
        functools.partial(per_device, sizes),
        mesh=mesh,
        in_specs=in_specs,
        out_specs=out_specs,
        check_vma=False,
    )
```

```python
import dataclasses
import functools
from typing import Any

import jax
import jax.numpy as jnp
from jax import lax
from jax.experimental import pallas as pl
from jax.experimental.pallas import tpu as pltpu
from jax.sharding import PartitionSpec as P

HEAD_DIM = 64
NORM_EPS = 1e-05
ROPE_THETA = 10000.0
LOG2E = 1.4426950408889634
MASKED = -1e30
F32 = jnp.float32
BF16 = jnp.bfloat16
MIB = 1024 * 1024


def touch(order, *xs):
    order.last = (*order.last, *xs)


def dot(a, b, ca=1, cb=0):
    return lax.dot_general(a, b, (((ca,), (cb,)), ((), ())), preferred_element_type=F32)


def call(body, grid, ins, outs, shapes, scratch=(), scalars=0, alias=None, vmem=20):
    return pl.pallas_call(
        body,
        out_shape=shapes,
        grid_spec=pltpu.PrefetchScalarGridSpec(
            num_scalar_prefetch=scalars,
            grid=grid,
            in_specs=ins,
            out_specs=outs,
            scratch_shapes=list(scratch),
        ),
        input_output_aliases=alias or {},
        compiler_params=pltpu.CompilerParams(vmem_limit_bytes=vmem * MIB),
        cost_estimate=pl.CostEstimate(flops=3000000000, bytes_accessed=8000000, transcendentals=0),
    )


@functools.partial(
    jax.tree_util.register_dataclass, data_fields=["array"], meta_fields=["base", "late"]
)
@dataclasses.dataclass(frozen=True)
class Part:
    array: Any
    base: int = 0
    late: Any = None

    def start(self, width, p):
        if self.late is None:
            return self.base
        return width // 2 + (p ^ self.late) * (width // 4) + self.base


class Order:
    def __init__(self):
        self.last = ()

    def __call__(self, step, *xs):
        flat, tree = jax.tree.flatten(xs)
        if self.last:
            flat = lax.optimization_barrier((tuple(flat), self.last))[0]
        out = step(*jax.tree.unflatten(tree, flat))
        self.last = tuple(jax.tree.leaves(out))
        return out


def first_norm(hidden, gain, place, block):
    rows, width = hidden.shape
    half = width // 2

    def body(p, a_ref, b_ref, g_ref, n_ref):
        a, b = a_ref[...], b_ref[...]
        total = jnp.sum(a * a, -1, keepdims=True) + jnp.sum(b * b, -1, keepdims=True)
        inv = lax.rsqrt(total * (1.0 / width) + NORM_EPS)
        n_ref[:, :half] = (a * inv * g_ref[:, :half]).astype(BF16)
        n_ref[:, half:] = (b * inv * g_ref[:, half:]).astype(BF16)

    return call(
        body,
        (rows // block,),
        [
            pl.BlockSpec((block, half), lambda i, p: (i, p[1])),
            pl.BlockSpec((block, half), lambda i, p: (i, 1 - p[1])),
            pl.BlockSpec((1, width), lambda i, p: (0, 0)),
        ],
        pl.BlockSpec((block, width), lambda i, p: (i, 0)),
        jax.ShapeDtypeStruct((rows, width), BF16),
        scalars=1,
    )(place, hidden, hidden, gain)


def local_cast(x, place, block):
    rows, width = x.shape
    half = width // 2

    def body(p, a_ref, b_ref, o_ref):
        o_ref[:, :half] = a_ref[...].astype(BF16)
        o_ref[:, half:] = b_ref[...].astype(BF16)

    def row(i, p):
        return (i // 4) * 4 + ((i % 4) ^ p[0])

    return call(
        body,
        (rows // block,),
        [
            pl.BlockSpec((block, half), lambda i, p: (row(i, p), p[1])),
            pl.BlockSpec((block, half), lambda i, p: (row(i, p), 1 - p[1])),
        ],
        pl.BlockSpec((block, width), lambda i, p: (i, 0)),
        jax.ShapeDtypeStruct((rows, width), BF16),
        scalars=1,
    )(place, x, x)


def join_gate_up(a, b, middle, at, rows, before):
    count, cols = a.shape
    ff = cols // 2
    block = min(128, count)

    def body(p, a_ref, b_ref, *refs):
        o_ref = refs[-1]

        def put(src):
            for j in range(ff // 128):
                for g in range(2):
                    o_ref[0, :, g, 128 * j : 128 * (j + 1)] = src[
                        :, 256 * j + 128 * g : 256 * j + 128 * (g + 1)
                    ].astype(F32)

        @pl.when(p[0] == 1)
        def _():
            put(a_ref)

        @pl.when(p[0] == 0)
        def _():
            put(b_ref)

    return call(
        body,
        (count // block,),
        [pl.BlockSpec((block, cols), lambda i, p: (i, 0))] * 2
        + [pl.BlockSpec(memory_space=pl.ANY)] * len(before),
        pl.BlockSpec((1, block, 2, ff), lambda i, p: (0, at // block + i, 0, 0)),
        jax.ShapeDtypeStruct((1, rows, 2, ff), F32),
        scalars=1,
        alias={3 + k: k for k in range(len(before))},
    )(middle, a, b, *before)


def project_qkv(normed, weights, cos_t, sin_t, group):
    rows, width = normed.shape
    seqs, half, length = cos_t.shape
    cols = weights[0].shape[1]
    tile = min(256, length)
    per = length // tile
    depth = width // len(weights)
    parts = len(weights)

    def body(n_ref, cos_ref, sin_ref, *refs):
        q_ref, kv_ref = refs[parts:]
        acc = dot(n_ref[:, :depth], refs[0][...])
        for k in range(1, parts):
            acc = acc + dot(n_ref[:, k * depth : (k + 1) * depth], refs[k][...])
        t = acc.T
        cos, sin = cos_ref[0], sin_ref[0]
        for h in range(group + 1):
            a, b = t[2 * half * h : 2 * half * h + half], t[2 * half * h + half : 2 * half * (h + 1)]
            r = jnp.concatenate([a * cos - b * sin, b * cos + a * sin], 0).astype(BF16)
            if h < group:
                q_ref[0, 2 * half * h : 2 * half * (h + 1)] = r
            else:
                kv_ref[0, : 2 * half] = r
        kv_ref[0, 2 * half :] = t[2 * half * (group + 1) :].astype(BF16)

    return call(
        body,
        (seqs, per),
        [
            pl.BlockSpec((tile, width), lambda s, i: (s * per + i, 0)),
            pl.BlockSpec((1, half, tile), lambda s, i: (s, 0, i)),
            pl.BlockSpec((1, half, tile), lambda s, i: (s, 0, i)),
        ]
        + [pl.BlockSpec((depth, cols), lambda s, i: (0, 0))] * parts,
        [
            pl.BlockSpec((1, group * HEAD_DIM, tile), lambda s, i: (s, 0, i)),
            pl.BlockSpec((1, 2 * HEAD_DIM, tile), lambda s, i: (s, 0, i)),
        ],
        [
            jax.ShapeDtypeStruct((seqs, group * HEAD_DIM, length), BF16),
            jax.ShapeDtypeStruct((seqs, 2 * HEAD_DIM, length), BF16),
        ],
    )(normed, cos_t, sin_t, *weights)


def attend(s, q_t, kv_t, starts, bounds, scale):
    seqs, cols, length = q_t.shape
    total = kv_t.shape[2]
    heads = cols // HEAD_DIM
    tq, tk = min(256, length), min(256, total)

    def body(b_ref, q_ref, kv_ref, st_ref, att_ref, att_t_ref, lse_ref, kn, m, l, acc):
        i = pl.program_id(0)

        @pl.when(i == 0)
        def _():
            kn[...] = kv_ref[0, :HEAD_DIM].astype(F32).T.astype(BF16)

        qid = b_ref[0] + i * tq + lax.broadcasted_iota(jnp.int32, (1, tq), 1)
        start = st_ref[0]
        m[...] = jnp.full_like(m, MASKED)
        l[...] = jnp.zeros_like(l)
        acc[...] = jnp.zeros_like(acc)

        def step(t, _):
            k0 = pl.multiple_of(t * tk, tk)
            kid = k0 + lax.broadcasted_iota(jnp.int32, (tk, 1), 0)
            ok = (kid <= qid) & (kid >= start)
            keys = kn[pl.ds(k0, tk), :]
            vals = kv_ref[0, HEAD_DIM:, pl.ds(k0, tk)]
            for h in range(heads):
                lo = h * HEAD_DIM
                sc = dot(keys, q_ref[0, lo : lo + HEAD_DIM]) * (scale * LOG2E)
                sc = jnp.where(ok, sc, MASKED)
                old = m[h : h + 1]
                new = jnp.maximum(old, jnp.max(sc, 0, keepdims=True))
                e = jnp.exp2(sc - new)
                fade = jnp.exp2(old - new)
                m[h : h + 1] = new
                l[h : h + 1] = l[h : h + 1] * fade + jnp.sum(e, 0, keepdims=True)
                acc[lo : lo + HEAD_DIM] = acc[lo : lo + HEAD_DIM] * fade + dot(vals, e.astype(BF16))
            return 0

        lax.fori_loop(b_ref[2 + 2 * i], b_ref[3 + 2 * i], step, 0)
        for h in range(heads):
            lo = h * HEAD_DIM
            acc[lo : lo + HEAD_DIM] = acc[lo : lo + HEAD_DIM] / l[h : h + 1]
        att_t_ref[...] = acc[...].astype(BF16)
        att_ref[...] = acc[...].T.astype(BF16)
        lse_ref[...] = m[...] + jnp.log2(l[...])

    return call(
        body,
        (length // tq,),
        [
            pl.BlockSpec((1, cols, tq), lambda i, b: (s, 0, i)),
            pl.BlockSpec((1, 2 * HEAD_DIM, total), lambda i, b: (s, 0, 0)),
            pl.BlockSpec((1, 1, tq), lambda i, b: (s, 0, i)),
        ],
        [
            pl.BlockSpec((tq, cols), lambda i, b: (i, 0)),
            pl.BlockSpec((cols, tq), lambda i, b: (0, i)),
            pl.BlockSpec((heads, tq), lambda i, b: (0, i)),
        ],
        [
            jax.ShapeDtypeStruct((length, cols), BF16),
            jax.ShapeDtypeStruct((cols, length), BF16),
            jax.ShapeDtypeStruct((heads, length), F32),
        ],
        scratch=[
            pltpu.VMEM((total, HEAD_DIM), BF16),
            pltpu.VMEM((heads, tq), F32),
            pltpu.VMEM((heads, tq), F32),
            pltpu.VMEM((cols, tq), F32),
        ],
        scalars=1,
    )(bounds, q_t, kv_t, starts)


def attend_back(s, q_t, kv_t, starts, bounds, att_t, out_parts, d2, lse, cos_t, sin_t, scale):
    seqs, cols, length = q_t.shape
    width = d2.shape[1]
    parts = len(out_parts)
    total = kv_t.shape[2]
    heads = cols // HEAD_DIM
    half = HEAD_DIM // 2
    tq, tk = min(256, length), min(256, total)

    def body(
        b_ref, q_ref, kv_ref, st_ref, a_ref, d2_ref, lse_ref, cos_ref, sin_ref, *refs
    ):
        w_refs = refs[:parts]
        dq_ref, dkv_ref, early_ref, kn, vn, delta, acc, d_ref = refs[parts:]
        i = pl.program_id(0)

        @pl.when(i == 0)
        def _():
            kn[...] = kv_ref[0, :HEAD_DIM].astype(F32).T.astype(BF16)
            vn[...] = kv_ref[0, HEAD_DIM:].astype(F32).T.astype(BF16)
            dkv_ref[...] = jnp.zeros_like(dkv_ref)

        d_att = 0.0
        for part, w_ref in zip(out_parts, w_refs):
            size = part.array.shape[1]
            at = part.start(width, b_ref[1])
            if part.late is not None:
                at = pl.multiple_of(at, 128)
            d_att = d_att + dot(w_ref[...], d2_ref[:, pl.ds(at, size)], 1, 1)
        d_ref[...] = d_att.astype(BF16)
        qid = b_ref[0] + i * tq + lax.broadcasted_iota(jnp.int32, (1, tq), 1)
        start = st_ref[0]
        for h in range(heads):
            lo = h * HEAD_DIM
            prod = d_ref[lo : lo + HEAD_DIM].astype(F32) * a_ref[lo : lo + HEAD_DIM].astype(F32)
            delta[h : h + 1] = jnp.sum(prod, 0, keepdims=True)
        acc[...] = jnp.zeros_like(acc)

        def step(t, _):
            k0 = pl.multiple_of(t * tk, tk)
            kid = k0 + lax.broadcasted_iota(jnp.int32, (tk, 1), 0)
            ok = (kid <= qid) & (kid >= start)
            keys, vals = kn[pl.ds(k0, tk), :], vn[pl.ds(k0, tk), :]
            keys_t = kv_ref[0, :HEAD_DIM, pl.ds(k0, tk)]
            dk = jnp.zeros((HEAD_DIM, tk), F32)
            dv = jnp.zeros((HEAD_DIM, tk), F32)
            for h in range(heads):
                lo = h * HEAD_DIM
                q, d = q_ref[0, lo : lo + HEAD_DIM], d_ref[lo : lo + HEAD_DIM]
                sc = dot(keys, q) * (scale * LOG2E) - lse_ref[h : h + 1]
                p = jnp.exp2(jnp.where(ok, sc, MASKED))
                dp = dot(vals, d)
                ds = (p * (dp - delta[h : h + 1]) * scale).astype(BF16)
                dv = dv + dot(d, p.astype(BF16), 1, 1)
                dk = dk + dot(q, ds, 1, 1)
                acc[lo : lo + HEAD_DIM] += dot(keys_t, ds)
            dkv_ref[:HEAD_DIM, pl.ds(k0, tk)] += dk
            dkv_ref[HEAD_DIM:, pl.ds(k0, tk)] += dv
            return 0

        lax.fori_loop(b_ref[2 + 2 * i], b_ref[3 + 2 * i], step, 0)
        cos, sin = cos_ref[0], sin_ref[0]
        for h in range(heads):
            lo = h * HEAD_DIM
            c, e = acc[lo : lo + half], acc[lo + half : lo + HEAD_DIM]
            acc[lo : lo + HEAD_DIM] = jnp.concatenate([c * cos + e * sin, e * cos - c * sin], 0)
        dq_ref[...] = acc[...].T.astype(BF16)
        early_ref[...] = dkv_ref[:, :length].astype(BF16)

    return call(
        body,
        (length // tq,),
        [
            pl.BlockSpec((1, cols, tq), lambda i, b: (s, 0, i)),
            pl.BlockSpec((1, 2 * HEAD_DIM, total), lambda i, b: (s, 0, 0)),
            pl.BlockSpec((1, 1, tq), lambda i, b: (s, 0, i)),
            pl.BlockSpec((cols, tq), lambda i, b: (0, i)),
            pl.BlockSpec((tq, d2.shape[1]), lambda i, b: (i, 0)),
            pl.BlockSpec((heads, tq), lambda i, b: (0, i)),
            pl.BlockSpec((1, half, tq), lambda i, b: (s, 0, i)),
            pl.BlockSpec((1, half, tq), lambda i, b: (s, 0, i)),
        ]
        + [pl.BlockSpec(p.array.shape, lambda i, b: (0, 0)) for p in out_parts],
        [
            pl.BlockSpec((tq, cols), lambda i, b: (i, 0)),
            pl.BlockSpec((2 * HEAD_DIM, total), lambda i, b: (0, 0)),
            pl.BlockSpec((2 * HEAD_DIM, length), lambda i, b: (0, 0)),
        ],
        [
            jax.ShapeDtypeStruct((length, cols), BF16),
            jax.ShapeDtypeStruct((2 * HEAD_DIM, total), F32),
            jax.ShapeDtypeStruct((2 * HEAD_DIM, length), BF16),
        ],
        scratch=[
            pltpu.VMEM((total, HEAD_DIM), BF16),
            pltpu.VMEM((total, HEAD_DIM), BF16),
            pltpu.VMEM((heads, tq), F32),
            pltpu.VMEM((cols, tq), F32),
            pltpu.VMEM((cols, tq), BF16),
        ],
        scalars=1,
    )(
        bounds, q_t, kv_t, starts, att_t, d2, lse, cos_t, sin_t, *[p.array for p in out_parts]
    )


def join_kv(mine, other, place):
    seqs, cols, length = mine.shape

    def body(p, m_ref, o_ref, out_ref):
        @pl.when(pl.program_id(0) == 0)
        def _():
            out_ref[...] = m_ref[...]

        @pl.when(pl.program_id(0) == 1)
        def _():
            out_ref[...] = o_ref[...]

    spec = pl.BlockSpec(mine.shape, lambda i, p: (0, 0, 0))
    return call(
        body,
        (2,),
        [spec, spec],
        pl.BlockSpec(mine.shape, lambda i, p: (0, 0, i ^ p[1])),
        jax.ShapeDtypeStruct((seqs, cols, 2 * length), mine.dtype),
        scalars=1,
    )(place, mine, other)


def stack(pieces, place):
    quarter, width = pieces[0].shape
    count = len(pieces)

    def body(p, *refs):
        for k in range(count):

            @pl.when(pl.program_id(0) == k)
            def _():
                refs[-1][...] = refs[k][...]

    return call(
        body,
        (count,),
        [pl.BlockSpec((quarter, width), lambda i, p: (0, 0))] * count,
        pl.BlockSpec((quarter, width), lambda i, p: ((i // 4) * 4 + ((i % 4) ^ p[0]), 0)),
        jax.ShapeDtypeStruct((count * quarter, width), BF16),
        scalars=1,
    )(place, *pieces)


def first_sum(keep, got):
    rows, width = keep.shape
    half = rows // 2
    tile = width // 4

    def body(k_ref, g_ref, send_ref, keep_ref):
        send_ref[...] = (k_ref[half:] + g_ref[half:].astype(F32)).astype(BF16)
        keep_ref[...] = k_ref[:half] + g_ref[:half].astype(F32)

    return call(
        body,
        (4,),
        [pl.BlockSpec((rows, tile), lambda j: (0, j))] * 2,
        [pl.BlockSpec((half, tile), lambda j: (0, j))] * 2,
        [jax.ShapeDtypeStruct((half, width), BF16), jax.ShapeDtypeStruct((half, width), F32)],
    )(keep, got)


def by_rows(step, place, s, quarter, owned, blocks, vectors, outs, sums=0):
    width = owned[0].shape[1]
    half = width // 2
    tile = min(32, quarter)
    per = quarter // tile
    seqs = owned[0].shape[0] // (4 * quarter) if s is None else 1
    n_in = 2 * len(owned) + len(blocks) + len(vectors)

    def body(p, *refs):
        vals = [
            jnp.concatenate([refs[2 * k][...], refs[2 * k + 1][...]], 1) for k in range(len(owned))
        ]
        vals += [r[...].astype(F32) for r in refs[2 * len(owned) : n_in]]
        got = step(*vals)
        for k in range(len(outs)):
            refs[n_in + k][...] = got[k].astype(outs[k])
        for k in range(sums):
            o_ref, x = refs[n_in + len(outs) + k], got[len(outs) + k]

            @pl.when(pl.program_id(0) == 0)
            def _():
                o_ref[...] = x

            @pl.when(pl.program_id(0) > 0)
            def _():
                o_ref[...] += x

    def at(i, p):
        if s is None:
            return ((i // per) * 4 + p[0]) * per + i % per
        return (s * 4 + p[0]) * per + i

    own_specs = [
        pl.BlockSpec((tile, half), lambda i, p: (at(i, p), p[1])),
        pl.BlockSpec((tile, half), lambda i, p: (at(i, p), 1 - p[1])),
    ]
    return call(
        body,
        (seqs * per,),
        own_specs * len(owned)
        + [pl.BlockSpec((tile, width), lambda i, p: (i, 0))] * len(blocks)
        + [pl.BlockSpec((1, width), lambda i, p: (0, 0))] * len(vectors),
        [pl.BlockSpec((tile, width), lambda i, p: (i, 0))] * len(outs)
        + [pl.BlockSpec((1, width), lambda i, p: (0, 0))] * sums,
        [jax.ShapeDtypeStruct((seqs * quarter, width), d) for d in outs]
        + [jax.ShapeDtypeStruct((1, width), F32)] * sums,
        scalars=1,
    )(place, *[x for a in owned for x in (a, a)], *blocks, *vectors)


def pack_dqkv(dqs, dkvs, others, cos_t, sin_t, place, seq_block):
    seqs = len(dqs)
    length, cols = dqs[0].shape
    half = HEAD_DIM // 2
    wide = cols + 2 * HEAD_DIM

    def body(p, cos_ref, sin_ref, *refs):
        o_ref = refs[-1]
        for s in range(seqs):

            @pl.when(pl.program_id(0) == s)
            def _():
                kv = refs[seqs + s][...]
                if others:
                    kv = kv + refs[2 * seqs + s][...].astype(F32)
                c, e = kv[:half], kv[half:HEAD_DIM]
                cos, sin = cos_ref[0], sin_ref[0]
                kv = jnp.concatenate([c * cos + e * sin, e * cos - c * sin, kv[HEAD_DIM:]], 0)
                o_ref[:, :cols] = refs[s][...]
                o_ref[:, cols:] = kv.T.astype(BF16)

    const = lambda i, p: (0, 0)
    return call(
        body,
        (seqs,),
        [pl.BlockSpec((1, half, length), lambda i, p: (i, 0, 0))] * 2
        + [pl.BlockSpec((length, cols), const)] * seqs
        + [
            pl.BlockSpec((2 * HEAD_DIM, length), lambda i, p: (0, p[1] if seq_block else 0))
        ]
        * seqs
        + [pl.BlockSpec((2 * HEAD_DIM, length), const)] * len(others),
        pl.BlockSpec((length, wide), lambda i, p: (i, 0)),
        jax.ShapeDtypeStruct((seqs * length, wide), BF16),
        scalars=1,
    )(place, cos_t, sin_t, *dqs, *dkvs, *others)


def add_pair(a, b):
    rows, cols = a.shape
    block = rows // 4

    def body(a_ref, b_ref, o_ref):
        o_ref[...] = (a_ref[...].astype(F32) + b_ref[...].astype(F32)).astype(BF16)

    spec = pl.BlockSpec((block, cols), lambda i: (i, 0))
    return call(body, (4,), [spec, spec], spec, jax.ShapeDtypeStruct((rows, cols), BF16))(a, b)


def place_rows(a, b, middle, at, rows, before):
    count, cols = a.shape
    block = 128

    def body(p, a_ref, b_ref, *refs):
        o_ref = refs[-1]

        @pl.when(p[0] == 1)
        def _():
            o_ref[...] = a_ref[...].astype(F32)

        @pl.when(p[0] == 0)
        def _():
            o_ref[...] = b_ref[...].astype(F32)

    return call(
        body,
        (count // block,),
        [pl.BlockSpec((block, cols), lambda i, p: (i, 0))] * 2
        + [pl.BlockSpec(memory_space=pl.ANY)] * len(before),
        pl.BlockSpec((block, cols), lambda i, p: (at // block + i, 0)),
        jax.ShapeDtypeStruct((rows, cols), F32),
        scalars=1,
        alias={3 + k: k for k in range(len(before))},
    )(middle, a, b, *before)


def spread_gate_up(w, place, blocks, apart, before):
    rows, _, ff = w.shape
    block = min(128, rows)
    steps = rows // block if blocks is None else len(blocks)

    def body(p, w_ref, *refs):
        outs = refs[len(before) :]
        for j in range(ff // 128):
            for g in range(2):
                outs[0][:, 256 * j + 128 * g : 256 * j + 128 * (g + 1)] = w_ref[
                    :, g, 128 * j : 128 * (j + 1)
                ]
        if apart:
            outs[1][...] = outs[0][...]

    def row(i, p):
        if blocks is None:
            return i
        r = blocks[0](p)
        for k in range(1, steps):
            r = jnp.where(i == k, blocks[k](p), r)
        return r

    return call(
        body,
        (steps,),
        [pl.BlockSpec((block, 2, ff), lambda i, p: (row(i, p), 0, 0))]
        + [pl.BlockSpec(memory_space=pl.ANY)] * len(before),
        [pl.BlockSpec((block, 2 * ff), lambda i, p: (row(i, p), 0))]
        + [pl.BlockSpec((block, 2 * ff), lambda i, p: (i, 0))] * apart,
        [jax.ShapeDtypeStruct((rows, 2 * ff), BF16)]
        + [jax.ShapeDtypeStruct((steps * block, 2 * ff), BF16)] * apart,
        scalars=1,
        alias={2 + k: k for k in range(len(before))},
    )(place, w, *before)


def gate_up(pieces, parts, place):
    quarter, width = pieces[0].shape
    count = len(pieces)
    rows = count * quarter
    own, rest = parts[0].array, parts[1:]
    depth = own.shape[0]
    ff = own.shape[1] // 2
    tile = 128

    def body(p, *refs):
        own_ref, *rest_refs = refs[count : count + len(parts)]
        n_ref, act_ref, gu_ref, w_ref = refs[count + len(parts) :]

        @pl.when(pl.program_id(0) == 0)
        def _():
            for k in range(count):
                n_ref[k * quarter : (k + 1) * quarter] = refs[k][...]

        gu = dot(n_ref[:, :depth], own_ref[...])
        if rest:
            for part, ref in zip(rest, rest_refs):
                size = part.array.shape[0]
                at = pl.multiple_of(part.start(width, p[2]) - depth, 128)
                w_ref[pl.ds(at, size), :] = ref[...]
            gu = gu + dot(n_ref[:, depth:], w_ref[...])
        gate, up = gu[:, :tile], gu[:, tile:]
        sig = 1.0 / (1.0 + jnp.exp2(gate * (-LOG2E)))
        act_ref[...] = (gate * sig * up).astype(BF16)
        gu_ref[...] = gu.astype(BF16)

    return call(
        body,
        (ff // tile,),
        [pl.BlockSpec((quarter, width), lambda j, p: (0, 0), pipeline_mode=pl.Buffered(1))] * count
        + [pl.BlockSpec((x.array.shape[0], 2 * tile), lambda j, p: (0, j)) for x in parts],
        [
            pl.BlockSpec((rows, width), lambda j, p: (0, 0)),
            pl.BlockSpec((rows, tile), lambda j, p: (0, j)),
            pl.BlockSpec((rows, 2 * tile), lambda j, p: (0, j)),
        ],
        [
            jax.ShapeDtypeStruct((rows, width), BF16),
            jax.ShapeDtypeStruct((rows, ff), BF16),
            jax.ShapeDtypeStruct((rows, 2 * ff), BF16),
        ],
        scratch=[pltpu.VMEM((max(width - depth, 8), 2 * tile), BF16)],
        scalars=1,
        vmem=30,
    )(place, *pieces, *[x.array for x in parts])


def gate_back(dhb, parts, gu, place):
    rows, width = dhb.shape
    ff = parts[0].array.shape[0]
    tile = 256

    def body(p, d_ref, gu_ref, *refs):
        o_ref = refs[-1]
        d_act = 0.0
        for part, ref in zip(parts, refs):
            at = part.start(width, p[2])
            if part.late is not None:
                at = pl.multiple_of(at, 128)
            d_act = d_act + dot(d_ref[:, pl.ds(at, part.array.shape[1])], ref[...], 1, 1)
        for k in range(tile // 128):
            d = d_act[:, 128 * k : 128 * (k + 1)]
            gate = gu_ref[:, 256 * k : 256 * k + 128].astype(F32)
            up = gu_ref[:, 256 * k + 128 : 256 * (k + 1)].astype(F32)
            sig = 1.0 / (1.0 + jnp.exp2(gate * (-LOG2E)))
            o_ref[:, 256 * k : 256 * k + 128] = (
                d * up * sig * (1.0 + gate * (1.0 - sig))
            ).astype(BF16)
            o_ref[:, 256 * k + 128 : 256 * (k + 1)] = (d * gate * sig).astype(BF16)

    return call(
        body,
        (pl.cdiv(ff, tile),),
        [
            pl.BlockSpec((rows, width), lambda j, p: (0, 0)),
            pl.BlockSpec((rows, 2 * tile), lambda j, p: (0, j)),
        ]
        + [pl.BlockSpec((tile, x.array.shape[1]), lambda j, p: (j, 0)) for x in parts],
        pl.BlockSpec((rows, 2 * tile), lambda j, p: (0, j)),
        jax.ShapeDtypeStruct((rows, 2 * ff), BF16),
        scalars=1,
    )(place, dhb, gu, *[x.array for x in parts])


def split_matmul(a, parts, transposed, natural, place, seqs):
    rows, depth = a.shape
    axis = 0 if transposed else 1
    tile = 256
    counts = [x.array.shape[axis] // tile for x in parts]
    bases = [sum(counts[:k]) for k in range(len(parts))]
    cols = tile * sum(counts)
    length = rows // seqs
    quarter = length // 4

    def body(p, a_ref, *refs):
        w_refs, outs, acc = refs[: len(parts)], refs[len(parts) : -1], refs[-1]
        j = pl.program_id(0)
        for k, w_ref in enumerate(w_refs):

            @pl.when((j >= bases[k]) & (j < bases[k] + counts[k]))
            def _():
                acc[...] = dot(a_ref[...], w_ref[...], 1, 1 - axis)

        for s in range(seqs):
            send, keep = outs[2 * s], outs[2 * s + 1]
            for b in range(4):
                at = s * length + (b ^ p[0] if natural else b) * quarter
                part = acc[pl.ds(at, quarter), :]
                to = (b % 2) * quarter
                if b < 2:
                    keep[to : to + quarter] = part
                else:
                    send[to : to + quarter] = part.astype(BF16)

    def w_spec(k):
        def index(j, p):
            t = jnp.clip(j - bases[k], 0, counts[k] - 1)
            return (t, 0) if transposed else (0, t)

        shape = (tile, depth) if transposed else (depth, tile)
        once = {"pipeline_mode": pl.Buffered(1)} if counts[k] == 1 else {}
        return pl.BlockSpec(shape, index, **once)

    def column(j, p):
        c = j
        for k in range(1, len(parts)):
            at = parts[k].start(cols, p[2]) // tile + j - bases[k]
            c = jnp.where(j >= bases[k], at, c)
        return (0, c)

    return call(
        body,
        (sum(counts),),
        [pl.BlockSpec((rows, depth), lambda j, p: (0, 0), pipeline_mode=pl.Buffered(1))]
        + [w_spec(k) for k in range(len(parts))],
        [pl.BlockSpec((length // 2, tile), column)] * (2 * seqs),
        [
            jax.ShapeDtypeStruct((length // 2, cols), BF16),
            jax.ShapeDtypeStruct((length // 2, cols), F32),
        ]
        * seqs,
        scratch=[pltpu.VMEM((rows, tile), F32)],
        scalars=1,
    )(place, a, *[x.array for x in parts])


def full_matmul(a, parts, transposed, place, seqs, extras):
    rows, depth = a.shape
    axis = 0 if transposed else 1
    tile = 256
    counts = [x.array.shape[axis] // tile for x in parts]
    bases = [sum(counts[:k]) for k in range(len(parts))]
    cols = tile * sum(counts)
    length = rows // seqs
    quarter = length // 4

    def body(p, a_ref, *refs):
        w_refs, o_ref, acc = refs[: len(parts)], refs[-2], refs[-1]
        j = pl.program_id(0)
        for k, w_ref in enumerate(w_refs):

            @pl.when((j >= bases[k]) & (j < bases[k] + counts[k]))
            def _():
                acc[...] = dot(a_ref[...], w_ref[...], 1, 1 - axis)

        if not extras:
            o_ref[...] = acc[...].astype(BF16)
        for s in range(len(extras)):
            for b in range(4):
                part = acc[s * length + b * quarter : s * length + (b + 1) * quarter]
                if b == 0:
                    part = part + refs[len(parts) + s][...].astype(F32)
                at = pl.multiple_of(s * length + (b ^ p[0]) * quarter, quarter)
                o_ref[pl.ds(at, quarter), :] = part.astype(BF16)

    def w_spec(k):
        def index(j, p):
            t = jnp.clip(j - bases[k], 0, counts[k] - 1)
            return (t, 0) if transposed else (0, t)

        return pl.BlockSpec((tile, depth) if transposed else (depth, tile), index)

    def column(j, p):
        c = j
        for k in range(1, len(parts)):
            c = jnp.where(j >= bases[k], parts[k].start(cols, p[2]) // tile + j - bases[k], c)
        return (0, c)

    return call(
        body,
        (sum(counts),),
        [pl.BlockSpec((rows, depth), lambda j, p: (0, 0), pipeline_mode=pl.Buffered(1))]
        + [w_spec(k) for k in range(len(parts))]
        + [pl.BlockSpec((quarter, tile), column)] * len(extras),
        pl.BlockSpec((rows, tile), column),
        jax.ShapeDtypeStruct((rows, cols), BF16),
        scratch=[pltpu.VMEM((rows, tile), F32)],
        scalars=1,
    )(place, a, *[x.array for x in parts], *extras)


def put_columns(o_ref, x, swapped, half):
    @pl.when(swapped == 0)
    def _():
        o_ref[...] = x

    @pl.when(swapped == 1)
    def _():
        o_ref[:, :half] = x[:, half:]
        o_ref[:, half:] = x[:, :half]


def add_columns(x, delta, place, block):
    rows, width = x.shape
    half = width // 2

    def body(p, a_ref, b_ref, d_ref, o_ref):
        mine = jnp.concatenate([a_ref[...], b_ref[...]], 1) + d_ref[...].astype(F32)
        put_columns(o_ref, mine, p[1], half)

    return call(
        body,
        (rows // block,),
        [
            pl.BlockSpec((block, half), lambda i, p: (i, p[1])),
            pl.BlockSpec((block, half), lambda i, p: (i, 1 - p[1])),
            pl.BlockSpec((block, width), lambda i, p: (i, 0)),
        ],
        pl.BlockSpec((block, width), lambda i, p: (i, 0)),
        jax.ShapeDtypeStruct((rows, width), F32),
        scalars=1,
    )(place, x, x, delta)


def first_norm_back(x, upstream, d2, gain, place, block):
    rows, width = x.shape
    half = width // 2
    per = d2[0].shape[0] // block
    count = len(d2)

    def body(p, a_ref, b_ref, u_ref, g_ref, *refs):
        o_ref, sum_ref = refs[count:]
        i = pl.program_id(0)
        h = jnp.concatenate([a_ref[...], b_ref[...]], 1)
        inv = lax.rsqrt(jnp.mean(h * h, axis=-1, keepdims=True) + NORM_EPS)
        mine = u_ref[...].astype(F32)
        w = g_ref[...] * mine
        back = inv * w - h * (inv * inv * inv) * jnp.mean(w * h, axis=-1, keepdims=True)
        for s in range(count):

            @pl.when(i // per == s)
            def _():
                put_columns(o_ref, back + refs[s][...].astype(F32), p[1], half)

        total = jnp.sum(mine * h * inv, axis=0, keepdims=True)

        @pl.when(i == 0)
        def _():
            sum_ref[...] = total

        @pl.when(i > 0)
        def _():
            sum_ref[...] += total

    def spec(s):
        return pl.BlockSpec((block, width), lambda i, p: (jnp.clip(i - s * per, 0, per - 1), 0))

    return call(
        body,
        (rows // block,),
        [
            pl.BlockSpec((block, half), lambda i, p: (i, p[1])),
            pl.BlockSpec((block, half), lambda i, p: (i, 1 - p[1])),
            pl.BlockSpec((block, width), lambda i, p: (i, 0)),
            pl.BlockSpec((1, width), lambda i, p: (0, 0)),
        ]
        + [spec(s) for s in range(count)],
        [
            pl.BlockSpec((block, width), lambda i, p: (i, 0)),
            pl.BlockSpec((1, width), lambda i, p: (0, 0)),
        ],
        [jax.ShapeDtypeStruct((rows, width), F32), jax.ShapeDtypeStruct((1, width), F32)],
        scalars=1,
    )(place, x, x, upstream, gain, *d2)


def per_device(
    sizes, hidden_in, cotangent, w_qkv, w_out, w_gate_up, w_down, norm_gains, segments
):
    n_seq, n_tp, n_rep = sizes
    seqs, length, width = hidden_in.shape
    total = segments.shape[1]
    qkv_width = w_qkv.shape[3]
    group = qkv_width // HEAD_DIM - 2
    ff = w_down.shape[1]
    rows = seqs * length
    scale = float(HEAD_DIM) ** (-0.5)
    two = n_seq == 2
    si = lax.axis_index("seq")
    ti = lax.axis_index("tp")
    zi = lax.axis_index("rep")
    core, yi = ti % 2, ti // 2
    half = width // 2
    fourth = width // 4
    quarter = length // 4
    own = core * 2 + yi
    col_swap = si if two else jnp.int32(0) * si
    pz = zi % 2
    place = jnp.stack([own, col_swap, pz]).astype(jnp.int32)
    middle = (zi == 1) | (zi == 2)
    mid_flag = jnp.reshape(middle, (1,)).astype(jnp.int32)
    order = Order()

    def swap_seq(x):
        return lax.ppermute(x, "seq", [(0, 1), (1, 0)])

    def swap_core(x):
        return lax.ppermute(x, "tp", [(0, 1), (1, 0), (2, 3), (3, 2)])

    def swap_y(x):
        return lax.ppermute(x, "tp", [(0, 2), (2, 0), (1, 3), (3, 1)])

    def swap_z(x):
        return lax.ppermute(x, "rep", [(0, 1), (1, 0), (2, 3), (3, 2)])

    def hop_in(x):
        return lax.ppermute(x, "rep", [(0, 1), (3, 2)])

    def hop_mid(x):
        return lax.ppermute(x, "rep", [(1, 2), (2, 1)])

    def hop_out(x):
        return lax.ppermute(x, "rep", [(1, 0), (2, 3)])

    def whole(shard, axis):
        return lax.all_gather(shard, "seq", axis=axis, tiled=True)

    def now(*xs):
        return lax.optimization_barrier((xs, order.last))[0]

    def share(x):
        far = swap_y(x)
        return [x, far, swap_core(x), swap_core(far)]

    wq, wo, wd, wg = w_qkv[0, :, 0, :], w_out[0], w_down[0], w_gate_up[0]
    if two:
        gains = jnp.concatenate([norm_gains[0], swap_seq(norm_gains[0])], 1).astype(F32)
        qkv_parts = [Part(wq), Part(swap_seq(wq), half)]
        out_x = swap_seq(lax.dynamic_slice_in_dim(wo, pz * fourth, fourth, 1))
        gu_own, gu_a = order(
            lambda w, p: spread_gate_up(w, p, [lambda p: 4 * p[2]], 1, []), wg, place
        )
    else:
        gains = whole(norm_gains[0], 1).astype(F32)
        qkv_parts, out_parts = [Part(whole(wq, 0))], [Part(whole(wo, 1))]
        down_parts = [Part(whole(wd, 1))]
        gu_parts = [Part(spread_gate_up(whole(wg, 0), place, None, 0, [])[0])]

    first_row = si * length
    ids = jnp.arange(total, dtype=jnp.int32)
    change = jnp.concatenate(
        [jnp.ones((seqs, 1), bool), segments[:, 1:] != segments[:, :-1]], axis=1
    )
    doc_start = lax.cummax(jnp.where(change, ids[None, :], 0), axis=1)
    starts = lax.dynamic_slice_in_dim(doc_start, first_row, length, 1)
    pos = first_row + jnp.arange(length, dtype=jnp.int32)[None, :] - starts
    inverse_freq = ROPE_THETA ** (-(jnp.arange(HEAD_DIM // 2, dtype=F32) / (HEAD_DIM // 2)))
    angles = inverse_freq[None, :, None] * pos.astype(F32)[:, None, :]
    cos_t, sin_t = jnp.cos(angles), jnp.sin(angles)
    starts3 = starts[:, None, :]
    tq, tk = min(256, length), min(256, total)
    tiles = jnp.arange(length // tq, dtype=jnp.int32)
    ends = (first_row + (tiles + 1) * tq + tk - 1) // tk
    bounds = [
        jnp.concatenate(
            [
                jnp.stack([first_row, pz]),
                jnp.stack([starts[s, ::tq] // tk, ends], axis=1).reshape(-1),
            ]
        ).astype(jnp.int32)
        for s in range(seqs)
    ]

    hidden = hidden_in.reshape(rows, width)
    d_hidden = cotangent.reshape(rows, width)
    late_blocks = [lambda p, k=k: 4 * (1 - p[2]) + k for k in (0, 2, 3)]
    normed1 = order(lambda h, g, p: first_norm(h, g, p, 2 * quarter), hidden, gains[:1], place)
    if two:
        gu_own = order(lambda w, p, b: spread_gate_up(w, p, late_blocks, 0, [b]), wg, place, gu_own)[0]
    dhb = order(lambda d, p: local_cast(d, p, quarter), d_hidden, place)
    q_t, kv_t = order(
        lambda n, w, c, s: project_qkv(n, w, c, s, group),
        normed1, [x.array for x in qkv_parts], cos_t, sin_t,
    )
    if two:
        kv_got = lax.ppermute(kv_t, "seq", [(0, 1)])
        gu_x = [swap_seq(*now(gu_a))]
        blocks_b = [lambda p, k=k: 4 * p[2] + k for k in (2, 3)]
        gu_own, gu_b = order(
            lambda w, p, b: spread_gate_up(w, p, blocks_b, 1, [b]), wg, place, gu_own
        )
        out_z = swap_z(*now(out_x))
        all_kv = order(join_kv, kv_t, kv_got, place)
        out_parts = [Part(wo), Part(out_x, 0, 0), Part(out_z, 0, 1)]
    else:
        all_kv = whole(kv_t, 2)

    att, att_t, lse = [None] * seqs, [None] * seqs, [None] * seqs
    hold, keep = [None] * seqs, [None] * seqs

    def attention(s):
        att[s], att_t[s], lse[s] = order(
            lambda q, kv, st, b, s=s: attend(s, q, kv, st, b, scale),
            q_t, all_kv, starts3, bounds[s],
        )

    def out_product(s):
        send, keep[s] = order(
            lambda a, w, p: split_matmul(a, w, False, True, p, 1), att[s], out_parts, place
        )
        hold[s] = swap_core(send)

    def summed(keep, hold, s):
        send, keep[s] = order(first_sum, keep[s], hold[s])
        hold[s] = swap_y(send)

    attention(0)
    if two:
        touch(order, gu_x[0])
        gu_z = [swap_z(*now(gu_x[0]))]
        gu_x += [swap_seq(*now(gu_b))]
    out_product(0)
    for s in range(1, seqs):
        attention(s)
        summed(keep, hold, s - 1)
        out_product(s)
    if two:
        blocks_c = [lambda p: 1, lambda p: 5]
        gu_own, gu_c = order(
            lambda w, p, b: spread_gate_up(w, p, blocks_c, 1, [b]), wg, place, gu_own
        )
        gu_c = [swap_seq(gu_c[k * 128 : (k + 1) * 128]) for k in range(2)]
        touch(order, gu_z[0])
    summed(keep, hold, seqs - 1)
    if two:
        touch(order, gu_x[1])
        gu_z += [swap_z(*now(gu_x[1]))]
        piece = fourth // 2
        down_send = order(
            lambda w: (
                lax.dynamic_slice_in_dim(w, pz * fourth, piece, 1),
                w[:, piece : 2 * piece],
                w[:, 3 * piece :],
            ),
            wd,
        )
    h2, n2, extra = [None] * seqs, [None] * seqs, [None] * seqs

    def second_norm(h, k, g, gain):
        x = h + k + g
        inv = lax.rsqrt(jnp.mean(x * x, axis=-1, keepdims=True) + NORM_EPS)
        return x, x * inv * gain, k + g

    for s in range(seqs):
        h2[s], mine, extra[s] = order(
            lambda h, k, g, gain, p, s=s: by_rows(
                second_norm, p, s, quarter, [h], [k, g], [gain], [F32, BF16, BF16]
            ),
            hidden, keep[s], hold[s], gains[1:], place,
        )
        n2[s] = share(mine)
        if two and s == 0:
            touch(order, gu_c[0])
            down_send = now(*down_send)
            down_x = swap_seq(down_send[0])
            down_c = [swap_seq(x) for x in down_send[1:]]
    if two:
        gu_parts = [Part(gu_own)]
        gu_parts += [Part(gu_x[k], k * 256, 0) for k in range(2)]
        gu_parts += [Part(gu_z[k], k * 256, 1) for k in range(2)]
        gu_parts += [Part(gu_c[k], half + k * fourth + 128) for k in range(2)]
        touch(order, down_x)
        down_z = swap_z(*now(down_x))
        down_parts = [Part(wd), Part(down_x, 0, 0), Part(down_z, 0, 1)]
        down_parts += [Part(down_c[k], half + k * fourth + piece) for k in range(2)]
    n2_all, act, gu = order(gate_up, [x for b in n2 for x in b], gu_parts, place)

    class Chunk:
        def __init__(self, finish):
            self.finish, self.stage = finish, 0

        def begin(self, make, *xs):
            self.make, self.xs = make, xs
            self.got = swap_seq(order(lambda *x: make(1, *x), *xs))

        def next(self):
            k = self.stage
            self.stage += 1
            assert k < 4
            if k == 0:
                self.sum = order(
                    lambda g, *x: (self.make(0, *x) + g.astype(F32)).astype(g.dtype),
                    self.got, *self.xs,
                )
            elif k < 3:
                self.sum = order(self.add, self.sum, self.got)
            else:
                self.finish(self.sum, self.got)
            if k < 3:
                self.got = (hop_in, hop_mid, hop_out)[k](self.sum)

        def add(self, a, b):
            return a + b if a.dtype == F32 else add_pair(a, b)

    chunks, results = {}, {}

    def begin(name, finish, make, *xs):
        if two:
            chunks[name] = Chunk(finish)
            chunks[name].begin(make, *xs)

    def go(*names):
        for name in names:
            if two:
                chunks[name].next()

    def into(name, writer):
        def finish(a, b):
            results[name] = [
                order(lambda a, b, m, r: writer(a, b, m, r), a, b, mid_flag, results.get(name, []))
            ]

        return finish

    def piece_of(x, k, at, size):
        return x[:, k * half + at : k * half + at + size]

    def tdot(a, b, k):
        x = dot(a, b, 0, 0)
        return x.astype(BF16) if k else x

    cuts = [0, 768, ff]
    gu_rows = [256, 256, 256, 128, 128]

    def begin_down(j):
        begin(
            f"d{j}",
            into("down", lambda a, b, m, r: place_rows(a, b, m, cuts[j], ff, r)),
            lambda k, a, d: tdot(a[:, cuts[j] : cuts[j + 1]], piece_of(d, k, 0, half), k),
            act, dhb,
        )

    def begin_gu(j):
        at = sum(gu_rows[:j])
        begin(
            f"g{j}",
            into("gu", lambda a, b, m, r: join_gate_up(a, b, m, at, half, r)),
            lambda k, n, d: tdot(piece_of(n, k, at, gu_rows[j]), d, k),
            n2_all, dgu,
        )

    begin_down(0)
    if two:

        def pair(a, c, first):
            return jnp.concatenate([a, jnp.where(first, c[0], c[1])])

        begin_down(1)
        pair_x = order(lambda a, c: pair(a, c, pz == 0), gu_x[0], gu_c)
        pair_z = order(lambda a, c: pair(a, c, pz == 1), gu_z[0], gu_c)
        gu_parts = [Part(gu_own), Part(pair_x, 0, 0), Part(gu_x[1], 256, 0)]
        gu_parts += [Part(pair_z, 0, 1), Part(gu_z[1], 256, 1)]
    dgu = order(gate_back, dhb, down_parts, gu, place)
    got = order(
        lambda a, w, p: split_matmul(a, w, True, False, p, seqs), dgu, gu_parts, place
    )
    keep, hold = list(got[1::2]), [swap_core(x) for x in got[::2]]
    go("d0")
    for s in range(seqs):
        summed(keep, hold, s)
    begin_gu(0)
    delta = order(
        lambda a, w, p, x: full_matmul(a, w, False, p, seqs, x), act, down_parts, place, extra
    )
    d2, gain2 = [None] * seqs, []

    def second_back(d, k, g, x, gain):
        mine = k + g
        inv = lax.rsqrt(jnp.mean(x * x, axis=-1, keepdims=True) + NORM_EPS)
        w = gain * mine
        back = inv * w - x * (inv * inv * inv) * jnp.mean(w * x, axis=-1, keepdims=True)
        return back + d, jnp.sum(mine * x * inv, axis=0, keepdims=True)

    for s in range(seqs):
        mine, g2 = order(
            lambda d, k, g, x, gain, p, s=s: by_rows(
                second_back, p, s, quarter, [d], [k, g, x], [gain], [BF16], 1
            ),
            d_hidden, keep[s], hold[s], h2[s], gains[1:], place,
        )
        gain2.append(g2)
        d2[s] = share(mine)
        if s == 0:
            go("d1")
    go("d0")
    dq, dkv, early = [None] * seqs, [None] * seqs, [None] * seqs
    dkv_got = []
    for s in range(seqs):
        d2[s] = order(stack, d2[s], place)
        dq[s], dkv[s], early[s] = order(
            lambda q, kv, st, b, a, w, *x, s=s: attend_back(s, q, kv, st, b, a, w, *x, scale),
            q_t, all_kv, starts3, bounds[s], att_t[s], out_parts, d2[s], lse[s], cos_t, sin_t,
        )
        if two:
            dkv_got.append(lax.ppermute(early[s], "seq", [(1, 0)]))
        if s == 0:
            go("g0")
    delta = lax.psum(lax.optimization_barrier((delta, d2[-1]))[0], "tp")
    begin(
        "out",
        into("out", lambda a, b, m, r: place_rows(a, b, m, 0, a.shape[0], r)),
        lambda k, a, d: sum(
            dot(x, piece_of(y, k, 0, half), 0, 0) for x, y in zip(a, d)
        ).astype(BF16 if k else F32),
        att, d2,
    )
    go("d0", "d1")
    if not two:
        dkv = [lax.psum_scatter(x, "seq", scatter_dimension=1, tiled=True) for x in dkv]
    d_qkv = order(
        lambda q, kv, g, c, s, p: pack_dqkv(q, kv, g, c, s, p, two),
        dq, dkv, dkv_got, cos_t, sin_t, place,
    )
    begin_gu(1)
    d_n1 = order(lambda a, w, p: full_matmul(a, w, True, p, seqs, []), d_qkv, qkv_parts, place)
    d_n1 = lax.psum(lax.optimization_barrier((d_n1, delta))[0], "tp")
    go("g0", "out")
    begin(
        "qkv",
        into("qkv", lambda a, b, m, r: place_rows(a, b, m, 0, half, r)),
        lambda k, n, d: tdot(piece_of(n, k, 0, half), d, k),
        normed1, d_qkv,
    )
    go("d1")
    gain2 = order(lambda g: sum(g), gain2)
    gain2 = order(lambda a, b: a + b, gain2, swap_core(gain2))
    gain2 = order(lambda a, b: a + b, gain2, swap_y(gain2))
    go("g1", "out", "g0")
    begin_gu(2)
    go("qkv", "g1", "d0")
    begin_gu(3)
    go("out", "g2", "qkv", "g0", "d1")
    begin_gu(4)
    go("g1", "g3", "g2", "qkv")
    hidden_out = order(lambda h, d, p: add_columns(h, d, p, quarter), hidden, delta, place)
    go("g4", "g3", "g2", "out")
    go("g4", "g3", "g1")
    grad_in, gain1 = order(
        lambda h, u, d, g, p: first_norm_back(h, u, d, g, p, quarter),
        hidden, d_n1, d2, gains[:1], place,
    )
    gain_sum = order(lambda a, b: jnp.concatenate([a, b]), gain1, gain2)

    def gain_finish(a, b):
        results["gain"] = [order(lambda a, b: jnp.where(middle, a, b), a, b)]

    begin("gain", gain_finish, lambda k, g: piece_of(g, k, 0, half), gain_sum)
    go("g4", "gain", "qkv", "gain", "g2", "gain", "g3", "g4", "gain")
    if two:
        g_qkv, g_out, g_down = results["qkv"][0], results["out"][0], results["down"][0]
        g_gu, gain_own = results["gu"][0], results["gain"][0]
    else:

        def reduce_rep(x):
            if n_rep != 4:
                return lax.psum(x.astype(F32), "rep").astype(BF16)
            x = x.astype(BF16)
            x = (x.astype(F32) + hop_in(x).astype(F32)).astype(BF16)
            x = (x.astype(F32) + hop_mid(x).astype(F32)).astype(BF16)
            return jnp.where(middle, x, hop_out(x))

        def reduce(x, axis):
            return reduce_rep(lax.psum_scatter(x, "seq", scatter_dimension=axis, tiled=True))

        g_down = reduce(dot(act, dhb, 0, 0), 1).astype(F32)
        g_out = reduce(sum(dot(x, y, 0, 0) for x, y in zip(att, d2)), 1).astype(F32)
        g_qkv = reduce(dot(normed1, d_qkv, 0, 0), 0).astype(F32)
        g_gu = reduce(dot(n2_all, dgu, 0, 0), 0)
        g_gu = join_gate_up(g_gu, g_gu, mid_flag, 0, g_gu.shape[0], [])
        gain_own = lax.psum_scatter(gain_sum, "seq", scatter_dimension=1, tiled=True)
        gain_own = lax.psum(gain_own, "rep")
    return (
        hidden_out.reshape(seqs, length, width),
        grad_in.reshape(seqs, length, width),
        g_qkv[None, :, None, :],
        g_out[None],
        g_gu,
        g_down[None],
        gain_own[None],
    )


def solution(mesh):
    in_specs = (
        P("rep", "seq", None),
        P("rep", "seq", None),
        P(None, "seq", "tp", None),
        P(None, "tp", "seq"),
        P(None, "seq", None, "tp"),
        P(None, "tp", "seq"),
        P(None, None, "seq"),
        P("rep", None),
    )
    out_specs = (
        P("rep", "seq", None),
        P("rep", "seq", None),
        P(None, "seq", "tp", None),
        P(None, "tp", "seq"),
        P(None, "seq", None, "tp"),
        P(None, "tp", "seq"),
        P(None, None, "seq"),
    )
    sizes = (mesh.shape["seq"], mesh.shape["tp"], mesh.shape["rep"])
    return jax.shard_map(
        functools.partial(per_device, sizes),
        mesh=mesh,
        in_specs=in_specs,
        out_specs=out_specs,
        check_vma=False,
    )
```

```python
import dataclasses
import functools
from typing import Any

import jax
import jax.numpy as jnp
from jax import lax
from jax.experimental import pallas as pl
from jax.experimental.pallas import tpu as pltpu
from jax.sharding import PartitionSpec as P

HEAD_DIM = 64
NORM_EPS = 1e-05
ROPE_THETA = 10000.0
LOG2E = 1.4426950408889634
MASKED = -1e30
F32 = jnp.float32
BF16 = jnp.bfloat16
MIB = 1024 * 1024


def touch(order, *xs):
    order.last = (*order.last, *xs)


def dot(a, b, ca=1, cb=0):
    return lax.dot_general(a, b, (((ca,), (cb,)), ((), ())), preferred_element_type=F32)


def call(body, grid, ins, outs, shapes, scratch=(), scalars=0, alias=None, vmem=16):
    return pl.pallas_call(
        body,
        out_shape=shapes,
        grid_spec=pltpu.PrefetchScalarGridSpec(
            num_scalar_prefetch=scalars,
            grid=grid,
            in_specs=ins,
            out_specs=outs,
            scratch_shapes=list(scratch),
        ),
        input_output_aliases=alias or {},
        compiler_params=pltpu.CompilerParams(vmem_limit_bytes=vmem * MIB),
        cost_estimate=pl.CostEstimate(flops=3000000000, bytes_accessed=8000000, transcendentals=0),
    )


@functools.partial(
    jax.tree_util.register_dataclass, data_fields=["array"], meta_fields=["base", "late"]
)
@dataclasses.dataclass(frozen=True)
class Part:
    array: Any
    base: int = 0
    late: Any = None

    def start(self, width, p):
        if self.late is None:
            return self.base
        return width // 2 + (p ^ self.late) * (width // 4) + self.base


class Order:
    def __init__(self):
        self.last = ()

    def __call__(self, step, *xs):
        flat, tree = jax.tree.flatten(xs)
        if self.last:
            flat = lax.optimization_barrier((tuple(flat), self.last))[0]
        out = step(*jax.tree.unflatten(tree, flat))
        self.last = tuple(jax.tree.leaves(out))
        return out


def first_norm(hidden, gain, place, block):
    rows, width = hidden.shape
    half = width // 2

    def body(p, a_ref, b_ref, g_ref, n_ref):
        a, b = a_ref[...], b_ref[...]
        total = jnp.sum(a * a, -1, keepdims=True) + jnp.sum(b * b, -1, keepdims=True)
        inv = lax.rsqrt(total * (1.0 / width) + NORM_EPS)
        n_ref[:, :half] = (a * inv * g_ref[:, :half]).astype(BF16)
        n_ref[:, half:] = (b * inv * g_ref[:, half:]).astype(BF16)

    return call(
        body,
        (rows // block,),
        [
            pl.BlockSpec((block, half), lambda i, p: (i, p[1])),
            pl.BlockSpec((block, half), lambda i, p: (i, 1 - p[1])),
            pl.BlockSpec((1, width), lambda i, p: (0, 0)),
        ],
        pl.BlockSpec((block, width), lambda i, p: (i, 0)),
        jax.ShapeDtypeStruct((rows, width), BF16),
        scalars=1,
    )(place, hidden, hidden, gain)


def local_cast(x, place, block):
    rows, width = x.shape
    half = width // 2

    def body(p, a_ref, b_ref, o_ref):
        o_ref[:, :half] = a_ref[...].astype(BF16)
        o_ref[:, half:] = b_ref[...].astype(BF16)

    def row(i, p):
        return (i // 4) * 4 + ((i % 4) ^ p[0])

    return call(
        body,
        (rows // block,),
        [
            pl.BlockSpec((block, half), lambda i, p: (row(i, p), p[1])),
            pl.BlockSpec((block, half), lambda i, p: (row(i, p), 1 - p[1])),
        ],
        pl.BlockSpec((block, width), lambda i, p: (i, 0)),
        jax.ShapeDtypeStruct((rows, width), BF16),
        scalars=1,
    )(place, x, x)


def join_gate_up(a, b, middle, at, rows, before):
    count, cols = a.shape
    ff = cols // 2
    block = min(128, count)

    def body(p, a_ref, b_ref, *refs):
        o_ref = refs[-1]

        def put(src):
            for j in range(ff // 128):
                for g in range(2):
                    o_ref[0, :, g, 128 * j : 128 * (j + 1)] = src[
                        :, 256 * j + 128 * g : 256 * j + 128 * (g + 1)
                    ].astype(F32)

        @pl.when(p[0] == 1)
        def _():
            put(a_ref)

        @pl.when(p[0] == 0)
        def _():
            put(b_ref)

    return call(
        body,
        (count // block,),
        [pl.BlockSpec((block, cols), lambda i, p: (i, 0))] * 2
        + [pl.BlockSpec(memory_space=pl.ANY)] * len(before),
        pl.BlockSpec((1, block, 2, ff), lambda i, p: (0, at // block + i, 0, 0)),
        jax.ShapeDtypeStruct((1, rows, 2, ff), F32),
        scalars=1,
        alias={3 + k: k for k in range(len(before))},
    )(middle, a, b, *before)


def project_qkv(normed, weights, cos_t, sin_t, group):
    rows, width = normed.shape
    seqs, half, length = cos_t.shape
    cols = weights[0].shape[1]
    tile = min(256, length)
    per = length // tile
    depth = width // len(weights)
    parts = len(weights)

    def body(n_ref, cos_ref, sin_ref, *refs):
        q_ref, kv_ref = refs[parts:]
        acc = dot(n_ref[:, :depth], refs[0][...])
        for k in range(1, parts):
            acc = acc + dot(n_ref[:, k * depth : (k + 1) * depth], refs[k][...])
        t = acc.T
        cos, sin = cos_ref[0], sin_ref[0]
        for h in range(group + 1):
            a, b = t[2 * half * h : 2 * half * h + half], t[2 * half * h + half : 2 * half * (h + 1)]
            r = jnp.concatenate([a * cos - b * sin, b * cos + a * sin], 0).astype(BF16)
            if h < group:
                q_ref[0, 2 * half * h : 2 * half * (h + 1)] = r
            else:
                kv_ref[0, : 2 * half] = r
        kv_ref[0, 2 * half :] = t[2 * half * (group + 1) :].astype(BF16)

    return call(
        body,
        (seqs, per),
        [
            pl.BlockSpec((tile, width), lambda s, i: (s * per + i, 0)),
            pl.BlockSpec((1, half, tile), lambda s, i: (s, 0, i)),
            pl.BlockSpec((1, half, tile), lambda s, i: (s, 0, i)),
        ]
        + [pl.BlockSpec((depth, cols), lambda s, i: (0, 0))] * parts,
        [
            pl.BlockSpec((1, group * HEAD_DIM, tile), lambda s, i: (s, 0, i)),
            pl.BlockSpec((1, 2 * HEAD_DIM, tile), lambda s, i: (s, 0, i)),
        ],
        [
            jax.ShapeDtypeStruct((seqs, group * HEAD_DIM, length), BF16),
            jax.ShapeDtypeStruct((seqs, 2 * HEAD_DIM, length), BF16),
        ],
    )(normed, cos_t, sin_t, *weights)


def attend(s, q_t, kv_t, starts, bounds, scale):
    seqs, cols, length = q_t.shape
    total = kv_t.shape[2]
    heads = cols // HEAD_DIM
    tq, tk = min(256, length), min(256, total)

    def body(b_ref, q_ref, kv_ref, st_ref, att_ref, att_t_ref, lse_ref, kn, m, l, acc):
        i = pl.program_id(0)

        @pl.when(i == 0)
        def _():
            kn[...] = kv_ref[0, :HEAD_DIM].astype(F32).T.astype(BF16)

        qid = b_ref[0] + i * tq + lax.broadcasted_iota(jnp.int32, (1, tq), 1)
        start = st_ref[0]
        m[...] = jnp.full_like(m, MASKED)
        l[...] = jnp.zeros_like(l)
        acc[...] = jnp.zeros_like(acc)

        def step(t, _):
            k0 = pl.multiple_of(t * tk, tk)
            kid = k0 + lax.broadcasted_iota(jnp.int32, (tk, 1), 0)
            ok = (kid <= qid) & (kid >= start)
            keys = kn[pl.ds(k0, tk), :]
            vals = kv_ref[0, HEAD_DIM:, pl.ds(k0, tk)]
            for h in range(heads):
                lo = h * HEAD_DIM
                sc = dot(keys, q_ref[0, lo : lo + HEAD_DIM]) * (scale * LOG2E)
                sc = jnp.where(ok, sc, MASKED)
                old = m[h : h + 1]
                new = jnp.maximum(old, jnp.max(sc, 0, keepdims=True))
                e = jnp.exp2(sc - new)
                fade = jnp.exp2(old - new)
                m[h : h + 1] = new
                l[h : h + 1] = l[h : h + 1] * fade + jnp.sum(e, 0, keepdims=True)
                acc[lo : lo + HEAD_DIM] = acc[lo : lo + HEAD_DIM] * fade + dot(vals, e.astype(BF16))
            return 0

        lax.fori_loop(b_ref[2 + 2 * i], b_ref[3 + 2 * i], step, 0)
        for h in range(heads):
            lo = h * HEAD_DIM
            acc[lo : lo + HEAD_DIM] = acc[lo : lo + HEAD_DIM] / l[h : h + 1]
        att_t_ref[...] = acc[...].astype(BF16)
        att_ref[...] = acc[...].T.astype(BF16)
        lse_ref[...] = m[...] + jnp.log2(l[...])

    return call(
        body,
        (length // tq,),
        [
            pl.BlockSpec((1, cols, tq), lambda i, b: (s, 0, i)),
            pl.BlockSpec((1, 2 * HEAD_DIM, total), lambda i, b: (s, 0, 0)),
            pl.BlockSpec((1, 1, tq), lambda i, b: (s, 0, i)),
        ],
        [
            pl.BlockSpec((tq, cols), lambda i, b: (i, 0)),
            pl.BlockSpec((cols, tq), lambda i, b: (0, i)),
            pl.BlockSpec((heads, tq), lambda i, b: (0, i)),
        ],
        [
            jax.ShapeDtypeStruct((length, cols), BF16),
            jax.ShapeDtypeStruct((cols, length), BF16),
            jax.ShapeDtypeStruct((heads, length), F32),
        ],
        scratch=[
            pltpu.VMEM((total, HEAD_DIM), BF16),
            pltpu.VMEM((heads, tq), F32),
            pltpu.VMEM((heads, tq), F32),
            pltpu.VMEM((cols, tq), F32),
        ],
        scalars=1,
    )(bounds, q_t, kv_t, starts)


def attend_back(s, q_t, kv_t, starts, bounds, att_t, out_parts, d2, lse, cos_t, sin_t, scale):
    seqs, cols, length = q_t.shape
    width = d2.shape[1]
    parts = len(out_parts)
    total = kv_t.shape[2]
    heads = cols // HEAD_DIM
    half = HEAD_DIM // 2
    tq, tk = min(256, length), min(256, total)

    def body(
        b_ref, q_ref, kv_ref, st_ref, a_ref, d2_ref, lse_ref, cos_ref, sin_ref, *refs
    ):
        w_refs = refs[:parts]
        dq_ref, dkv_ref, early_ref, kn, vn, delta, acc, d_ref = refs[parts:]
        i = pl.program_id(0)

        @pl.when(i == 0)
        def _():
            kn[...] = kv_ref[0, :HEAD_DIM].astype(F32).T.astype(BF16)
            vn[...] = kv_ref[0, HEAD_DIM:].astype(F32).T.astype(BF16)
            dkv_ref[...] = jnp.zeros_like(dkv_ref)

        d_att = 0.0
        for part, w_ref in zip(out_parts, w_refs):
            size = part.array.shape[1]
            at = part.start(width, b_ref[1])
            if part.late is not None:
                at = pl.multiple_of(at, 128)
            d_att = d_att + dot(w_ref[...], d2_ref[:, pl.ds(at, size)], 1, 1)
        d_ref[...] = d_att.astype(BF16)
        qid = b_ref[0] + i * tq + lax.broadcasted_iota(jnp.int32, (1, tq), 1)
        start = st_ref[0]
        for h in range(heads):
            lo = h * HEAD_DIM
            prod = d_ref[lo : lo + HEAD_DIM].astype(F32) * a_ref[lo : lo + HEAD_DIM].astype(F32)
            delta[h : h + 1] = jnp.sum(prod, 0, keepdims=True)
        acc[...] = jnp.zeros_like(acc)

        def step(t, _):
            k0 = pl.multiple_of(t * tk, tk)
            kid = k0 + lax.broadcasted_iota(jnp.int32, (tk, 1), 0)
            ok = (kid <= qid) & (kid >= start)
            keys, vals = kn[pl.ds(k0, tk), :], vn[pl.ds(k0, tk), :]
            keys_t = kv_ref[0, :HEAD_DIM, pl.ds(k0, tk)]
            dk = jnp.zeros((HEAD_DIM, tk), F32)
            dv = jnp.zeros((HEAD_DIM, tk), F32)
            for h in range(heads):
                lo = h * HEAD_DIM
                q, d = q_ref[0, lo : lo + HEAD_DIM], d_ref[lo : lo + HEAD_DIM]
                sc = dot(keys, q) * (scale * LOG2E) - lse_ref[h : h + 1]
                p = jnp.exp2(jnp.where(ok, sc, MASKED))
                dp = dot(vals, d)
                ds = (p * (dp - delta[h : h + 1]) * scale).astype(BF16)
                dv = dv + dot(d, p.astype(BF16), 1, 1)
                dk = dk + dot(q, ds, 1, 1)
                acc[lo : lo + HEAD_DIM] += dot(keys_t, ds)
            dkv_ref[:HEAD_DIM, pl.ds(k0, tk)] += dk
            dkv_ref[HEAD_DIM:, pl.ds(k0, tk)] += dv
            return 0

        lax.fori_loop(b_ref[2 + 2 * i], b_ref[3 + 2 * i], step, 0)
        cos, sin = cos_ref[0], sin_ref[0]
        for h in range(heads):
            lo = h * HEAD_DIM
            c, e = acc[lo : lo + half], acc[lo + half : lo + HEAD_DIM]
            acc[lo : lo + HEAD_DIM] = jnp.concatenate([c * cos + e * sin, e * cos - c * sin], 0)
        dq_ref[...] = acc[...].T.astype(BF16)
        early_ref[...] = dkv_ref[:, :length].astype(BF16)

    return call(
        body,
        (length // tq,),
        [
            pl.BlockSpec((1, cols, tq), lambda i, b: (s, 0, i)),
            pl.BlockSpec((1, 2 * HEAD_DIM, total), lambda i, b: (s, 0, 0)),
            pl.BlockSpec((1, 1, tq), lambda i, b: (s, 0, i)),
            pl.BlockSpec((cols, tq), lambda i, b: (0, i)),
            pl.BlockSpec((tq, d2.shape[1]), lambda i, b: (i, 0)),
            pl.BlockSpec((heads, tq), lambda i, b: (0, i)),
            pl.BlockSpec((1, half, tq), lambda i, b: (s, 0, i)),
            pl.BlockSpec((1, half, tq), lambda i, b: (s, 0, i)),
        ]
        + [pl.BlockSpec(p.array.shape, lambda i, b: (0, 0)) for p in out_parts],
        [
            pl.BlockSpec((tq, cols), lambda i, b: (i, 0)),
            pl.BlockSpec((2 * HEAD_DIM, total), lambda i, b: (0, 0)),
            pl.BlockSpec((2 * HEAD_DIM, length), lambda i, b: (0, 0)),
        ],
        [
            jax.ShapeDtypeStruct((length, cols), BF16),
            jax.ShapeDtypeStruct((2 * HEAD_DIM, total), F32),
            jax.ShapeDtypeStruct((2 * HEAD_DIM, length), BF16),
        ],
        scratch=[
            pltpu.VMEM((total, HEAD_DIM), BF16),
            pltpu.VMEM((total, HEAD_DIM), BF16),
            pltpu.VMEM((heads, tq), F32),
            pltpu.VMEM((cols, tq), F32),
            pltpu.VMEM((cols, tq), BF16),
        ],
        scalars=1,
    )(
        bounds, q_t, kv_t, starts, att_t, d2, lse, cos_t, sin_t, *[p.array for p in out_parts]
    )


def join_kv(mine, other, place):
    seqs, cols, length = mine.shape

    def body(p, m_ref, o_ref, out_ref):
        @pl.when(pl.program_id(0) == 0)
        def _():
            out_ref[...] = m_ref[...]

        @pl.when(pl.program_id(0) == 1)
        def _():
            out_ref[...] = o_ref[...]

    spec = pl.BlockSpec(mine.shape, lambda i, p: (0, 0, 0))
    return call(
        body,
        (2,),
        [spec, spec],
        pl.BlockSpec(mine.shape, lambda i, p: (0, 0, i ^ p[1])),
        jax.ShapeDtypeStruct((seqs, cols, 2 * length), mine.dtype),
        scalars=1,
    )(place, mine, other)


def stack(pieces, place):
    quarter, width = pieces[0].shape
    count = len(pieces)

    def body(p, *refs):
        for k in range(count):

            @pl.when(pl.program_id(0) == k)
            def _():
                refs[-1][...] = refs[k][...]

    return call(
        body,
        (count,),
        [pl.BlockSpec((quarter, width), lambda i, p: (0, 0))] * count,
        pl.BlockSpec((quarter, width), lambda i, p: ((i // 4) * 4 + ((i % 4) ^ p[0]), 0)),
        jax.ShapeDtypeStruct((count * quarter, width), BF16),
        scalars=1,
    )(place, *pieces)


def first_sum(keep, got):
    rows, width = keep.shape
    half = rows // 2
    tile = width // 4

    def body(k_ref, g_ref, send_ref, keep_ref):
        send_ref[...] = (k_ref[half:] + g_ref[half:].astype(F32)).astype(BF16)
        keep_ref[...] = k_ref[:half] + g_ref[:half].astype(F32)

    return call(
        body,
        (4,),
        [pl.BlockSpec((rows, tile), lambda j: (0, j))] * 2,
        [pl.BlockSpec((half, tile), lambda j: (0, j))] * 2,
        [jax.ShapeDtypeStruct((half, width), BF16), jax.ShapeDtypeStruct((half, width), F32)],
    )(keep, got)


def by_rows(step, place, s, quarter, owned, blocks, vectors, outs, sums=0):
    width = (owned or blocks)[0].shape[1]
    half = width // 2
    tile = min(32, quarter)
    per = quarter // tile
    seqs = owned[0].shape[0] // (4 * quarter) if s is None else 1
    n_in = 2 * len(owned) + len(blocks) + len(vectors)

    def body(p, *refs):
        vals = [
            jnp.concatenate([refs[2 * k][...], refs[2 * k + 1][...]], 1) for k in range(len(owned))
        ]
        vals += [r[...].astype(F32) for r in refs[2 * len(owned) : n_in]]
        got = step(*vals)
        for k in range(len(outs)):
            refs[n_in + k][...] = got[k].astype(outs[k])
        for k in range(sums):
            o_ref, x = refs[n_in + len(outs) + k], got[len(outs) + k]

            @pl.when(pl.program_id(0) == 0)
            def _():
                o_ref[...] = x

            @pl.when(pl.program_id(0) > 0)
            def _():
                o_ref[...] += x

    def at(i, p):
        if s is None:
            return ((i // per) * 4 + p[0]) * per + i % per
        return (s * 4 + p[0]) * per + i

    own_specs = [
        pl.BlockSpec((tile, half), lambda i, p: (at(i, p), p[1])),
        pl.BlockSpec((tile, half), lambda i, p: (at(i, p), 1 - p[1])),
    ]
    return call(
        body,
        (seqs * per,),
        own_specs * len(owned)
        + [pl.BlockSpec((tile, width), lambda i, p: (i, 0))] * len(blocks)
        + [pl.BlockSpec((1, width), lambda i, p: (0, 0))] * len(vectors),
        [pl.BlockSpec((tile, width), lambda i, p: (i, 0))] * len(outs)
        + [pl.BlockSpec((1, width), lambda i, p: (0, 0))] * sums,
        [jax.ShapeDtypeStruct((seqs * quarter, width), d) for d in outs]
        + [jax.ShapeDtypeStruct((1, width), F32)] * sums,
        scalars=1,
    )(place, *[x for a in owned for x in (a, a)], *blocks, *vectors)


def pack_dqkv(dqs, dkvs, others, cos_t, sin_t, place, seq_block):
    seqs = len(dqs)
    length, cols = dqs[0].shape
    half = HEAD_DIM // 2
    wide = cols + 2 * HEAD_DIM

    def body(p, cos_ref, sin_ref, *refs):
        o_ref = refs[-1]
        for s in range(seqs):

            @pl.when(pl.program_id(0) == s)
            def _():
                kv = refs[seqs + s][...]
                if others:
                    kv = kv + refs[2 * seqs + s][...].astype(F32)
                c, e = kv[:half], kv[half:HEAD_DIM]
                cos, sin = cos_ref[0], sin_ref[0]
                kv = jnp.concatenate([c * cos + e * sin, e * cos - c * sin, kv[HEAD_DIM:]], 0)
                o_ref[:, :cols] = refs[s][...]
                o_ref[:, cols:] = kv.T.astype(BF16)

    const = lambda i, p: (0, 0)
    return call(
        body,
        (seqs,),
        [pl.BlockSpec((1, half, length), lambda i, p: (i, 0, 0))] * 2
        + [pl.BlockSpec((length, cols), const)] * seqs
        + [
            pl.BlockSpec((2 * HEAD_DIM, length), lambda i, p: (0, p[1] if seq_block else 0))
        ]
        * seqs
        + [pl.BlockSpec((2 * HEAD_DIM, length), const)] * len(others),
        pl.BlockSpec((length, wide), lambda i, p: (i, 0)),
        jax.ShapeDtypeStruct((seqs * length, wide), BF16),
        scalars=1,
    )(place, cos_t, sin_t, *dqs, *dkvs, *others)


def add_pair(a, b):
    rows, cols = a.shape
    block = rows // 4

    def body(a_ref, b_ref, o_ref):
        o_ref[...] = (a_ref[...].astype(F32) + b_ref[...].astype(F32)).astype(BF16)

    spec = pl.BlockSpec((block, cols), lambda i: (i, 0))
    return call(body, (4,), [spec, spec], spec, jax.ShapeDtypeStruct((rows, cols), BF16))(a, b)


def place_rows(a, b, middle, at, rows, before):
    count, cols = a.shape
    block = 128

    def body(p, a_ref, b_ref, *refs):
        o_ref = refs[-1]

        @pl.when(p[0] == 1)
        def _():
            o_ref[...] = a_ref[...].astype(F32)

        @pl.when(p[0] == 0)
        def _():
            o_ref[...] = b_ref[...].astype(F32)

    return call(
        body,
        (count // block,),
        [pl.BlockSpec((block, cols), lambda i, p: (i, 0))] * 2
        + [pl.BlockSpec(memory_space=pl.ANY)] * len(before),
        pl.BlockSpec((block, cols), lambda i, p: (at // block + i, 0)),
        jax.ShapeDtypeStruct((rows, cols), F32),
        scalars=1,
        alias={3 + k: k for k in range(len(before))},
    )(middle, a, b, *before)


def spread_gate_up(w, place, blocks):
    rows, _, ff = w.shape
    block = min(128, rows)
    steps = rows // block if blocks is None else len(blocks)

    def body(p, w_ref, o_ref):
        for j in range(ff // 128):
            for g in range(2):
                o_ref[:, 256 * j + 128 * g : 256 * j + 128 * (g + 1)] = w_ref[
                    :, g, 128 * j : 128 * (j + 1)
                ]

    def row(i, p):
        if blocks is None:
            return i
        r = blocks[0](p)
        for k in range(1, steps):
            r = jnp.where(i == k, blocks[k](p), r)
        return r

    return call(
        body,
        (steps,),
        [pl.BlockSpec((block, 2, ff), lambda i, p: (row(i, p), 0, 0))],
        pl.BlockSpec((block, 2 * ff), lambda i, p: (i, 0)),
        jax.ShapeDtypeStruct((steps * block, 2 * ff), BF16),
        scalars=1,
    )(place, w)


def gate_up(pieces, parts, place):
    quarter, width = pieces[0].shape
    count = len(pieces)
    rows = count * quarter
    ff = parts[0].array.shape[1] // 2
    tile = 128

    def body(p, *refs):
        w_refs = refs[count : count + len(parts)]
        n_ref, act_ref, gu_ref, w_ref = refs[count + len(parts) :]

        @pl.when(pl.program_id(0) == 0)
        def _():
            for k in range(count):
                n_ref[k * quarter : (k + 1) * quarter] = refs[k][...]

        for part, ref in zip(parts, w_refs):
            size = part.array.shape[0]
            at = part.start(width, p[2])
            at = at if part.late is None else pl.multiple_of(at, 128)
            w_ref[pl.ds(at, size), :] = ref[...]
        gu = dot(n_ref[...], w_ref[...])
        gate, up = gu[:, :tile], gu[:, tile:]
        sig = 1.0 / (1.0 + jnp.exp2(gate * (-LOG2E)))
        act_ref[...] = (gate * sig * up).astype(BF16)
        gu_ref[...] = gu.astype(BF16)

    return call(
        body,
        (ff // tile,),
        [pl.BlockSpec((quarter, width), lambda j, p: (0, 0), pipeline_mode=pl.Buffered(1))] * count
        + [pl.BlockSpec((x.array.shape[0], 2 * tile), lambda j, p: (0, j)) for x in parts],
        [
            pl.BlockSpec((rows, width), lambda j, p: (0, 0)),
            pl.BlockSpec((rows, tile), lambda j, p: (0, j)),
            pl.BlockSpec((rows, 2 * tile), lambda j, p: (0, j)),
        ],
        [
            jax.ShapeDtypeStruct((rows, width), BF16),
            jax.ShapeDtypeStruct((rows, ff), BF16),
            jax.ShapeDtypeStruct((rows, 2 * ff), BF16),
        ],
        scratch=[pltpu.VMEM((width, 2 * tile), BF16)],
        scalars=1,
        vmem=30,
    )(place, *pieces, *[x.array for x in parts])


def gate_back(dhb, parts, gu, place):
    rows, width = dhb.shape
    ff = parts[0].array.shape[0]
    tile = 256

    def body(p, d_ref, gu_ref, *refs):
        o_ref = refs[-1]
        d_act = 0.0
        for part, ref in zip(parts, refs):
            at = part.start(width, p[2])
            if part.late is not None:
                at = pl.multiple_of(at, 128)
            d_act = d_act + dot(d_ref[:, pl.ds(at, part.array.shape[1])], ref[...], 1, 1)
        for k in range(tile // 128):
            d = d_act[:, 128 * k : 128 * (k + 1)]
            gate = gu_ref[:, 256 * k : 256 * k + 128].astype(F32)
            up = gu_ref[:, 256 * k + 128 : 256 * (k + 1)].astype(F32)
            sig = 1.0 / (1.0 + jnp.exp2(gate * (-LOG2E)))
            o_ref[:, 256 * k : 256 * k + 128] = (
                d * up * sig * (1.0 + gate * (1.0 - sig))
            ).astype(BF16)
            o_ref[:, 256 * k + 128 : 256 * (k + 1)] = (d * gate * sig).astype(BF16)

    return call(
        body,
        (pl.cdiv(ff, tile),),
        [
            pl.BlockSpec((rows, width), lambda j, p: (0, 0)),
            pl.BlockSpec((rows, 2 * tile), lambda j, p: (0, j)),
        ]
        + [pl.BlockSpec((tile, x.array.shape[1]), lambda j, p: (j, 0)) for x in parts],
        pl.BlockSpec((rows, 2 * tile), lambda j, p: (0, j)),
        jax.ShapeDtypeStruct((rows, 2 * ff), BF16),
        scalars=1,
    )(place, dhb, gu, *[x.array for x in parts])


def split_matmul(a, parts, transposed, natural, place, seqs):
    rows, depth = a.shape
    axis = 0 if transposed else 1
    tile = 256
    counts = [x.array.shape[axis] // tile for x in parts]
    bases = [sum(counts[:k]) for k in range(len(parts))]
    cols = tile * sum(counts)
    length = rows // seqs
    quarter = length // 4

    def body(p, a_ref, *refs):
        w_refs, outs, acc = refs[: len(parts)], refs[len(parts) : -1], refs[-1]
        j = pl.program_id(0)
        for k, w_ref in enumerate(w_refs):

            @pl.when((j >= bases[k]) & (j < bases[k] + counts[k]))
            def _():
                acc[...] = dot(a_ref[...], w_ref[...], 1, 1 - axis)

        for s in range(seqs):
            send, keep = outs[2 * s], outs[2 * s + 1]
            for b in range(4):
                at = s * length + (b ^ p[0] if natural else b) * quarter
                part = acc[pl.ds(at, quarter), :]
                to = (b % 2) * quarter
                if b < 2:
                    keep[to : to + quarter] = part
                else:
                    send[to : to + quarter] = part.astype(BF16)

    def w_spec(k):
        def index(j, p):
            t = jnp.clip(j - bases[k], 0, counts[k] - 1)
            return (t, 0) if transposed else (0, t)

        shape = (tile, depth) if transposed else (depth, tile)
        once = {"pipeline_mode": pl.Buffered(1)} if counts[k] == 1 else {}
        return pl.BlockSpec(shape, index, **once)

    def column(j, p):
        c = parts[0].start(cols, p[2]) // tile + j
        for k in range(1, len(parts)):
            at = parts[k].start(cols, p[2]) // tile + j - bases[k]
            c = jnp.where(j >= bases[k], at, c)
        return (0, c)

    return call(
        body,
        (sum(counts),),
        [pl.BlockSpec((rows, depth), lambda j, p: (0, 0), pipeline_mode=pl.Buffered(1))]
        + [w_spec(k) for k in range(len(parts))],
        [pl.BlockSpec((length // 2, tile), column)] * (2 * seqs),
        [
            jax.ShapeDtypeStruct((length // 2, cols), BF16),
            jax.ShapeDtypeStruct((length // 2, cols), F32),
        ]
        * seqs,
        scratch=[pltpu.VMEM((rows, tile), F32)],
        scalars=1,
    )(place, a, *[x.array for x in parts])


def full_matmul(a, parts, transposed, place, seqs, extras):
    rows, depth = a.shape
    axis = 0 if transposed else 1
    tile = 256
    counts = [x.array.shape[axis] // tile for x in parts]
    bases = [sum(counts[:k]) for k in range(len(parts))]
    cols = tile * sum(counts)
    length = rows // seqs
    quarter = length // 4

    def body(p, a_ref, *refs):
        w_refs, o_ref, acc = refs[: len(parts)], refs[-2], refs[-1]
        j = pl.program_id(0)
        for k, w_ref in enumerate(w_refs):

            @pl.when((j >= bases[k]) & (j < bases[k] + counts[k]))
            def _():
                acc[...] = dot(a_ref[...], w_ref[...], 1, 1 - axis)

        if not extras:
            o_ref[...] = acc[...].astype(BF16)
        for s in range(len(extras)):
            for b in range(4):
                part = acc[s * length + b * quarter : s * length + (b + 1) * quarter]
                if b == 0:
                    part = part + refs[len(parts) + s][...].astype(F32)
                at = pl.multiple_of(s * length + (b ^ p[0]) * quarter, quarter)
                o_ref[pl.ds(at, quarter), :] = part.astype(BF16)

    def w_spec(k):
        def index(j, p):
            t = jnp.clip(j - bases[k], 0, counts[k] - 1)
            return (t, 0) if transposed else (0, t)

        return pl.BlockSpec((tile, depth) if transposed else (depth, tile), index)

    def column(j, p):
        c = parts[0].start(cols, p[2]) // tile + j
        for k in range(1, len(parts)):
            c = jnp.where(j >= bases[k], parts[k].start(cols, p[2]) // tile + j - bases[k], c)
        return (0, c)

    return call(
        body,
        (sum(counts),),
        [pl.BlockSpec((rows, depth), lambda j, p: (0, 0), pipeline_mode=pl.Buffered(1))]
        + [w_spec(k) for k in range(len(parts))]
        + [pl.BlockSpec((quarter, tile), column)] * len(extras),
        pl.BlockSpec((rows, tile), column),
        jax.ShapeDtypeStruct((rows, cols), BF16),
        scratch=[pltpu.VMEM((rows, tile), F32)],
        scalars=1,
    )(place, a, *[x.array for x in parts], *extras)


def put_columns(o_ref, x, swapped, half):
    @pl.when(swapped == 0)
    def _():
        o_ref[...] = x

    @pl.when(swapped == 1)
    def _():
        o_ref[:, :half] = x[:, half:]
        o_ref[:, half:] = x[:, :half]


def add_columns(x, delta, place, block):
    rows, width = x.shape
    half = width // 2

    def body(p, a_ref, b_ref, d_ref, o_ref):
        mine = jnp.concatenate([a_ref[...], b_ref[...]], 1) + d_ref[...].astype(F32)
        put_columns(o_ref, mine, p[1], half)

    return call(
        body,
        (rows // block,),
        [
            pl.BlockSpec((block, half), lambda i, p: (i, p[1])),
            pl.BlockSpec((block, half), lambda i, p: (i, 1 - p[1])),
            pl.BlockSpec((block, width), lambda i, p: (i, 0)),
        ],
        pl.BlockSpec((block, width), lambda i, p: (i, 0)),
        jax.ShapeDtypeStruct((rows, width), F32),
        scalars=1,
    )(place, x, x, delta)


def first_norm_back(x, upstream, d2, gain, place, block):
    rows, width = x.shape
    half = width // 2
    per = d2[0].shape[0] // block
    count = len(d2)

    def body(p, a_ref, b_ref, u_ref, g_ref, *refs):
        o_ref = refs[count]
        i = pl.program_id(0)
        h = jnp.concatenate([a_ref[...], b_ref[...]], 1)
        inv = lax.rsqrt(jnp.mean(h * h, axis=-1, keepdims=True) + NORM_EPS)
        mine = u_ref[...].astype(F32)
        w = g_ref[...] * mine
        back = inv * w - h * (inv * inv * inv) * jnp.mean(w * h, axis=-1, keepdims=True)
        for s in range(count):

            @pl.when(i // per == s)
            def _():
                put_columns(o_ref, back + refs[s][...].astype(F32), p[1], half)

    def spec(s):
        return pl.BlockSpec((block, width), lambda i, p: (jnp.clip(i - s * per, 0, per - 1), 0))

    return call(
        body,
        (rows // block,),
        [
            pl.BlockSpec((block, half), lambda i, p: (i, p[1])),
            pl.BlockSpec((block, half), lambda i, p: (i, 1 - p[1])),
            pl.BlockSpec((block, width), lambda i, p: (i, 0)),
            pl.BlockSpec((1, width), lambda i, p: (0, 0)),
        ]
        + [spec(s) for s in range(count)],
        pl.BlockSpec((block, width), lambda i, p: (i, 0)),
        jax.ShapeDtypeStruct((rows, width), F32),
        scalars=1,
    )(place, x, x, upstream, gain, *d2)


def gain_rows(x, upstream, place, block):
    rows, width = x.shape
    half = width // 2

    def body(p, a_ref, b_ref, u_ref, sum_ref):
        i = pl.program_id(0)
        h = jnp.concatenate([a_ref[...], b_ref[...]], 1)
        inv = lax.rsqrt(jnp.mean(h * h, axis=-1, keepdims=True) + NORM_EPS)
        total = jnp.sum(u_ref[...].astype(F32) * h * inv, axis=0, keepdims=True)

        @pl.when(i == 0)
        def _():
            sum_ref[...] = total

        @pl.when(i > 0)
        def _():
            sum_ref[...] += total

    return call(
        body,
        (rows // block,),
        [
            pl.BlockSpec((block, half), lambda i, p: (i, p[1])),
            pl.BlockSpec((block, half), lambda i, p: (i, 1 - p[1])),
            pl.BlockSpec((block, width), lambda i, p: (i, 0)),
        ],
        pl.BlockSpec((1, width), lambda i, p: (0, 0)),
        jax.ShapeDtypeStruct((1, width), F32),
        scalars=1,
    )(place, x, x, upstream)


def per_device(
    sizes, hidden_in, cotangent, w_qkv, w_out, w_gate_up, w_down, norm_gains, segments
):
    n_seq, n_tp, n_rep = sizes
    seqs, length, width = hidden_in.shape
    total = segments.shape[1]
    qkv_width = w_qkv.shape[3]
    group = qkv_width // HEAD_DIM - 2
    ff = w_down.shape[1]
    rows = seqs * length
    scale = float(HEAD_DIM) ** (-0.5)
    two = n_seq == 2
    si = lax.axis_index("seq")
    ti = lax.axis_index("tp")
    zi = lax.axis_index("rep")
    core, yi = ti % 2, ti // 2
    half = width // 2
    fourth = width // 4
    quarter = length // 4
    own = core * 2 + yi
    col_swap = si if two else jnp.int32(0) * si
    pz = zi % 2
    place = jnp.stack([own, col_swap, pz]).astype(jnp.int32)
    middle = (zi == 1) | (zi == 2)
    mid_flag = jnp.reshape(middle, (1,)).astype(jnp.int32)
    order = Order()

    def swap_seq(x):
        return lax.ppermute(x, "seq", [(0, 1), (1, 0)])

    def swap_core(x):
        return lax.ppermute(x, "tp", [(0, 1), (1, 0), (2, 3), (3, 2)])

    def swap_y(x):
        return lax.ppermute(x, "tp", [(0, 2), (2, 0), (1, 3), (3, 1)])

    def swap_z(x):
        return lax.ppermute(x, "rep", [(0, 1), (1, 0), (2, 3), (3, 2)])

    def hop_in(x):
        return lax.ppermute(x, "rep", [(0, 1), (3, 2)])

    def hop_mid(x):
        return lax.ppermute(x, "rep", [(1, 2), (2, 1)])

    def hop_out(x):
        return lax.ppermute(x, "rep", [(1, 0), (2, 3)])

    def whole(shard, axis):
        return lax.all_gather(shard, "seq", axis=axis, tiled=True)

    def now(*xs):
        return lax.optimization_barrier((xs, order.last))[0]

    def share(x):
        far = swap_y(x)
        return [x, far, swap_core(x), swap_core(far)]

    wq, wo, wd, wg = w_qkv[0, :, 0, :], w_out[0], w_down[0], w_gate_up[0]
    if two:
        gains = jnp.concatenate([norm_gains[0], swap_seq(norm_gains[0])], 1).astype(F32)
        qkv_parts = [Part(wq), Part(swap_seq(wq), half)]
        out_x = swap_seq(lax.dynamic_slice_in_dim(wo, pz * fourth, fourth, 1))

        def spread(*blocks):
            return order(lambda w, p: spread_gate_up(w, p, list(blocks)), wg, place)

        gu_a = spread(lambda p: 4 * p[2])
    else:
        gains = whole(norm_gains[0], 1).astype(F32)
        qkv_parts, out_parts = [Part(whole(wq, 0))], [Part(whole(wo, 1))]
        down_parts = [Part(whole(wd, 1))]
        gu_parts = [Part(spread_gate_up(whole(wg, 0), place, None))]

    first_row = si * length
    ids = jnp.arange(total, dtype=jnp.int32)
    change = jnp.concatenate(
        [jnp.ones((seqs, 1), bool), segments[:, 1:] != segments[:, :-1]], axis=1
    )
    doc_start = lax.cummax(jnp.where(change, ids[None, :], 0), axis=1)
    starts = lax.dynamic_slice_in_dim(doc_start, first_row, length, 1)
    pos = first_row + jnp.arange(length, dtype=jnp.int32)[None, :] - starts
    inverse_freq = ROPE_THETA ** (-(jnp.arange(HEAD_DIM // 2, dtype=F32) / (HEAD_DIM // 2)))
    angles = inverse_freq[None, :, None] * pos.astype(F32)[:, None, :]
    cos_t, sin_t = jnp.cos(angles), jnp.sin(angles)
    starts3 = starts[:, None, :]
    tq, tk = min(256, length), min(256, total)
    tiles = jnp.arange(length // tq, dtype=jnp.int32)
    ends = (first_row + (tiles + 1) * tq + tk - 1) // tk
    bounds = [
        jnp.concatenate(
            [
                jnp.stack([first_row, pz]),
                jnp.stack([starts[s, ::tq] // tk, ends], axis=1).reshape(-1),
            ]
        ).astype(jnp.int32)
        for s in range(seqs)
    ]

    hidden = hidden_in.reshape(rows, width)
    d_hidden = cotangent.reshape(rows, width)
    normed1 = order(lambda h, g, p: first_norm(h, g, p, 2 * quarter), hidden, gains[:1], place)
    if two:
        gu_c = spread(lambda p: 1, lambda p: 5)
    dhb = order(lambda d, p: local_cast(d, p, quarter), d_hidden, place)
    own_h, own_d = [None] * seqs, [None] * seqs
    for s in range(seqs):
        own_h[s], own_d[s] = order(
            lambda h, d, p, s=s: by_rows(
                lambda h, d: (h, d), p, s, quarter, [h, d], [], [], [F32, F32]
            ),
            hidden, d_hidden, place,
        )
    q_t, kv_t = order(
        lambda n, w, c, s: project_qkv(n, w, c, s, group),
        normed1, [x.array for x in qkv_parts], cos_t, sin_t,
    )
    if two:
        kv_got = lax.ppermute(kv_t, "seq", [(0, 1)])
        gu_x = [swap_seq(*now(gu_a))]
        gu_b = spread(lambda p: 4 * p[2] + 2, lambda p: 4 * p[2] + 3)
        out_z = swap_z(*now(out_x))
        all_kv = order(join_kv, kv_t, kv_got, place)
        out_parts = [Part(wo), Part(out_x, 0, 0), Part(out_z, 0, 1)]
    else:
        all_kv = whole(kv_t, 2)

    att, att_t, lse = [None] * seqs, [None] * seqs, [None] * seqs
    hold, keep = [None] * seqs, [None] * seqs

    def attention(s):
        att[s], att_t[s], lse[s] = order(
            lambda q, kv, st, b, s=s: attend(s, q, kv, st, b, scale),
            q_t, all_kv, starts3, bounds[s],
        )

    def out_product(s):
        send, keep[s] = order(
            lambda a, w, p: split_matmul(a, w, False, True, p, 1), att[s], out_parts, place
        )
        hold[s] = swap_core(send)

    def summed(keep, hold, s):
        send, keep[s] = order(first_sum, keep[s], hold[s])
        hold[s] = swap_y(send)

    attention(0)
    if two:
        touch(order, gu_x[0])
        gu_z = [swap_z(*now(gu_x[0]))]
        gu_x += [swap_seq(*now(gu_b))]
    out_product(0)
    for s in range(1, seqs):
        attention(s)
        summed(keep, hold, s - 1)
        out_product(s)
    if two:
        own_c = [gu_c[k * 128 : (k + 1) * 128] for k in range(2)]
        gu_c = [swap_seq(x) for x in now(*own_c)]
    summed(keep, hold, seqs - 1)
    if two:
        touch(order, gu_x[1])
        gu_z += [swap_z(*now(gu_x[1]))]
        piece = fourth // 2
        down_send = order(
            lambda w: (
                lax.dynamic_slice_in_dim(w, pz * fourth, piece, 1),
                w[:, piece : 2 * piece],
                w[:, 3 * piece :],
            ),
            wd,
        )
    h2, n2, extra = [None] * seqs, [None] * seqs, [None] * seqs

    def second_norm(h, k, g, gain):
        x = h + k + g
        inv = lax.rsqrt(jnp.mean(x * x, axis=-1, keepdims=True) + NORM_EPS)
        return x, x * inv * gain, k + g

    for s in range(seqs):
        h2[s], mine, extra[s] = order(
            lambda h, k, g, gain, p, s=s: by_rows(
                second_norm, p, s, quarter, [], [h, k, g], [gain], [F32, BF16, BF16]
            ),
            own_h[s], keep[s], hold[s], gains[1:], place,
        )
        n2[s] = share(mine)
        if two and s == 0:
            gu_d = spread(*[lambda p, k=k: 4 * (1 - p[2]) + k for k in (0, 2, 3)])
            touch(order, gu_z[0], gu_c[0])
            down_send = now(*down_send)
            down_x = swap_seq(down_send[0])
            down_c = [swap_seq(x) for x in down_send[1:]]
    if two:
        gu_parts = [Part(gu_a, -half, 0), Part(gu_b, 256 - half, 0)]
        gu_parts += [Part(own_c[k], k * fourth + 128) for k in range(2)]
        gu_parts += [Part(gu_d[:128], -half, 1), Part(gu_d[128:], 256 - half, 1)]
        gu_parts += [Part(gu_x[k], k * 256, 0) for k in range(2)]
        gu_parts += [Part(gu_z[k], k * 256, 1) for k in range(2)]
        gu_parts += [Part(gu_c[k], half + k * fourth + 128) for k in range(2)]
        touch(order, down_x)
        down_z = swap_z(*now(down_x))
        down_parts = [Part(wd), Part(down_x, 0, 0), Part(down_z, 0, 1)]
        down_parts += [Part(down_c[k], half + k * fourth + piece) for k in range(2)]
    n2_all, act, gu = order(gate_up, [x for b in n2 for x in b], gu_parts, place)

    class Chunk:
        def __init__(self, finish):
            self.finish, self.stage = finish, 0

        def begin(self, make, *xs):
            self.make, self.xs = make, xs
            self.got = swap_seq(order(lambda *x: make(1, *x), *xs))

        def next(self):
            k = self.stage
            self.stage += 1
            assert k < 4
            if k == 0:
                self.sum = order(
                    lambda g, *x: (self.make(0, *x) + g.astype(F32)).astype(g.dtype),
                    self.got, *self.xs,
                )
            elif k < 3:
                self.sum = order(self.add, self.sum, self.got)
            else:
                self.finish(self.sum, self.got)
            if k < 3:
                self.got = (hop_in, hop_mid, hop_out)[k](self.sum)

        def add(self, a, b):
            return a + b if a.dtype == F32 else add_pair(a, b)

    chunks, results = {}, {}

    def begin(name, finish, make, *xs):
        if two:
            chunks[name] = Chunk(finish)
            chunks[name].begin(make, *xs)

    def go(*names):
        for name in names:
            if two:
                chunks[name].next()

    def into(name, writer):
        def finish(a, b):
            results[name] = [
                order(lambda a, b, m, r: writer(a, b, m, r), a, b, mid_flag, results.get(name, []))
            ]

        return finish

    def piece_of(x, k, at, size):
        return x[:, k * half + at : k * half + at + size]

    def tdot(a, b, k):
        x = dot(a, b, 0, 0)
        return x.astype(BF16) if k else x

    cuts = [0, 768, ff]
    gu_rows = [256, 256, 256, 128, 128]

    def begin_down(j):
        begin(
            f"d{j}",
            into("down", lambda a, b, m, r: place_rows(a, b, m, cuts[j], ff, r)),
            lambda k, a, d: tdot(a[:, cuts[j] : cuts[j + 1]], piece_of(d, k, 0, half), k),
            act, dhb,
        )

    def begin_gu(j):
        at = sum(gu_rows[:j])
        begin(
            f"g{j}",
            into("gu", lambda a, b, m, r: join_gate_up(a, b, m, at, half, r)),
            lambda k, n, d: tdot(piece_of(n, k, at, gu_rows[j]), d, k),
            n2_all, dgu,
        )

    begin_down(0)
    if two:

        def pair(a, c, first):
            return jnp.concatenate([a, jnp.where(first, c[0], c[1])])

        begin_down(1)
        near = order(lambda a, c: pair(a, c, pz == 0), gu_a, own_c)
        far = order(lambda a, c: pair(a, c, pz == 1), gu_d[:128], own_c)
        pair_x = order(lambda a, c: pair(a, c, pz == 0), gu_x[0], gu_c)
        pair_z = order(lambda a, c: pair(a, c, pz == 1), gu_z[0], gu_c)
        gu_parts = [Part(near, -half, 0), Part(gu_b, 256 - half, 0)]
        gu_parts += [Part(far, -half, 1), Part(gu_d[128:], 256 - half, 1)]
        gu_parts += [Part(pair_x, 0, 0), Part(gu_x[1], 256, 0)]
        gu_parts += [Part(pair_z, 0, 1), Part(gu_z[1], 256, 1)]
    dgu = order(gate_back, dhb, down_parts, gu, place)
    got = order(
        lambda a, w, p: split_matmul(a, w, True, False, p, seqs), dgu, gu_parts, place
    )
    keep, hold = list(got[1::2]), [swap_core(x) for x in got[::2]]
    go("d0")
    for s in range(seqs):
        summed(keep, hold, s)
    begin_gu(0)
    d2, gain2 = [None] * seqs, []

    def second_back(d, k, g, x, gain):
        mine = k + g
        inv = lax.rsqrt(jnp.mean(x * x, axis=-1, keepdims=True) + NORM_EPS)
        w = gain * mine
        back = inv * w - x * (inv * inv * inv) * jnp.mean(w * x, axis=-1, keepdims=True)
        return back + d, jnp.sum(mine * x * inv, axis=0, keepdims=True)

    for s in range(seqs):
        mine, g2 = order(
            lambda d, k, g, x, gain, p, s=s: by_rows(
                second_back, p, s, quarter, [], [d, k, g, x], [gain], [BF16], 1
            ),
            own_d[s], keep[s], hold[s], h2[s], gains[1:], place,
        )
        gain2.append(g2)
        d2[s] = share(mine)
        if s == 0:
            go("d1")
    go("d0")
    dq, dkv, early = [None] * seqs, [None] * seqs, [None] * seqs
    dkv_got = []
    for s in range(seqs):
        d2[s] = order(stack, d2[s], place)
        dq[s], dkv[s], early[s] = order(
            lambda q, kv, st, b, a, w, *x, s=s: attend_back(s, q, kv, st, b, a, w, *x, scale),
            q_t, all_kv, starts3, bounds[s], att_t[s], out_parts, d2[s], lse[s], cos_t, sin_t,
        )
        if two:
            dkv_got.append(lax.ppermute(early[s], "seq", [(1, 0)]))
        if s == 0:
            go("g0")
    begin(
        "out",
        into("out", lambda a, b, m, r: place_rows(a, b, m, 0, a.shape[0], r)),
        lambda k, a, d: sum(
            dot(x, piece_of(y, k, 0, half), 0, 0) for x, y in zip(a, d)
        ).astype(BF16 if k else F32),
        att, d2,
    )
    go("d0", "d1")
    delta = order(
        lambda a, w, p, x: full_matmul(a, w, False, p, seqs, x), act, down_parts, place, extra
    )
    if not two:
        dkv = [lax.psum_scatter(x, "seq", scatter_dimension=1, tiled=True) for x in dkv]
    d_qkv = order(
        lambda q, kv, g, c, s, p: pack_dqkv(q, kv, g, c, s, p, two),
        dq, dkv, dkv_got, cos_t, sin_t, place,
    )
    begin_gu(1)
    d_n1 = order(lambda a, w, p: full_matmul(a, w, True, p, seqs, []), d_qkv, qkv_parts, place)
    d_part = d_n1
    delta, d_n1 = lax.psum((delta, d_n1), "tp")
    go("g0", "out")
    begin(
        "qkv",
        into("qkv", lambda a, b, m, r: place_rows(a, b, m, 0, half, r)),
        lambda k, n, d: tdot(piece_of(n, k, 0, half), d, k),
        normed1, d_qkv,
    )
    go("d0", "d1")
    gain1 = order(lambda h, u, p: gain_rows(h, u, p, quarter), hidden, d_part, place)
    go("g1", "out", "g0")
    begin_gu(2)
    gain_sum = order(lambda a, b: jnp.concatenate([a, sum(b)]), gain1, gain2)
    gain_sum = order(lambda a, b: a + b, gain_sum, swap_core(gain_sum))
    gain_sum = order(lambda a, b: a + b, gain_sum, swap_y(gain_sum))

    def gain_finish(a, b):
        results["gain"] = [order(lambda a, b: jnp.where(middle, a, b), a, b)]

    go("qkv", "d1", "g1", "out", "g0")
    begin_gu(3)
    begin("gain", gain_finish, lambda k, g: piece_of(g, k, 0, half), gain_sum)
    go("g2", "qkv", "g1", "out", "gain")
    begin_gu(4)
    go("g3", "g2", "qkv", "gain", "g1")
    go("g4", "g3", "g2", "gain", "qkv")
    go("g4", "g3", "g2", "gain", "g4")
    hidden_out = order(lambda h, d, p: add_columns(h, d, p, quarter), hidden, delta, place)
    grad_in = order(
        lambda h, u, d, g, p: first_norm_back(h, u, d, g, p, quarter),
        hidden, d_n1, d2, gains[:1], place,
    )
    go("g3", "g4")
    if two:
        g_qkv, g_out, g_down = results["qkv"][0], results["out"][0], results["down"][0]
        g_gu, gain_own = results["gu"][0], results["gain"][0]
    else:

        def reduce_rep(x):
            if n_rep != 4:
                return lax.psum(x.astype(F32), "rep").astype(BF16)
            x = x.astype(BF16)
            x = (x.astype(F32) + hop_in(x).astype(F32)).astype(BF16)
            x = (x.astype(F32) + hop_mid(x).astype(F32)).astype(BF16)
            return jnp.where(middle, x, hop_out(x))

        def reduce(x, axis):
            return reduce_rep(lax.psum_scatter(x, "seq", scatter_dimension=axis, tiled=True))

        g_down = reduce(dot(act, dhb, 0, 0), 1).astype(F32)
        g_out = reduce(sum(dot(x, y, 0, 0) for x, y in zip(att, d2)), 1).astype(F32)
        g_qkv = reduce(dot(normed1, d_qkv, 0, 0), 0).astype(F32)
        g_gu = reduce(dot(n2_all, dgu, 0, 0), 0)
        g_gu = join_gate_up(g_gu, g_gu, mid_flag, 0, g_gu.shape[0], [])
        gain_own = lax.psum_scatter(gain_sum, "seq", scatter_dimension=1, tiled=True)
        gain_own = lax.psum(gain_own, "rep")
    return (
        hidden_out.reshape(seqs, length, width),
        grad_in.reshape(seqs, length, width),
        g_qkv[None, :, None, :],
        g_out[None],
        g_gu,
        g_down[None],
        gain_own[None],
    )


def solution(mesh):
    in_specs = (
        P("rep", "seq", None),
        P("rep", "seq", None),
        P(None, "seq", "tp", None),
        P(None, "tp", "seq"),
        P(None, "seq", None, "tp"),
        P(None, "tp", "seq"),
        P(None, None, "seq"),
        P("rep", None),
    )
    out_specs = (
        P("rep", "seq", None),
        P("rep", "seq", None),
        P(None, "seq", "tp", None),
        P(None, "tp", "seq"),
        P(None, "seq", None, "tp"),
        P(None, "tp", "seq"),
        P(None, None, "seq"),
    )
    sizes = (mesh.shape["seq"], mesh.shape["tp"], mesh.shape["rep"])
    return jax.shard_map(
        functools.partial(per_device, sizes),
        mesh=mesh,
        in_specs=in_specs,
        out_specs=out_specs,
        check_vma=False,
    )
```

```python
import dataclasses
import functools
from typing import Any

import jax
import jax.numpy as jnp
from jax import lax
from jax.experimental import pallas as pl
from jax.experimental.pallas import tpu as pltpu
from jax.sharding import PartitionSpec as P

HEAD_DIM = 64
NORM_EPS = 1e-05
ROPE_THETA = 10000.0
LOG2E = 1.4426950408889634
MASKED = -1e30
F32 = jnp.float32
BF16 = jnp.bfloat16
MIB = 1024 * 1024


def touch(order, *xs):
    order.last = (*order.last, *xs)


def dot(a, b, ca=1, cb=0):
    return lax.dot_general(a, b, (((ca,), (cb,)), ((), ())), preferred_element_type=F32)


def call(body, grid, ins, outs, shapes, scratch=(), scalars=0, alias=None, vmem=16):
    return pl.pallas_call(
        body,
        out_shape=shapes,
        grid_spec=pltpu.PrefetchScalarGridSpec(
            num_scalar_prefetch=scalars,
            grid=grid,
            in_specs=ins,
            out_specs=outs,
            scratch_shapes=list(scratch),
        ),
        input_output_aliases=alias or {},
        compiler_params=pltpu.CompilerParams(vmem_limit_bytes=vmem * MIB),
        cost_estimate=pl.CostEstimate(flops=3000000000, bytes_accessed=8000000, transcendentals=0),
    )


@functools.partial(
    jax.tree_util.register_dataclass, data_fields=["array"], meta_fields=["base", "late"]
)
@dataclasses.dataclass(frozen=True)
class Part:
    array: Any
    base: int = 0
    late: Any = None

    def start(self, width, p):
        if self.late is None:
            return self.base
        return width // 2 + (p ^ self.late) * (width // 4) + self.base


class Order:
    def __init__(self):
        self.last = ()

    def __call__(self, step, *xs):
        flat, tree = jax.tree.flatten(xs)
        if self.last:
            flat = lax.optimization_barrier((tuple(flat), self.last))[0]
        out = step(*jax.tree.unflatten(tree, flat))
        self.last = tuple(jax.tree.leaves(out))
        return out


def first_norm(hidden, gain, place, block):
    rows, width = hidden.shape
    half = width // 2

    def body(p, a_ref, b_ref, g_ref, n_ref):
        a, b = a_ref[...], b_ref[...]
        total = jnp.sum(a * a, -1, keepdims=True) + jnp.sum(b * b, -1, keepdims=True)
        inv = lax.rsqrt(total * (1.0 / width) + NORM_EPS)
        n_ref[:, :half] = (a * inv * g_ref[:, :half]).astype(BF16)
        n_ref[:, half:] = (b * inv * g_ref[:, half:]).astype(BF16)

    return call(
        body,
        (rows // block,),
        [
            pl.BlockSpec((block, half), lambda i, p: (i, p[1])),
            pl.BlockSpec((block, half), lambda i, p: (i, 1 - p[1])),
            pl.BlockSpec((1, width), lambda i, p: (0, 0)),
        ],
        pl.BlockSpec((block, width), lambda i, p: (i, 0)),
        jax.ShapeDtypeStruct((rows, width), BF16),
        scalars=1,
    )(place, hidden, hidden, gain)


def local_cast(x, place, block):
    rows, width = x.shape
    half = width // 2

    def body(p, a_ref, b_ref, o_ref):
        o_ref[:, :half] = a_ref[...].astype(BF16)
        o_ref[:, half:] = b_ref[...].astype(BF16)

    def row(i, p):
        return (i // 4) * 4 + ((i % 4) ^ p[0])

    return call(
        body,
        (rows // block,),
        [
            pl.BlockSpec((block, half), lambda i, p: (row(i, p), p[1])),
            pl.BlockSpec((block, half), lambda i, p: (row(i, p), 1 - p[1])),
        ],
        pl.BlockSpec((block, width), lambda i, p: (i, 0)),
        jax.ShapeDtypeStruct((rows, width), BF16),
        scalars=1,
    )(place, x, x)


def join_gate_up(a, b, middle, at, rows, before):
    count, cols = a.shape
    ff = cols // 2
    block = min(128, count)

    def body(p, a_ref, b_ref, *refs):
        o_ref = refs[-1]

        def put(src):
            for j in range(ff // 128):
                for g in range(2):
                    o_ref[0, :, g, 128 * j : 128 * (j + 1)] = src[
                        :, 256 * j + 128 * g : 256 * j + 128 * (g + 1)
                    ].astype(F32)

        @pl.when(p[0] == 1)
        def _():
            put(a_ref)

        @pl.when(p[0] == 0)
        def _():
            put(b_ref)

    return call(
        body,
        (count // block,),
        [pl.BlockSpec((block, cols), lambda i, p: (i, 0))] * 2
        + [pl.BlockSpec(memory_space=pl.ANY)] * len(before),
        pl.BlockSpec((1, block, 2, ff), lambda i, p: (0, at // block + i, 0, 0)),
        jax.ShapeDtypeStruct((1, rows, 2, ff), F32),
        scalars=1,
        alias={3 + k: k for k in range(len(before))},
    )(middle, a, b, *before)


def project_qkv(normed, weights, cos_t, sin_t, group):
    rows, width = normed.shape
    seqs, half, length = cos_t.shape
    cols = weights[0].shape[1]
    tile = min(256, length)
    per = length // tile
    depth = width // len(weights)
    parts = len(weights)

    def body(n_ref, cos_ref, sin_ref, *refs):
        q_ref, kv_ref = refs[parts:]
        acc = dot(n_ref[:, :depth], refs[0][...])
        for k in range(1, parts):
            acc = acc + dot(n_ref[:, k * depth : (k + 1) * depth], refs[k][...])
        t = acc.T
        cos, sin = cos_ref[0], sin_ref[0]
        for h in range(group + 1):
            a, b = t[2 * half * h : 2 * half * h + half], t[2 * half * h + half : 2 * half * (h + 1)]
            r = jnp.concatenate([a * cos - b * sin, b * cos + a * sin], 0).astype(BF16)
            if h < group:
                q_ref[0, 2 * half * h : 2 * half * (h + 1)] = r
            else:
                kv_ref[0, : 2 * half] = r
        kv_ref[0, 2 * half :] = t[2 * half * (group + 1) :].astype(BF16)

    return call(
        body,
        (seqs, per),
        [
            pl.BlockSpec((tile, width), lambda s, i: (s * per + i, 0)),
            pl.BlockSpec((1, half, tile), lambda s, i: (s, 0, i)),
            pl.BlockSpec((1, half, tile), lambda s, i: (s, 0, i)),
        ]
        + [pl.BlockSpec((depth, cols), lambda s, i: (0, 0))] * parts,
        [
            pl.BlockSpec((1, group * HEAD_DIM, tile), lambda s, i: (s, 0, i)),
            pl.BlockSpec((1, 2 * HEAD_DIM, tile), lambda s, i: (s, 0, i)),
        ],
        [
            jax.ShapeDtypeStruct((seqs, group * HEAD_DIM, length), BF16),
            jax.ShapeDtypeStruct((seqs, 2 * HEAD_DIM, length), BF16),
        ],
    )(normed, cos_t, sin_t, *weights)


def attend(s, q_t, kv_t, starts, bounds, scale):
    seqs, cols, length = q_t.shape
    total = kv_t.shape[2]
    heads = cols // HEAD_DIM
    tq, tk = min(256, length), min(256, total)

    def body(b_ref, q_ref, kv_ref, st_ref, att_ref, att_t_ref, lse_ref, kn, m, l, acc):
        i = pl.program_id(0)

        @pl.when(i == 0)
        def _():
            kn[...] = kv_ref[0, :HEAD_DIM].astype(F32).T.astype(BF16)

        qid = b_ref[0] + i * tq + lax.broadcasted_iota(jnp.int32, (1, tq), 1)
        start = st_ref[0]
        m[...] = jnp.full_like(m, MASKED)
        l[...] = jnp.zeros_like(l)
        acc[...] = jnp.zeros_like(acc)

        def step(t, _):
            k0 = pl.multiple_of(t * tk, tk)
            kid = k0 + lax.broadcasted_iota(jnp.int32, (tk, 1), 0)
            ok = (kid <= qid) & (kid >= start)
            keys = kn[pl.ds(k0, tk), :]
            vals = kv_ref[0, HEAD_DIM:, pl.ds(k0, tk)]
            for h in range(heads):
                lo = h * HEAD_DIM
                sc = dot(keys, q_ref[0, lo : lo + HEAD_DIM]) * (scale * LOG2E)
                sc = jnp.where(ok, sc, MASKED)
                old = m[h : h + 1]
                new = jnp.maximum(old, jnp.max(sc, 0, keepdims=True))
                e = jnp.exp2(sc - new)
                fade = jnp.exp2(old - new)
                m[h : h + 1] = new
                l[h : h + 1] = l[h : h + 1] * fade + jnp.sum(e, 0, keepdims=True)
                acc[lo : lo + HEAD_DIM] = acc[lo : lo + HEAD_DIM] * fade + dot(vals, e.astype(BF16))
            return 0

        lax.fori_loop(b_ref[2 + 2 * i], b_ref[3 + 2 * i], step, 0)
        for h in range(heads):
            lo = h * HEAD_DIM
            acc[lo : lo + HEAD_DIM] = acc[lo : lo + HEAD_DIM] / l[h : h + 1]
        att_t_ref[...] = acc[...].astype(BF16)
        att_ref[...] = acc[...].T.astype(BF16)
        lse_ref[...] = m[...] + jnp.log2(l[...])

    return call(
        body,
        (length // tq,),
        [
            pl.BlockSpec((1, cols, tq), lambda i, b: (s, 0, i)),
            pl.BlockSpec((1, 2 * HEAD_DIM, total), lambda i, b: (s, 0, 0)),
            pl.BlockSpec((1, 1, tq), lambda i, b: (s, 0, i)),
        ],
        [
            pl.BlockSpec((tq, cols), lambda i, b: (i, 0)),
            pl.BlockSpec((cols, tq), lambda i, b: (0, i)),
            pl.BlockSpec((heads, tq), lambda i, b: (0, i)),
        ],
        [
            jax.ShapeDtypeStruct((length, cols), BF16),
            jax.ShapeDtypeStruct((cols, length), BF16),
            jax.ShapeDtypeStruct((heads, length), F32),
        ],
        scratch=[
            pltpu.VMEM((total, HEAD_DIM), BF16),
            pltpu.VMEM((heads, tq), F32),
            pltpu.VMEM((heads, tq), F32),
            pltpu.VMEM((cols, tq), F32),
        ],
        scalars=1,
    )(bounds, q_t, kv_t, starts)


def attend_back(s, q_t, kv_t, starts, bounds, att_t, out_parts, d2, lse, cos_t, sin_t, scale):
    seqs, cols, length = q_t.shape
    width = d2.shape[1]
    parts = len(out_parts)
    total = kv_t.shape[2]
    heads = cols // HEAD_DIM
    half = HEAD_DIM // 2
    tq, tk = min(256, length), min(256, total)

    def body(
        b_ref, q_ref, kv_ref, st_ref, a_ref, d2_ref, lse_ref, cos_ref, sin_ref, *refs
    ):
        w_refs = refs[:parts]
        dq_ref, dkv_ref, early_ref, kn, vn, delta, acc, d_ref = refs[parts:]
        i = pl.program_id(0)

        @pl.when(i == 0)
        def _():
            kn[...] = kv_ref[0, :HEAD_DIM].astype(F32).T.astype(BF16)
            vn[...] = kv_ref[0, HEAD_DIM:].astype(F32).T.astype(BF16)
            dkv_ref[...] = jnp.zeros_like(dkv_ref)

        d_att = 0.0
        for part, w_ref in zip(out_parts, w_refs):
            size = part.array.shape[1]
            at = part.start(width, b_ref[1])
            if part.late is not None:
                at = pl.multiple_of(at, 128)
            d_att = d_att + dot(w_ref[...], d2_ref[:, pl.ds(at, size)], 1, 1)
        d_ref[...] = d_att.astype(BF16)
        qid = b_ref[0] + i * tq + lax.broadcasted_iota(jnp.int32, (1, tq), 1)
        start = st_ref[0]
        for h in range(heads):
            lo = h * HEAD_DIM
            prod = d_ref[lo : lo + HEAD_DIM].astype(F32) * a_ref[lo : lo + HEAD_DIM].astype(F32)
            delta[h : h + 1] = jnp.sum(prod, 0, keepdims=True)
        acc[...] = jnp.zeros_like(acc)

        def step(t, _):
            k0 = pl.multiple_of(t * tk, tk)
            kid = k0 + lax.broadcasted_iota(jnp.int32, (tk, 1), 0)
            ok = (kid <= qid) & (kid >= start)
            keys, vals = kn[pl.ds(k0, tk), :], vn[pl.ds(k0, tk), :]
            keys_t = kv_ref[0, :HEAD_DIM, pl.ds(k0, tk)]
            dk = jnp.zeros((HEAD_DIM, tk), F32)
            dv = jnp.zeros((HEAD_DIM, tk), F32)
            for h in range(heads):
                lo = h * HEAD_DIM
                q, d = q_ref[0, lo : lo + HEAD_DIM], d_ref[lo : lo + HEAD_DIM]
                sc = dot(keys, q) * (scale * LOG2E) - lse_ref[h : h + 1]
                p = jnp.exp2(jnp.where(ok, sc, MASKED))
                dp = dot(vals, d)
                ds = (p * (dp - delta[h : h + 1]) * scale).astype(BF16)
                dv = dv + dot(d, p.astype(BF16), 1, 1)
                dk = dk + dot(q, ds, 1, 1)
                acc[lo : lo + HEAD_DIM] += dot(keys_t, ds)
            dkv_ref[:HEAD_DIM, pl.ds(k0, tk)] += dk
            dkv_ref[HEAD_DIM:, pl.ds(k0, tk)] += dv
            return 0

        lax.fori_loop(b_ref[2 + 2 * i], b_ref[3 + 2 * i], step, 0)
        cos, sin = cos_ref[0], sin_ref[0]
        for h in range(heads):
            lo = h * HEAD_DIM
            c, e = acc[lo : lo + half], acc[lo + half : lo + HEAD_DIM]
            acc[lo : lo + HEAD_DIM] = jnp.concatenate([c * cos + e * sin, e * cos - c * sin], 0)
        dq_ref[...] = acc[...].T.astype(BF16)
        early_ref[...] = dkv_ref[:, :length].astype(BF16)

    return call(
        body,
        (length // tq,),
        [
            pl.BlockSpec((1, cols, tq), lambda i, b: (s, 0, i)),
            pl.BlockSpec((1, 2 * HEAD_DIM, total), lambda i, b: (s, 0, 0)),
            pl.BlockSpec((1, 1, tq), lambda i, b: (s, 0, i)),
            pl.BlockSpec((cols, tq), lambda i, b: (0, i)),
            pl.BlockSpec((tq, d2.shape[1]), lambda i, b: (i, 0)),
            pl.BlockSpec((heads, tq), lambda i, b: (0, i)),
            pl.BlockSpec((1, half, tq), lambda i, b: (s, 0, i)),
            pl.BlockSpec((1, half, tq), lambda i, b: (s, 0, i)),
        ]
        + [pl.BlockSpec(p.array.shape, lambda i, b: (0, 0)) for p in out_parts],
        [
            pl.BlockSpec((tq, cols), lambda i, b: (i, 0)),
            pl.BlockSpec((2 * HEAD_DIM, total), lambda i, b: (0, 0)),
            pl.BlockSpec((2 * HEAD_DIM, length), lambda i, b: (0, 0)),
        ],
        [
            jax.ShapeDtypeStruct((length, cols), BF16),
            jax.ShapeDtypeStruct((2 * HEAD_DIM, total), F32),
            jax.ShapeDtypeStruct((2 * HEAD_DIM, length), BF16),
        ],
        scratch=[
            pltpu.VMEM((total, HEAD_DIM), BF16),
            pltpu.VMEM((total, HEAD_DIM), BF16),
            pltpu.VMEM((heads, tq), F32),
            pltpu.VMEM((cols, tq), F32),
            pltpu.VMEM((cols, tq), BF16),
        ],
        scalars=1,
    )(
        bounds, q_t, kv_t, starts, att_t, d2, lse, cos_t, sin_t, *[p.array for p in out_parts]
    )


def join_kv(mine, other, place):
    seqs, cols, length = mine.shape

    def body(p, m_ref, o_ref, out_ref):
        @pl.when(pl.program_id(0) == 0)
        def _():
            out_ref[...] = m_ref[...]

        @pl.when(pl.program_id(0) == 1)
        def _():
            out_ref[...] = o_ref[...]

    spec = pl.BlockSpec(mine.shape, lambda i, p: (0, 0, 0))
    return call(
        body,
        (2,),
        [spec, spec],
        pl.BlockSpec(mine.shape, lambda i, p: (0, 0, i ^ p[1])),
        jax.ShapeDtypeStruct((seqs, cols, 2 * length), mine.dtype),
        scalars=1,
    )(place, mine, other)


def stack(pieces, place):
    quarter, width = pieces[0].shape
    count = len(pieces)

    def body(p, *refs):
        for k in range(count):

            @pl.when(pl.program_id(0) == k)
            def _():
                refs[-1][...] = refs[k][...]

    return call(
        body,
        (count,),
        [pl.BlockSpec((quarter, width), lambda i, p: (0, 0))] * count,
        pl.BlockSpec((quarter, width), lambda i, p: ((i // 4) * 4 + ((i % 4) ^ p[0]), 0)),
        jax.ShapeDtypeStruct((count * quarter, width), BF16),
        scalars=1,
    )(place, *pieces)


def first_sum(keep, got):
    rows, width = keep.shape
    half = rows // 2
    tile = width // 4

    def body(k_ref, g_ref, send_ref, keep_ref):
        send_ref[...] = (k_ref[half:] + g_ref[half:].astype(F32)).astype(BF16)
        keep_ref[...] = k_ref[:half] + g_ref[:half].astype(F32)

    return call(
        body,
        (4,),
        [pl.BlockSpec((rows, tile), lambda j: (0, j))] * 2,
        [pl.BlockSpec((half, tile), lambda j: (0, j))] * 2,
        [jax.ShapeDtypeStruct((half, width), BF16), jax.ShapeDtypeStruct((half, width), F32)],
    )(keep, got)


def by_rows(step, place, s, quarter, owned, blocks, vectors, outs, sums=0):
    width = (owned or blocks)[0].shape[1]
    half = width // 2
    tile = min(32, quarter)
    per = quarter // tile
    seqs = owned[0].shape[0] // (4 * quarter) if s is None else 1
    n_in = 2 * len(owned) + len(blocks) + len(vectors)

    def body(p, *refs):
        vals = [
            jnp.concatenate([refs[2 * k][...], refs[2 * k + 1][...]], 1) for k in range(len(owned))
        ]
        vals += [r[...].astype(F32) for r in refs[2 * len(owned) : n_in]]
        got = step(*vals)
        for k in range(len(outs)):
            refs[n_in + k][...] = got[k].astype(outs[k])
        for k in range(sums):
            o_ref, x = refs[n_in + len(outs) + k], got[len(outs) + k]

            @pl.when(pl.program_id(0) == 0)
            def _():
                o_ref[...] = x

            @pl.when(pl.program_id(0) > 0)
            def _():
                o_ref[...] += x

    def at(i, p):
        if s is None:
            return ((i // per) * 4 + p[0]) * per + i % per
        return (s * 4 + p[0]) * per + i

    own_specs = [
        pl.BlockSpec((tile, half), lambda i, p: (at(i, p), p[1])),
        pl.BlockSpec((tile, half), lambda i, p: (at(i, p), 1 - p[1])),
    ]
    return call(
        body,
        (seqs * per,),
        own_specs * len(owned)
        + [pl.BlockSpec((tile, width), lambda i, p: (i, 0))] * len(blocks)
        + [pl.BlockSpec((1, width), lambda i, p: (0, 0))] * len(vectors),
        [pl.BlockSpec((tile, width), lambda i, p: (i, 0))] * len(outs)
        + [pl.BlockSpec((1, width), lambda i, p: (0, 0))] * sums,
        [jax.ShapeDtypeStruct((seqs * quarter, width), d) for d in outs]
        + [jax.ShapeDtypeStruct((1, width), F32)] * sums,
        scalars=1,
    )(place, *[x for a in owned for x in (a, a)], *blocks, *vectors)


def pack_dqkv(dqs, dkvs, others, cos_t, sin_t, place, seq_block):
    seqs = len(dqs)
    length, cols = dqs[0].shape
    half = HEAD_DIM // 2
    wide = cols + 2 * HEAD_DIM

    def body(p, cos_ref, sin_ref, *refs):
        o_ref = refs[-1]
        for s in range(seqs):

            @pl.when(pl.program_id(0) == s)
            def _():
                kv = refs[seqs + s][...]
                if others:
                    kv = kv + refs[2 * seqs + s][...].astype(F32)
                c, e = kv[:half], kv[half:HEAD_DIM]
                cos, sin = cos_ref[0], sin_ref[0]
                kv = jnp.concatenate([c * cos + e * sin, e * cos - c * sin, kv[HEAD_DIM:]], 0)
                o_ref[:, :cols] = refs[s][...]
                o_ref[:, cols:] = kv.T.astype(BF16)

    const = lambda i, p: (0, 0)
    return call(
        body,
        (seqs,),
        [pl.BlockSpec((1, half, length), lambda i, p: (i, 0, 0))] * 2
        + [pl.BlockSpec((length, cols), const)] * seqs
        + [
            pl.BlockSpec((2 * HEAD_DIM, length), lambda i, p: (0, p[1] if seq_block else 0))
        ]
        * seqs
        + [pl.BlockSpec((2 * HEAD_DIM, length), const)] * len(others),
        pl.BlockSpec((length, wide), lambda i, p: (i, 0)),
        jax.ShapeDtypeStruct((seqs * length, wide), BF16),
        scalars=1,
    )(place, cos_t, sin_t, *dqs, *dkvs, *others)


def add_pair(a, b):
    rows, cols = a.shape
    block = rows // 4

    def body(a_ref, b_ref, o_ref):
        o_ref[...] = (a_ref[...].astype(F32) + b_ref[...].astype(F32)).astype(BF16)

    spec = pl.BlockSpec((block, cols), lambda i: (i, 0))
    return call(body, (4,), [spec, spec], spec, jax.ShapeDtypeStruct((rows, cols), BF16))(a, b)


def place_rows(a, b, middle, at, rows, before):
    count, cols = a.shape
    block = 128

    def body(p, a_ref, b_ref, *refs):
        o_ref = refs[-1]

        @pl.when(p[0] == 1)
        def _():
            o_ref[...] = a_ref[...].astype(F32)

        @pl.when(p[0] == 0)
        def _():
            o_ref[...] = b_ref[...].astype(F32)

    return call(
        body,
        (count // block,),
        [pl.BlockSpec((block, cols), lambda i, p: (i, 0))] * 2
        + [pl.BlockSpec(memory_space=pl.ANY)] * len(before),
        pl.BlockSpec((block, cols), lambda i, p: (at // block + i, 0)),
        jax.ShapeDtypeStruct((rows, cols), F32),
        scalars=1,
        alias={3 + k: k for k in range(len(before))},
    )(middle, a, b, *before)


def spread_gate_up(w, place, blocks):
    rows, _, ff = w.shape
    block = min(128, rows)
    steps = rows // block if blocks is None else len(blocks)

    def body(p, w_ref, o_ref):
        for j in range(ff // 128):
            for g in range(2):
                o_ref[:, 256 * j + 128 * g : 256 * j + 128 * (g + 1)] = w_ref[
                    :, g, 128 * j : 128 * (j + 1)
                ]

    def row(i, p):
        if blocks is None:
            return i
        r = blocks[0](p)
        for k in range(1, steps):
            r = jnp.where(i == k, blocks[k](p), r)
        return r

    return call(
        body,
        (steps,),
        [pl.BlockSpec((block, 2, ff), lambda i, p: (row(i, p), 0, 0))],
        pl.BlockSpec((block, 2 * ff), lambda i, p: (i, 0)),
        jax.ShapeDtypeStruct((steps * block, 2 * ff), BF16),
        scalars=1,
    )(place, w)


def gate_up(pieces, parts, place):
    quarter, width = pieces[0].shape
    count = len(pieces)
    rows = count * quarter
    ff = parts[0].array.shape[1] // 2
    tile = 128

    def body(p, *refs):
        w_refs = refs[count : count + len(parts)]
        n_ref, act_ref, gu_ref, w_ref = refs[count + len(parts) :]

        @pl.when(pl.program_id(0) == 0)
        def _():
            for k in range(count):
                n_ref[k * quarter : (k + 1) * quarter] = refs[k][...]

        for part, ref in zip(parts, w_refs):
            size = part.array.shape[0]
            at = part.start(width, p[2])
            at = at if part.late is None else pl.multiple_of(at, 128)
            w_ref[pl.ds(at, size), :] = ref[...]
        gu = dot(n_ref[...], w_ref[...])
        gate, up = gu[:, :tile], gu[:, tile:]
        sig = 1.0 / (1.0 + jnp.exp2(gate * (-LOG2E)))
        act_ref[...] = (gate * sig * up).astype(BF16)
        gu_ref[...] = gu.astype(BF16)

    return call(
        body,
        (ff // tile,),
        [pl.BlockSpec((quarter, width), lambda j, p: (0, 0), pipeline_mode=pl.Buffered(1))] * count
        + [pl.BlockSpec((x.array.shape[0], 2 * tile), lambda j, p: (0, j)) for x in parts],
        [
            pl.BlockSpec((rows, width), lambda j, p: (0, 0)),
            pl.BlockSpec((rows, tile), lambda j, p: (0, j)),
            pl.BlockSpec((rows, 2 * tile), lambda j, p: (0, j)),
        ],
        [
            jax.ShapeDtypeStruct((rows, width), BF16),
            jax.ShapeDtypeStruct((rows, ff), BF16),
            jax.ShapeDtypeStruct((rows, 2 * ff), BF16),
        ],
        scratch=[pltpu.VMEM((width, 2 * tile), BF16)],
        scalars=1,
        vmem=30,
    )(place, *pieces, *[x.array for x in parts])


def gate_back(dhb, parts, gu, place):
    rows, width = dhb.shape
    ff = parts[0].array.shape[0]
    tile = 256

    def body(p, d_ref, gu_ref, *refs):
        o_ref = refs[-1]
        d_act = 0.0
        for part, ref in zip(parts, refs):
            at = part.start(width, p[2])
            if part.late is not None:
                at = pl.multiple_of(at, 128)
            d_act = d_act + dot(d_ref[:, pl.ds(at, part.array.shape[1])], ref[...], 1, 1)
        for k in range(tile // 128):
            d = d_act[:, 128 * k : 128 * (k + 1)]
            gate = gu_ref[:, 256 * k : 256 * k + 128].astype(F32)
            up = gu_ref[:, 256 * k + 128 : 256 * (k + 1)].astype(F32)
            sig = 1.0 / (1.0 + jnp.exp2(gate * (-LOG2E)))
            o_ref[:, 256 * k : 256 * k + 128] = (
                d * up * sig * (1.0 + gate * (1.0 - sig))
            ).astype(BF16)
            o_ref[:, 256 * k + 128 : 256 * (k + 1)] = (d * gate * sig).astype(BF16)

    return call(
        body,
        (pl.cdiv(ff, tile),),
        [
            pl.BlockSpec((rows, width), lambda j, p: (0, 0)),
            pl.BlockSpec((rows, 2 * tile), lambda j, p: (0, j)),
        ]
        + [pl.BlockSpec((tile, x.array.shape[1]), lambda j, p: (j, 0)) for x in parts],
        pl.BlockSpec((rows, 2 * tile), lambda j, p: (0, j)),
        jax.ShapeDtypeStruct((rows, 2 * ff), BF16),
        scalars=1,
    )(place, dhb, gu, *[x.array for x in parts])


def split_matmul(a, parts, transposed, natural, place, seqs):
    rows, depth = a.shape
    axis = 0 if transposed else 1
    tile = 256
    counts = [x.array.shape[axis] // tile for x in parts]
    bases = [sum(counts[:k]) for k in range(len(parts))]
    cols = tile * sum(counts)
    length = rows // seqs
    quarter = length // 4

    def body(p, a_ref, *refs):
        w_refs, outs, acc = refs[: len(parts)], refs[len(parts) : -1], refs[-1]
        j = pl.program_id(0)
        for k, w_ref in enumerate(w_refs):

            @pl.when((j >= bases[k]) & (j < bases[k] + counts[k]))
            def _():
                acc[...] = dot(a_ref[...], w_ref[...], 1, 1 - axis)

        for s in range(seqs):
            send, keep = outs[2 * s], outs[2 * s + 1]
            for b in range(4):
                at = s * length + (b ^ p[0] if natural else b) * quarter
                part = acc[pl.ds(at, quarter), :]
                to = (b % 2) * quarter
                if b < 2:
                    keep[to : to + quarter] = part
                else:
                    send[to : to + quarter] = part.astype(BF16)

    def w_spec(k):
        def index(j, p):
            t = jnp.clip(j - bases[k], 0, counts[k] - 1)
            return (t, 0) if transposed else (0, t)

        shape = (tile, depth) if transposed else (depth, tile)
        once = {"pipeline_mode": pl.Buffered(1)} if counts[k] == 1 else {}
        return pl.BlockSpec(shape, index, **once)

    def column(j, p):
        c = parts[0].start(cols, p[2]) // tile + j
        for k in range(1, len(parts)):
            at = parts[k].start(cols, p[2]) // tile + j - bases[k]
            c = jnp.where(j >= bases[k], at, c)
        return (0, c)

    return call(
        body,
        (sum(counts),),
        [pl.BlockSpec((rows, depth), lambda j, p: (0, 0), pipeline_mode=pl.Buffered(1))]
        + [w_spec(k) for k in range(len(parts))],
        [pl.BlockSpec((length // 2, tile), column)] * (2 * seqs),
        [
            jax.ShapeDtypeStruct((length // 2, cols), BF16),
            jax.ShapeDtypeStruct((length // 2, cols), F32),
        ]
        * seqs,
        scratch=[pltpu.VMEM((rows, tile), F32)],
        scalars=1,
    )(place, a, *[x.array for x in parts])


def full_matmul(a, parts, transposed, place, seqs, extras):
    rows, depth = a.shape
    axis = 0 if transposed else 1
    tile = 256
    counts = [x.array.shape[axis] // tile for x in parts]
    bases = [sum(counts[:k]) for k in range(len(parts))]
    cols = tile * sum(counts)
    length = rows // seqs
    quarter = length // 4

    def body(p, a_ref, *refs):
        w_refs, o_ref, acc = refs[: len(parts)], refs[-2], refs[-1]
        j = pl.program_id(0)
        for k, w_ref in enumerate(w_refs):

            @pl.when((j >= bases[k]) & (j < bases[k] + counts[k]))
            def _():
                acc[...] = dot(a_ref[...], w_ref[...], 1, 1 - axis)

        if not extras:
            o_ref[...] = acc[...].astype(BF16)
        for s in range(len(extras)):
            for b in range(4):
                part = acc[s * length + b * quarter : s * length + (b + 1) * quarter]
                if b == 0:
                    part = part + refs[len(parts) + s][...].astype(F32)
                at = pl.multiple_of(s * length + (b ^ p[0]) * quarter, quarter)
                o_ref[pl.ds(at, quarter), :] = part.astype(BF16)

    def w_spec(k):
        def index(j, p):
            t = jnp.clip(j - bases[k], 0, counts[k] - 1)
            return (t, 0) if transposed else (0, t)

        return pl.BlockSpec((tile, depth) if transposed else (depth, tile), index)

    def column(j, p):
        c = parts[0].start(cols, p[2]) // tile + j
        for k in range(1, len(parts)):
            c = jnp.where(j >= bases[k], parts[k].start(cols, p[2]) // tile + j - bases[k], c)
        return (0, c)

    return call(
        body,
        (sum(counts),),
        [pl.BlockSpec((rows, depth), lambda j, p: (0, 0), pipeline_mode=pl.Buffered(1))]
        + [w_spec(k) for k in range(len(parts))]
        + [pl.BlockSpec((quarter, tile), column)] * len(extras),
        pl.BlockSpec((rows, tile), column),
        jax.ShapeDtypeStruct((rows, cols), BF16),
        scratch=[pltpu.VMEM((rows, tile), F32)],
        scalars=1,
    )(place, a, *[x.array for x in parts], *extras)


def put_columns(o_ref, x, swapped, half):
    @pl.when(swapped == 0)
    def _():
        o_ref[...] = x

    @pl.when(swapped == 1)
    def _():
        o_ref[:, :half] = x[:, half:]
        o_ref[:, half:] = x[:, :half]


def add_columns(x, delta, place, block):
    rows, width = x.shape
    half = width // 2

    def body(p, a_ref, b_ref, d_ref, o_ref):
        mine = jnp.concatenate([a_ref[...], b_ref[...]], 1) + d_ref[...].astype(F32)
        put_columns(o_ref, mine, p[1], half)

    return call(
        body,
        (rows // block,),
        [
            pl.BlockSpec((block, half), lambda i, p: (i, p[1])),
            pl.BlockSpec((block, half), lambda i, p: (i, 1 - p[1])),
            pl.BlockSpec((block, width), lambda i, p: (i, 0)),
        ],
        pl.BlockSpec((block, width), lambda i, p: (i, 0)),
        jax.ShapeDtypeStruct((rows, width), F32),
        scalars=1,
    )(place, x, x, delta)


def first_norm_back(x, upstream, d2, gain, place, block):
    rows, width = x.shape
    half = width // 2
    per = d2[0].shape[0] // block
    count = len(d2)

    def body(p, a_ref, b_ref, u_ref, g_ref, *refs):
        o_ref = refs[count]
        i = pl.program_id(0)
        h = jnp.concatenate([a_ref[...], b_ref[...]], 1)
        inv = lax.rsqrt(jnp.mean(h * h, axis=-1, keepdims=True) + NORM_EPS)
        mine = u_ref[...].astype(F32)
        w = g_ref[...] * mine
        back = inv * w - h * (inv * inv * inv) * jnp.mean(w * h, axis=-1, keepdims=True)
        for s in range(count):

            @pl.when(i // per == s)
            def _():
                put_columns(o_ref, back + refs[s][...].astype(F32), p[1], half)

    def spec(s):
        return pl.BlockSpec((block, width), lambda i, p: (jnp.clip(i - s * per, 0, per - 1), 0))

    return call(
        body,
        (rows // block,),
        [
            pl.BlockSpec((block, half), lambda i, p: (i, p[1])),
            pl.BlockSpec((block, half), lambda i, p: (i, 1 - p[1])),
            pl.BlockSpec((block, width), lambda i, p: (i, 0)),
            pl.BlockSpec((1, width), lambda i, p: (0, 0)),
        ]
        + [spec(s) for s in range(count)],
        pl.BlockSpec((block, width), lambda i, p: (i, 0)),
        jax.ShapeDtypeStruct((rows, width), F32),
        scalars=1,
    )(place, x, x, upstream, gain, *d2)


def gain_rows(x, upstream, place, block):
    rows, width = x.shape
    half = width // 2

    def body(p, a_ref, b_ref, u_ref, sum_ref):
        i = pl.program_id(0)
        h = jnp.concatenate([a_ref[...], b_ref[...]], 1)
        inv = lax.rsqrt(jnp.mean(h * h, axis=-1, keepdims=True) + NORM_EPS)
        total = jnp.sum(u_ref[...].astype(F32) * h * inv, axis=0, keepdims=True)

        @pl.when(i == 0)
        def _():
            sum_ref[...] = total

        @pl.when(i > 0)
        def _():
            sum_ref[...] += total

    return call(
        body,
        (rows // block,),
        [
            pl.BlockSpec((block, half), lambda i, p: (i, p[1])),
            pl.BlockSpec((block, half), lambda i, p: (i, 1 - p[1])),
            pl.BlockSpec((block, width), lambda i, p: (i, 0)),
        ],
        pl.BlockSpec((1, width), lambda i, p: (0, 0)),
        jax.ShapeDtypeStruct((1, width), F32),
        scalars=1,
    )(place, x, x, upstream)


def per_device(
    sizes, hidden_in, cotangent, w_qkv, w_out, w_gate_up, w_down, norm_gains, segments
):
    n_seq, n_tp, n_rep = sizes
    seqs, length, width = hidden_in.shape
    total = segments.shape[1]
    qkv_width = w_qkv.shape[3]
    group = qkv_width // HEAD_DIM - 2
    ff = w_down.shape[1]
    rows = seqs * length
    scale = float(HEAD_DIM) ** (-0.5)
    two = n_seq == 2
    si = lax.axis_index("seq")
    ti = lax.axis_index("tp")
    zi = lax.axis_index("rep")
    core, yi = ti % 2, ti // 2
    half = width // 2
    fourth = width // 4
    quarter = length // 4
    own = core * 2 + yi
    col_swap = si if two else jnp.int32(0) * si
    pz = zi % 2
    place = jnp.stack([own, col_swap, pz]).astype(jnp.int32)
    middle = (zi == 1) | (zi == 2)
    mid_flag = jnp.reshape(middle, (1,)).astype(jnp.int32)
    order = Order()

    def swap_seq(x):
        return lax.ppermute(x, "seq", [(0, 1), (1, 0)])

    def swap_core(x):
        return lax.ppermute(x, "tp", [(0, 1), (1, 0), (2, 3), (3, 2)])

    def swap_y(x):
        return lax.ppermute(x, "tp", [(0, 2), (2, 0), (1, 3), (3, 1)])

    def swap_z(x):
        return lax.ppermute(x, "rep", [(0, 1), (1, 0), (2, 3), (3, 2)])

    def hop_in(x):
        return lax.ppermute(x, "rep", [(0, 1), (3, 2)])

    def hop_mid(x):
        return lax.ppermute(x, "rep", [(1, 2), (2, 1)])

    def hop_out(x):
        return lax.ppermute(x, "rep", [(1, 0), (2, 3)])

    def whole(shard, axis):
        return lax.all_gather(shard, "seq", axis=axis, tiled=True)

    def now(*xs):
        return lax.optimization_barrier((xs, order.last))[0]

    def share(x):
        far = swap_y(x)
        return [x, far, swap_core(x), swap_core(far)]

    wq, wo, wd, wg = w_qkv[0, :, 0, :], w_out[0], w_down[0], w_gate_up[0]
    if two:
        gains = jnp.concatenate([norm_gains[0], swap_seq(norm_gains[0])], 1).astype(F32)
        qkv_parts = [Part(wq), Part(swap_seq(wq), half)]
        out_x = swap_seq(lax.dynamic_slice_in_dim(wo, pz * fourth, fourth, 1))

        def spread(*blocks):
            return order(lambda w, p: spread_gate_up(w, p, list(blocks)), wg, place)

        gu_a = spread(lambda p: 4 * p[2])
    else:
        gains = whole(norm_gains[0], 1).astype(F32)
        qkv_parts, out_parts = [Part(whole(wq, 0))], [Part(whole(wo, 1))]
        down_parts = [Part(whole(wd, 1))]
        gu_parts = [Part(spread_gate_up(whole(wg, 0), place, None))]

    first_row = si * length
    ids = jnp.arange(total, dtype=jnp.int32)
    change = jnp.concatenate(
        [jnp.ones((seqs, 1), bool), segments[:, 1:] != segments[:, :-1]], axis=1
    )
    doc_start = lax.cummax(jnp.where(change, ids[None, :], 0), axis=1)
    starts = lax.dynamic_slice_in_dim(doc_start, first_row, length, 1)
    pos = first_row + jnp.arange(length, dtype=jnp.int32)[None, :] - starts
    inverse_freq = ROPE_THETA ** (-(jnp.arange(HEAD_DIM // 2, dtype=F32) / (HEAD_DIM // 2)))
    angles = inverse_freq[None, :, None] * pos.astype(F32)[:, None, :]
    cos_t, sin_t = jnp.cos(angles), jnp.sin(angles)
    starts3 = starts[:, None, :]
    tq, tk = min(256, length), min(256, total)
    tiles = jnp.arange(length // tq, dtype=jnp.int32)
    ends = (first_row + (tiles + 1) * tq + tk - 1) // tk
    bounds = [
        jnp.concatenate(
            [
                jnp.stack([first_row, pz]),
                jnp.stack([starts[s, ::tq] // tk, ends], axis=1).reshape(-1),
            ]
        ).astype(jnp.int32)
        for s in range(seqs)
    ]

    hidden = hidden_in.reshape(rows, width)
    d_hidden = cotangent.reshape(rows, width)
    normed1 = order(lambda h, g, p: first_norm(h, g, p, 2 * quarter), hidden, gains[:1], place)
    if two:
        gu_c = spread(lambda p: 1, lambda p: 5)
    dhb = order(lambda d, p: local_cast(d, p, quarter), d_hidden, place)
    own_h, own_d = [None] * seqs, [None] * seqs
    for s in range(seqs):
        own_h[s], own_d[s] = order(
            lambda h, d, p, s=s: by_rows(
                lambda h, d: (h, d), p, s, quarter, [h, d], [], [], [F32, F32]
            ),
            hidden, d_hidden, place,
        )
    q_t, kv_t = order(
        lambda n, w, c, s: project_qkv(n, w, c, s, group),
        normed1, [x.array for x in qkv_parts], cos_t, sin_t,
    )
    if two:
        kv_got = lax.ppermute(kv_t, "seq", [(0, 1)])
        gu_x = [swap_seq(*now(gu_a))]
        gu_b = spread(lambda p: 4 * p[2] + 2, lambda p: 4 * p[2] + 3)
        out_z = swap_z(*now(out_x))
        all_kv = order(join_kv, kv_t, kv_got, place)
        out_parts = [Part(wo), Part(out_x, 0, 0), Part(out_z, 0, 1)]
    else:
        all_kv = whole(kv_t, 2)

    att, att_t, lse = [None] * seqs, [None] * seqs, [None] * seqs
    hold, keep = [None] * seqs, [None] * seqs

    def attention(s):
        att[s], att_t[s], lse[s] = order(
            lambda q, kv, st, b, s=s: attend(s, q, kv, st, b, scale),
            q_t, all_kv, starts3, bounds[s],
        )

    def out_product(s):
        send, keep[s] = order(
            lambda a, w, p: split_matmul(a, w, False, True, p, 1), att[s], out_parts, place
        )
        hold[s] = swap_core(send)

    def summed(keep, hold, s):
        send, keep[s] = order(first_sum, keep[s], hold[s])
        hold[s] = swap_y(send)

    attention(0)
    if two:
        touch(order, gu_x[0])
        gu_z = [swap_z(*now(gu_x[0]))]
        gu_x += [swap_seq(*now(gu_b))]
    out_product(0)
    for s in range(1, seqs):
        attention(s)
        summed(keep, hold, s - 1)
        out_product(s)
    if two:
        own_c = [gu_c[k * 128 : (k + 1) * 128] for k in range(2)]
        gu_c = [swap_seq(x) for x in now(*own_c)]
    summed(keep, hold, seqs - 1)
    if two:
        touch(order, gu_x[1])
        gu_z += [swap_z(*now(gu_x[1]))]
        piece = fourth // 2
        down_send = order(
            lambda w: (
                lax.dynamic_slice_in_dim(w, pz * fourth, piece, 1),
                w[:, piece : 2 * piece],
                w[:, 3 * piece :],
            ),
            wd,
        )
    h2, n2, extra = [None] * seqs, [None] * seqs, [None] * seqs

    def second_norm(h, k, g, gain):
        x = h + k + g
        inv = lax.rsqrt(jnp.mean(x * x, axis=-1, keepdims=True) + NORM_EPS)
        return x, x * inv * gain, k + g

    for s in range(seqs):
        h2[s], mine, extra[s] = order(
            lambda h, k, g, gain, p, s=s: by_rows(
                second_norm, p, s, quarter, [], [h, k, g], [gain], [F32, BF16, BF16]
            ),
            own_h[s], keep[s], hold[s], gains[1:], place,
        )
        n2[s] = share(mine)
        if two and s == 0:
            gu_d = spread(*[lambda p, k=k: 4 * (1 - p[2]) + k for k in (0, 2, 3)])
            touch(order, gu_z[0], gu_c[0])
            down_send = now(*down_send)
            down_x = swap_seq(down_send[0])
            down_c = [swap_seq(x) for x in down_send[1:]]
    if two:
        gu_parts = [Part(gu_a, -half, 0), Part(gu_b, 256 - half, 0)]
        gu_parts += [Part(own_c[k], k * fourth + 128) for k in range(2)]
        gu_parts += [Part(gu_d[:128], -half, 1), Part(gu_d[128:], 256 - half, 1)]
        gu_parts += [Part(gu_x[k], k * 256, 0) for k in range(2)]
        gu_parts += [Part(gu_z[k], k * 256, 1) for k in range(2)]
        gu_parts += [Part(gu_c[k], half + k * fourth + 128) for k in range(2)]
        touch(order, down_x)
        down_z = swap_z(*now(down_x))
        down_parts = [Part(wd), Part(down_x, 0, 0), Part(down_z, 0, 1)]
        down_parts += [Part(down_c[k], half + k * fourth + piece) for k in range(2)]
    n2_all, act, gu = order(gate_up, [x for b in n2 for x in b], gu_parts, place)

    class Chunk:
        def __init__(self, finish):
            self.finish, self.stage = finish, 0

        def begin(self, make, *xs):
            self.make, self.xs = make, xs
            self.got = swap_seq(order(lambda *x: make(1, *x), *xs))

        def next(self):
            k = self.stage
            self.stage += 1
            assert k < 4
            if k == 0:
                self.sum = order(
                    lambda g, *x: (self.make(0, *x) + g.astype(F32)).astype(g.dtype),
                    self.got, *self.xs,
                )
            elif k < 3:
                self.sum = order(self.add, self.sum, self.got)
            else:
                self.finish(self.sum, self.got)
            if k < 3:
                self.got = (hop_in, hop_mid, hop_out)[k](self.sum)

        def add(self, a, b):
            return a + b if a.dtype == F32 else add_pair(a, b)

    chunks, results = {}, {}

    def begin(name, finish, make, *xs):
        if two:
            chunks[name] = Chunk(finish)
            chunks[name].begin(make, *xs)

    def go(*names):
        for name in names:
            if two:
                chunks[name].next()

    def into(name, writer):
        def finish(a, b):
            results[name] = [
                order(lambda a, b, m, r: writer(a, b, m, r), a, b, mid_flag, results.get(name, []))
            ]

        return finish

    def piece_of(x, k, at, size):
        return x[:, k * half + at : k * half + at + size]

    def tdot(a, b, k):
        x = dot(a, b, 0, 0)
        return x.astype(BF16) if k else x

    cuts = [0, 768, ff]
    gu_rows = [256, 256, 256, 128, 128]

    def begin_down(j):
        begin(
            f"d{j}",
            into("down", lambda a, b, m, r: place_rows(a, b, m, cuts[j], ff, r)),
            lambda k, a, d: tdot(a[:, cuts[j] : cuts[j + 1]], piece_of(d, k, 0, half), k),
            act, dhb,
        )

    def begin_gu(j):
        at = sum(gu_rows[:j])
        begin(
            f"g{j}",
            into("gu", lambda a, b, m, r: join_gate_up(a, b, m, at, half, r)),
            lambda k, n, d: tdot(piece_of(n, k, at, gu_rows[j]), d, k),
            n2_all, dgu,
        )

    begin_down(0)
    if two:

        def pair(a, c, first):
            return jnp.concatenate([a, jnp.where(first, c[0], c[1])])

        begin_down(1)
        near = order(lambda a, c: pair(a, c, pz == 0), gu_a, own_c)
        far = order(lambda a, c: pair(a, c, pz == 1), gu_d[:128], own_c)
        pair_x = order(lambda a, c: pair(a, c, pz == 0), gu_x[0], gu_c)
        pair_z = order(lambda a, c: pair(a, c, pz == 1), gu_z[0], gu_c)
        gu_parts = [Part(near, -half, 0), Part(gu_b, 256 - half, 0)]
        gu_parts += [Part(far, -half, 1), Part(gu_d[128:], 256 - half, 1)]
        gu_parts += [Part(pair_x, 0, 0), Part(gu_x[1], 256, 0)]
        gu_parts += [Part(pair_z, 0, 1), Part(gu_z[1], 256, 1)]
    dgu = order(gate_back, dhb, down_parts, gu, place)
    got = order(
        lambda a, w, p: split_matmul(a, w, True, False, p, seqs), dgu, gu_parts, place
    )
    keep, hold = list(got[1::2]), [swap_core(x) for x in got[::2]]
    go("d0")
    for s in range(seqs):
        summed(keep, hold, s)
    begin_gu(0)
    d2, gain2 = [None] * seqs, []

    def second_back(d, k, g, x, gain):
        mine = k + g
        inv = lax.rsqrt(jnp.mean(x * x, axis=-1, keepdims=True) + NORM_EPS)
        w = gain * mine
        back = inv * w - x * (inv * inv * inv) * jnp.mean(w * x, axis=-1, keepdims=True)
        return back + d, jnp.sum(mine * x * inv, axis=0, keepdims=True)

    for s in range(seqs):
        mine, g2 = order(
            lambda d, k, g, x, gain, p, s=s: by_rows(
                second_back, p, s, quarter, [], [d, k, g, x], [gain], [BF16], 1
            ),
            own_d[s], keep[s], hold[s], h2[s], gains[1:], place,
        )
        gain2.append(g2)
        d2[s] = share(mine)
        if s == 0:
            go("d1")
    go("d0")
    dq, dkv, early = [None] * seqs, [None] * seqs, [None] * seqs
    dkv_got = []
    for s in range(seqs):
        d2[s] = order(stack, d2[s], place)
        dq[s], dkv[s], early[s] = order(
            lambda q, kv, st, b, a, w, *x, s=s: attend_back(s, q, kv, st, b, a, w, *x, scale),
            q_t, all_kv, starts3, bounds[s], att_t[s], out_parts, d2[s], lse[s], cos_t, sin_t,
        )
        if two:
            dkv_got.append(lax.ppermute(early[s], "seq", [(1, 0)]))
        if s == 0:
            go("g0")
    begin(
        "out",
        into("out", lambda a, b, m, r: place_rows(a, b, m, 0, a.shape[0], r)),
        lambda k, a, d: sum(
            dot(x, piece_of(y, k, 0, half), 0, 0) for x, y in zip(a, d)
        ).astype(BF16 if k else F32),
        att, d2,
    )
    go("d0", "d1")
    delta = order(
        lambda a, w, p, x: full_matmul(a, w, False, p, seqs, x), act, down_parts, place, extra
    )
    if not two:
        dkv = [lax.psum_scatter(x, "seq", scatter_dimension=1, tiled=True) for x in dkv]
    d_qkv = order(
        lambda q, kv, g, c, s, p: pack_dqkv(q, kv, g, c, s, p, two),
        dq, dkv, dkv_got, cos_t, sin_t, place,
    )
    begin_gu(1)
    d_n1 = order(lambda a, w, p: full_matmul(a, w, True, p, seqs, []), d_qkv, qkv_parts, place)
    d_part = d_n1
    delta, d_n1 = lax.psum((delta, d_n1), "tp")
    go("g0", "out")
    begin(
        "qkv",
        into("qkv", lambda a, b, m, r: place_rows(a, b, m, 0, half, r)),
        lambda k, n, d: tdot(piece_of(n, k, 0, half), d, k),
        normed1, d_qkv,
    )
    go("d0", "d1")
    gain1 = order(lambda h, u, p: gain_rows(h, u, p, quarter), hidden, d_part, place)
    go("g1", "out", "g0")
    begin_gu(2)
    gain_sum = order(lambda a, b: jnp.concatenate([a, sum(b)]), gain1, gain2)
    gain_sum = order(lambda a, b: a + b, gain_sum, swap_core(gain_sum))
    gain_sum = order(lambda a, b: a + b, gain_sum, swap_y(gain_sum))

    def gain_finish(a, b):
        results["gain"] = [order(lambda a, b: jnp.where(middle, a, b), a, b)]

    go("qkv", "d1", "g1", "out", "g0")
    begin_gu(3)
    begin("gain", gain_finish, lambda k, g: piece_of(g, k, 0, half), gain_sum)
    go("g2", "qkv", "g1", "out", "gain")
    begin_gu(4)
    go("g3", "g2", "qkv", "gain", "g1")
    go("g4", "g3", "g2", "gain", "qkv")
    go("g4", "g3", "g2", "gain", "g4")
    hidden_out = order(lambda h, d, p: add_columns(h, d, p, quarter), hidden, delta, place)
    go("g3")
    grad_in = order(
        lambda h, u, d, g, p: first_norm_back(h, u, d, g, p, quarter),
        hidden, d_n1, d2, gains[:1], place,
    )
    go("g4")
    if two:
        g_qkv, g_out, g_down = results["qkv"][0], results["out"][0], results["down"][0]
        g_gu, gain_own = results["gu"][0], results["gain"][0]
    else:

        def reduce_rep(x):
            if n_rep != 4:
                return lax.psum(x.astype(F32), "rep").astype(BF16)
            x = x.astype(BF16)
            x = (x.astype(F32) + hop_in(x).astype(F32)).astype(BF16)
            x = (x.astype(F32) + hop_mid(x).astype(F32)).astype(BF16)
            return jnp.where(middle, x, hop_out(x))

        def reduce(x, axis):
            return reduce_rep(lax.psum_scatter(x, "seq", scatter_dimension=axis, tiled=True))

        g_down = reduce(dot(act, dhb, 0, 0), 1).astype(F32)
        g_out = reduce(sum(dot(x, y, 0, 0) for x, y in zip(att, d2)), 1).astype(F32)
        g_qkv = reduce(dot(normed1, d_qkv, 0, 0), 0).astype(F32)
        g_gu = reduce(dot(n2_all, dgu, 0, 0), 0)
        g_gu = join_gate_up(g_gu, g_gu, mid_flag, 0, g_gu.shape[0], [])
        gain_own = lax.psum_scatter(gain_sum, "seq", scatter_dimension=1, tiled=True)
        gain_own = lax.psum(gain_own, "rep")
    return (
        hidden_out.reshape(seqs, length, width),
        grad_in.reshape(seqs, length, width),
        g_qkv[None, :, None, :],
        g_out[None],
        g_gu,
        g_down[None],
        gain_own[None],
    )


def solution(mesh):
    in_specs = (
        P("rep", "seq", None),
        P("rep", "seq", None),
        P(None, "seq", "tp", None),
        P(None, "tp", "seq"),
        P(None, "seq", None, "tp"),
        P(None, "tp", "seq"),
        P(None, None, "seq"),
        P("rep", None),
    )
    out_specs = (
        P("rep", "seq", None),
        P("rep", "seq", None),
        P(None, "seq", "tp", None),
        P(None, "tp", "seq"),
        P(None, "seq", None, "tp"),
        P(None, "tp", "seq"),
        P(None, None, "seq"),
    )
    sizes = (mesh.shape["seq"], mesh.shape["tp"], mesh.shape["rep"])
    return jax.shard_map(
        functools.partial(per_device, sizes),
        mesh=mesh,
        in_specs=in_specs,
        out_specs=out_specs,
        check_vma=False,
    )
```
